32 devices in a mesh: seq: 4 (over x, core), fsdp: 8 (over z, y).
Axes of the slice: x: 2, y: 2, z: 4, core: 2. Of those that a mesh axis runs over, the one named last changes fastest.
Arguments:
- tokens: bfloat16 [8, 1024, 1536], P('fsdp', 'seq'), may hold values from -6 to 6
- segment_ids: int32 [8, 1024], P('fsdp'), may hold values from 0 to 2, as said below
- attn_gain: bfloat16 [1536], P('fsdp'), may hold values from 0.5 to 1.5
- qkv_weight: bfloat16 [1536, 2048], P('fsdp'), may hold values from -0.15625 to 0.15625
- qkv_bias: bfloat16 [2048], P('fsdp'), may hold values from -3 to 3
- proj_weight: bfloat16 [1536, 1536], P('fsdp'), may hold values from -1.25 to 1.25
- mlp_gain: bfloat16 [1536], P('fsdp'), may hold values from 0.5 to 1.5
- gate_up_weight: bfloat16 [1536, 17920], P('fsdp'), may hold values from -0.15625 to 0.15625
- down_weight: bfloat16 [8960, 1536], P('fsdp'), may hold values from -0.0625 to 0.0625
- cotangent: bfloat16 [8, 1024, 1536], P('fsdp', 'seq'), may hold values from -6 to 6
Outputs:
- block_out: bfloat16 [8, 1024, 1536], P('fsdp', 'seq')
- tokens_grad: float32 [8, 1024, 1536], P('fsdp', 'seq')
- attn_gain_grad: float32 [1536], P('fsdp')
- qkv_weight_grad: float32 [1536, 2048], P('fsdp')
- qkv_bias_grad: float32 [2048], P('fsdp')
- proj_weight_grad: float32 [1536, 1536], P('fsdp')
- mlp_gain_grad: float32 [1536], P('fsdp')
- gate_up_weight_grad: float32 [1536, 17920], P('fsdp')
- down_weight_grad: float32 [8960, 1536], P('fsdp')
The draws below stay inside these ranges and needn't reach their ends.
Inputs may be any that keep to these rules, and one draw needn't show every extreme that they name: `segment_ids`: each row is one sequence holding three documents in order: segment ids never fall along a row, each of 0, 1 and 2 occurs, and the first and the last document have at most 128 tokens each.
All inputs are finite; a program needn't handle non-finite values.
Results may differ from the reference program's by a relative error of at most 0.013.
Values may be sent and summed in bfloat16 or wider, within the bound.
A program may use at most 448 MiB of HBM per device.

```python
import jax
import jax.numpy as jnp
from jax import lax

D = 1536
H = 12
KV = 2
HD = 128
FF = 8960
TOK_DEV = 256
LEN = 1024
SEQS = 8
QKV = 2048
N_SEQ = 4


def draw_segment_ids(key, part):
    key = jax.random.fold_in(key, 11)
    first_key, last_key = jax.random.split(key)
    first_end = jax.random.randint(first_key, (SEQS, 1), 1, TOK_DEV // 2)
    last_start = jax.random.randint(last_key, (SEQS, 1), LEN - TOK_DEV // 2, LEN)
    position = jnp.arange(LEN, dtype=jnp.int32)[None, :]
    return (position >= first_end).astype(jnp.int32) + (position >= last_start).astype(jnp.int32)


def steps_of(own_key, shape, cuts, low, top_value):
    loudness, own = 1.0, jax.random.fold_in(own_key, 6)
    for dim, shards_of in cuts:
        heights = jnp.exp(jax.random.uniform(jax.random.fold_in(own, dim), (shards_of,), jnp.float32, low / len(cuts), top_value / len(cuts)))
        loudness = loudness * jnp.repeat(heights, shape[dim] // shards_of).reshape([-1 if axis == dim else 1 for axis in range(len(shape))])
    return loudness


def normal_values(rng, shape, width, limit, cuts=(), kind=jnp.bfloat16):
    array = width * jax.random.normal(rng, shape, jnp.float32)
    if cuts:
        array = array * steps_of(rng, shape, cuts, -0.22, 0.18)
    return jnp.clip(array, -limit, limit).astype(kind)


def setup_inputs(seed: int = 0) -> dict:
    arg_keys = jax.random.split(jax.random.key(seed), 11)
    tokens = normal_values(arg_keys[0], (SEQS, LEN, D), 1.0, 6.0, ((0, 8), (1, 4)))
    segment_ids = draw_segment_ids(jax.random.fold_in(arg_keys[10], 71), 0)
    attn_gain = jnp.clip(1.0 + 0.1 * jax.random.normal(arg_keys[2], (D,), jnp.float32), 0.5, 1.5).astype(jnp.bfloat16)
    qkv_weight = normal_values(arg_keys[3], (D, QKV), D ** -0.5, 0.15625, ((0, 8),))
    qkv_bias = normal_values(arg_keys[4], (QKV,), 0.5, 3.0, ((0, 8),))
    proj_weight = normal_values(arg_keys[5], (D, D), (D * 16 // LEN) ** -0.5, 1.25, ((0, 8),))
    mlp_gain = jnp.clip(1.0 + 0.1 * jax.random.normal(arg_keys[6], (D,), jnp.float32), 0.5, 1.5).astype(jnp.bfloat16)
    gate_up_weight = normal_values(arg_keys[7], (D, 2 * FF), D ** -0.5, 0.15625, ((0, 8),))
    down_weight = normal_values(arg_keys[8], (FF, D), FF ** -0.5, 0.0625, ((0, 8),))
    cotangent = normal_values(arg_keys[9], (SEQS, LEN, D), 1.0, 6.0, ((0, 8), (1, 4)))
    return dict(tokens=tokens, segment_ids=segment_ids, attn_gain=attn_gain, qkv_weight=qkv_weight, qkv_bias=qkv_bias, proj_weight=proj_weight, mlp_gain=mlp_gain, gate_up_weight=gate_up_weight, down_weight=down_weight, cotangent=cotangent)


EPSILON = 1e-06
THETA = 1000000.0
PRECISE = lax.Precision.HIGHEST

@jax.custom_vjp
def low(v):
    return lax.optimization_barrier(v.astype(jnp.bfloat16)).astype(jnp.float32)

@jax.custom_vjp
def low_back(v):
    return v

def low_keep(v):
    return (low(v), None)

def low_pass(kept, grad):
    return (grad,)

def back_keep(v):
    return (v, None)

def back_low(kept, grad):
    return (low(grad),)
low.defvjp(low_keep, low_pass)
low_back.defvjp(back_keep, back_low)

def matmul(left, right):
    return jnp.dot(left, right, precision=PRECISE, preferred_element_type=jnp.float32)

def normed(value, gain):
    return value * lax.rsqrt(lax.optimization_barrier(jnp.mean(value * value, axis=-1, keepdims=True)) + EPSILON) * gain

def turned(value):
    halfway = value.shape[-1] // 2
    return jnp.concatenate([-value[..., halfway:], value[..., :halfway]], axis=-1)

def rotary(segments):
    length = segments.shape[0]
    starts = lax.optimization_barrier(jnp.sum((segments[None, :] < segments[:, None]).astype(jnp.int32), axis=1))
    places = jnp.arange(length, dtype=jnp.int32) - starts
    inverse = THETA ** (-2.0 * jnp.arange(HD // 2, dtype=jnp.float32) / HD)
    angles = places.astype(jnp.float32)[:, None] * inverse[None, :]
    angles = jnp.concatenate([angles, angles], axis=-1)
    return (jnp.cos(angles), jnp.sin(angles))

def layer(value, attn_gain, qkv_weight, qkv_bias, proj_weight, mlp_gain, gate_up_weight, down_weight, segments):
    cosines, sines = rotary(segments)
    cosines = cosines[:, None, :]
    sines = sines[:, None, :]
    normed_in = low(normed(value, attn_gain))
    projected = low_back(matmul(normed_in, qkv_weight) + qkv_bias)
    queries = projected[:, :H * HD].reshape(LEN, H, HD)
    key_heads = projected[:, H * HD:(H + KV) * HD].reshape(LEN, KV, HD)
    value_heads = projected[:, (H + KV) * HD:].reshape(LEN, KV, HD)
    queries = low_back(low(queries * cosines + turned(queries) * sines))
    key_heads = low(key_heads * cosines + turned(key_heads) * sines)
    value_heads = low(value_heads)
    copies = N_SEQ // KV
    key_heads = low_back(jnp.repeat(key_heads, copies, axis=1))
    value_heads = low_back(jnp.repeat(value_heads, copies, axis=1))
    per_dev = H // N_SEQ
    block_rows = min(512, LEN)
    blocks = LEN // block_rows
    key_index = jnp.arange(LEN, dtype=jnp.int32)
    score_scale = HD ** (-0.5)

    def attend(element):
        query_block, first_row = element
        row_index = first_row + jnp.arange(block_rows, dtype=jnp.int32)
        row_segments = lax.dynamic_slice_in_dim(segments, first_row, block_rows)
        allowed = (key_index[None, :] <= row_index[:, None]) & (segments[None, :] == row_segments[:, None])
        scores = low_back(score_scale * jnp.einsum('qnhd,knd->nhqk', query_block, key_heads, precision=PRECISE))
        scores = jnp.where(allowed[None, None], scores, -1e+30)
        weights = low(jax.nn.softmax(scores, axis=-1))
        return jnp.einsum('nhqk,knd->qnhd', weights, value_heads, precision=PRECISE)
    block_starts = jnp.arange(blocks, dtype=jnp.int32) * block_rows
    grouped = queries.reshape(blocks, block_rows, N_SEQ, per_dev, HD)
    attention = lax.map(jax.checkpoint(attend), (grouped, block_starts))
    merged = low_back(low(attention.reshape(LEN, H * HD)))
    attended = low_back(matmul(merged, proj_weight))
    hidden_in = value + attended
    normed_mid = low(normed(hidden_in, mlp_gain))
    gate_up = low_back(matmul(normed_mid, gate_up_weight))
    activated = low(jax.nn.silu(gate_up[:, :FF]) * gate_up[:, FF:])
    return low(hidden_in + low_back(matmul(activated, down_weight)))

def reference(tokens, segment_ids, attn_gain, qkv_weight, qkv_bias, proj_weight, mlp_gain, gate_up_weight, down_weight, cotangent):
    tensors = tuple((tensor.astype(jnp.float32) for tensor in (attn_gain, qkv_weight, qkv_bias, proj_weight, mlp_gain, gate_up_weight, down_weight)))

    def per_sequence(totals, element):
        sequence, segments, upstream = element

        def applied(value, *weights):
            return layer(value, *weights, segments)
        result, pullback = jax.vjp(applied, sequence.astype(jnp.float32), *tensors)
        gradients = pullback(upstream.astype(jnp.float32))
        totals = tuple((total + gradient for total, gradient in zip(totals, gradients[1:])))
        return (totals, (result.astype(jnp.bfloat16), gradients[0]))
    initial = tuple((jnp.zeros(tensor.shape, jnp.float32) for tensor in tensors))
    totals, (results, input_grads) = lax.scan(per_sequence, initial, (tokens, segment_ids, cotangent))
    return (results, input_grads, totals[0], totals[1], totals[2], totals[3], totals[4], totals[5], totals[6])
```

```python
import jax
import jax.numpy as jnp
from jax import lax
from jax.sharding import PartitionSpec as P

H = 12
KV = 2
HD = 128
EPSILON = 1e-06
THETA = 1000000.0
FLOOR = -1e30
LOW = jnp.bfloat16
F32 = jnp.float32


def inverse_rms(value):
    return lax.rsqrt(jnp.mean(value * value, axis=-1, keepdims=True) + EPSILON)


def turned(value):
    halfway = value.shape[-1] // 2
    return jnp.concatenate([-value[..., halfway:], value[..., :halfway]], axis=-1)


def turned_back(value):
    halfway = value.shape[-1] // 2
    return jnp.concatenate([value[..., halfway:], -value[..., :halfway]], axis=-1)


def norm_back(value, factor, gain, upstream):
    weighted = upstream * gain
    gain_term = jnp.sum(upstream * value * factor, axis=0)
    through = factor * weighted - value * factor**3 * jnp.mean(
        weighted * value, axis=-1, keepdims=True
    )
    return (through, gain_term)


def dot(left, right):
    return jnp.dot(left, right, preferred_element_type=F32)


def column_product(left, right):
    return lax.dot_general(left, right, (((0,), (0,)), ((), ())), preferred_element_type=F32)


def times_transpose(left, right):
    return lax.dot_general(left, right, (((1,), (1,)), ((), ())), preferred_element_type=F32)


def swap(value, axis, distance):
    return lax.ppermute(value, axis, [(i, i ^ distance) for i in range(lax.axis_size(axis))])


def lines():
    size = lax.axis_size("fsdp")
    return [list(range(first, size, 2)) for first in range(2)]


def line_gather(value):
    return lax.all_gather(value, "fsdp", axis=0, axis_index_groups=lines(), tiled=False)


def line_reduce(value):
    return lax.psum_scatter(
        value, "fsdp", scatter_dimension=0, axis_index_groups=lines(), tiled=False
    )


def seq_gather(value):
    return lax.all_gather(value, "seq", axis=0, tiled=True)


def seq_reduce(value):
    return lax.psum_scatter(value, "seq", scatter_dimension=0, tiled=True)


def seq_exchange(pieces):
    size = pieces.shape[0]
    me = lax.axis_index("seq")
    taken = [lax.dynamic_index_in_dim(pieces, me ^ k, 0, keepdims=False) for k in range(size)]
    arrived = [taken[0]] + [swap(taken[k], "seq", k) for k in range(1, size)]
    bits = 1
    while bits < size:
        flip = (me & bits) != 0
        arrived = [jnp.where(flip, arrived[k ^ bits], arrived[k]) for k in range(size)]
        bits *= 2
    return arrived


def by_pair(own, other):
    second = lax.axis_index("fsdp") % 2 == 1
    return (jnp.where(second, other, own), jnp.where(second, own, other))


def pick(flag, first, second):
    return (jnp.where(flag, second, first), jnp.where(flag, first, second))


def local(
    tokens,
    segment_ids,
    attn_gain,
    qkv_weight,
    qkv_bias,
    proj_weight,
    mlp_gain,
    gate_up_weight,
    down_weight,
    cotangent,
):
    seq_count = lax.axis_size("seq")
    fsdp_count = lax.axis_size("fsdp")
    line = fsdp_count // 2
    place = lax.axis_index("seq")
    odd = lax.axis_index("fsdp") % 2 == 1
    tok_rows, width = tokens.shape[1:]
    seq_len = tok_rows * seq_count
    owned = qkv_weight.shape[0]
    owned_hidden = down_weight.shape[0]
    hidden = owned_hidden * fsdp_count
    quarter = width // seq_count
    per_dev = H // seq_count
    head_cols = per_dev * HD
    score_scale = HD ** (-0.5)
    group = line // seq_count
    mine_ff = group * owned_hidden

    holds_values = place % 2 == 1
    pair_head = place // 2
    kv_first = (H + KV * (place % 2) + pair_head) * HD
    qkv_own = jnp.concatenate(
        [
            lax.dynamic_slice_in_dim(qkv_weight, place * head_cols, head_cols, 1),
            lax.dynamic_slice_in_dim(qkv_weight, kv_first, HD, 1),
        ],
        axis=1,
    )
    cols = head_cols + HD
    vector = jnp.concatenate([attn_gain, mlp_gain, qkv_bias])
    vector_size = vector.shape[0]
    vector_rows = -(-vector_size // (16 * cols)) * 16
    vector = jnp.pad(vector, (0, vector_rows * cols - vector_size)).reshape(vector_rows, cols)
    qkv_line = line_gather(jnp.concatenate([qkv_own, vector], axis=0))
    tokens_all = seq_gather(tokens[0])
    qkv_both = jnp.stack(by_pair(qkv_line, swap(qkv_line, "fsdp", 1)), axis=1)
    qkv_mine = qkv_both[:, :, :owned].reshape(width, cols)
    vectors = qkv_both[:, :, owned:].reshape(fsdp_count, vector_rows * cols)[:, :vector_size]
    gain_one = vectors[:, :owned].reshape(width).astype(F32)
    gain_two = vectors[:, owned : 2 * owned].reshape(width).astype(F32)
    bias = vectors[:, 2 * owned :].reshape(-1).astype(F32)
    bias_mine = jnp.concatenate(
        [
            lax.dynamic_slice_in_dim(bias, place * head_cols, head_cols),
            lax.dynamic_slice_in_dim(bias, kv_first, HD),
        ]
    )

    proj_cols = lax.dynamic_slice_in_dim(proj_weight, place * quarter, quarter, 1)
    proj_line = line_gather(proj_cols).reshape(seq_count, group * owned, quarter)
    proj_half = jnp.concatenate(seq_exchange(proj_line), axis=1).reshape(group, owned, width)
    proj_mine = jnp.stack(by_pair(proj_half, swap(proj_half, "fsdp", 1)), axis=1).reshape(
        head_cols, width
    )

    down_cols = lax.dynamic_slice_in_dim(down_weight, place * quarter, quarter, 1)
    down_line = line_gather(down_cols).reshape(seq_count, mine_ff, quarter)
    down_mine = jnp.concatenate(seq_exchange(down_line), axis=1)

    def ff_slice(first):
        both = lax.dynamic_slice_in_dim(
            gate_up_weight, first + place * 2 * mine_ff, 2 * mine_ff, 1
        ).reshape(owned, group, 2, owned_hidden)
        return (
            both[:, :, 0].reshape(owned, mine_ff),
            both[:, :, 1].reshape(owned, mine_ff),
        )

    gate_pair, up_pair = ff_slice(0), ff_slice(hidden)
    for_even = jnp.concatenate([gate_pair[0], up_pair[0]], axis=1)
    for_odd = jnp.concatenate([gate_pair[1], up_pair[1]], axis=1)
    kept, given = pick(odd, for_even, for_odd)
    gate_up_pair = jnp.stack(by_pair(kept, swap(given, "fsdp", 1)), axis=0)
    gate_up_mine = line_gather(gate_up_pair).reshape(width, 2 * mine_ff)

    segment_row = segment_ids[0]
    doc_starts = jnp.sum((segment_row[None, :] < segment_row[:, None]).astype(jnp.int32), axis=1)
    places = jnp.arange(seq_len, dtype=jnp.int32) - doc_starts
    inverse = THETA ** (-2.0 * jnp.arange(HD // 2, dtype=F32) / HD)
    angles = places.astype(F32)[:, None] * inverse[None, :]
    angles = jnp.concatenate([angles, angles], axis=-1)
    cosines = jnp.cos(angles)
    sines = jnp.sin(angles)

    resid_all = tokens_all.astype(F32)
    normed_in = (resid_all * inverse_rms(resid_all) * gain_one).astype(LOW)
    projected = dot(normed_in, qkv_mine) + bias_mine
    heads = projected.reshape(seq_len, per_dev + 1, HD)
    rotated = (heads * cosines[:, None] + turned(heads) * sines[:, None]).astype(LOW)
    queries = rotated[:, :per_dev]
    kv_own = jnp.where(holds_values, heads[:, per_dev].astype(LOW), rotated[:, per_dev])
    kv_other = swap(kv_own, "seq", 1)
    head_keys, head_values = pick(holds_values, kv_own, kv_other)

    block_rows = min(512, seq_len)
    blocks = seq_len // block_rows

    def scores_of(index):
        first, last = index * block_rows, (index + 1) * block_rows
        row_index = first + jnp.arange(block_rows, dtype=jnp.int32)
        key_index = jnp.arange(last, dtype=jnp.int32)
        allowed = (key_index[None, :] <= row_index[:, None]) & (
            segment_row[None, :last] == segment_row[first:last, None]
        )
        scores = (
            jnp.einsum(
                "qhd,kd->hqk", queries[first:last], head_keys[:last], preferred_element_type=F32
            )
            * score_scale
        )
        return (jnp.where(allowed[None], scores, FLOOR), allowed)

    head_parts, logsums = [], []
    for index in range(blocks):
        last = (index + 1) * block_rows
        scores, allowed = scores_of(index)
        highest = jnp.max(scores, axis=-1, keepdims=True)
        exponent = jnp.exp(scores - highest)
        row_total = jnp.sum(exponent, axis=-1, keepdims=True)
        weights = (exponent / row_total).astype(LOW)
        mixture = jnp.einsum("hqk,kd->qhd", weights, head_values[:last], preferred_element_type=F32)
        head_parts.append(mixture.astype(LOW).reshape(block_rows, head_cols))
        logsums.append((highest + jnp.log(row_total))[..., 0])
    merged = jnp.concatenate(head_parts, axis=0)

    resid = tokens[0].astype(F32)
    attended = seq_reduce(dot(merged, proj_mine).astype(LOW))
    hidden_in = resid + attended.astype(F32)
    factor_two = inverse_rms(hidden_in)
    normed_own = (hidden_in * factor_two * gain_two).astype(LOW)

    mids = (seq_gather(normed_own), seq_gather(swap(normed_own, "fsdp", 1)))
    cots = (seq_gather(cotangent[0]), seq_gather(swap(cotangent[0], "fsdp", 1)))
    acts, grads, blocks_out, grad_mids = [], [], [], []
    for mid, cot in zip(mids, cots):
        gate_up = dot(mid, gate_up_mine)
        gate, upward = gate_up[:, :mine_ff], gate_up[:, mine_ff:]
        sigmoid_gate = jax.nn.sigmoid(gate)
        act = (gate * sigmoid_gate * upward).astype(LOW)
        grad_act = times_transpose(cot, down_mine)
        grad_gate = grad_act * upward * sigmoid_gate * (1.0 + gate * (1.0 - sigmoid_gate))
        grad_up = grad_act * gate * sigmoid_gate
        grad = jnp.concatenate([grad_gate, grad_up], axis=-1).astype(LOW)
        acts.append(act)
        grads.append(grad)
        blocks_out.append(dot(act, down_mine).astype(LOW))
        grad_mids.append(times_transpose(grad, gate_up_mine).astype(LOW))

    def to_tokens(parts):
        return seq_reduce(parts[0]).astype(F32) + swap(seq_reduce(parts[1]), "fsdp", 1).astype(F32)

    grad_mid = to_tokens(grad_mids)
    block_out = (hidden_in + to_tokens(blocks_out)).astype(LOW)
    down_term = sum(column_product(a, c) for a, c in zip(acts, cots)).astype(LOW)
    gate_up_term = sum(column_product(m, g) for m, g in zip(mids, grads)).astype(LOW)

    through_two, gain_two_term = norm_back(hidden_in, factor_two, gain_two, grad_mid)
    grad_hidden = cotangent[0].astype(F32) + through_two

    grad_attended = seq_gather(grad_hidden.astype(LOW))
    proj_term = column_product(merged, grad_attended).astype(LOW)
    grad_merged = times_transpose(grad_attended, proj_mine).astype(LOW)
    grad_heads = grad_merged.reshape(seq_len, per_dev, HD)
    grad_key = jnp.zeros((seq_len, HD), F32)
    grad_value = jnp.zeros((seq_len, HD), F32)
    grad_queries = []
    for index in range(blocks):
        first, last = index * block_rows, (index + 1) * block_rows
        scores, allowed = scores_of(index)
        probs = jnp.where(allowed[None], jnp.exp(scores - logsums[index][..., None]), 0.0)
        grad_block = grad_heads[first:last]
        grad_probs = jnp.einsum(
            "qhd,kd->hqk", grad_block, head_values[:last], preferred_element_type=F32
        )
        inner = jnp.sum(probs * grad_probs, axis=-1, keepdims=True)
        grad_scores = (probs * (grad_probs - inner)).astype(LOW)
        grad_queries.append(
            (
                jnp.einsum(
                    "hqk,kd->qhd", grad_scores, head_keys[:last], preferred_element_type=F32
                )
                * score_scale
            ).astype(LOW)
        )
        key_term = (
            jnp.einsum(
                "hqk,qhd->kd", grad_scores, queries[first:last], preferred_element_type=F32
            )
            * score_scale
        )
        value_term = jnp.einsum(
            "hqk,qhd->kd", probs.astype(LOW), grad_block, preferred_element_type=F32
        )
        grad_key = grad_key + jnp.pad(key_term, ((0, seq_len - last), (0, 0)))
        grad_value = grad_value + jnp.pad(value_term, ((0, seq_len - last), (0, 0)))
    kept_kv, given_kv = pick(holds_values, grad_key.astype(LOW), grad_value.astype(LOW))
    grad_kv = kept_kv.astype(F32) + swap(given_kv, "seq", 1).astype(F32)
    grad_q = jnp.concatenate(grad_queries, axis=0).astype(F32)
    grad_rot = jnp.concatenate([grad_q, grad_kv[:, None]], axis=1)
    unturned = grad_rot * cosines[:, None] + turned_back(grad_rot * sines[:, None])
    grad_projected = jnp.concatenate(
        [unturned[:, :per_dev], jnp.where(holds_values, grad_kv[:, None], unturned[:, per_dev:])],
        axis=1,
    ).reshape(seq_len, cols).astype(LOW)
    bias_part = jnp.sum(grad_projected.astype(F32), axis=0)
    grad_in = seq_reduce(times_transpose(grad_projected, qkv_mine).astype(LOW)).astype(F32)
    qkv_term = column_product(normed_in, grad_projected).astype(LOW)
    through_one, gain_one_term = norm_back(resid, inverse_rms(resid), gain_one, grad_in)
    tokens_grad = grad_hidden + through_one

    def pair_sum(value):
        kept_rows, given_rows = pick(odd, value[:, 0], value[:, 1])
        arrived = swap(given_rows, "fsdp", 1)
        return (kept_rows.astype(F32) + arrived.astype(F32)).astype(LOW)

    def col_exchange(value):
        rows = value.shape[0]
        cut = jnp.stack([value[:, k * quarter : (k + 1) * quarter] for k in range(seq_count)])
        return jnp.stack(seq_exchange(cut)).reshape(line, rows // group, quarter)

    def from_quarters(value):
        wide = lax.all_gather(value, "seq", axis=0, tiled=False)
        return jnp.concatenate([wide[k] for k in range(seq_count)], axis=-1).astype(F32)

    down_grad = from_quarters(line_reduce(col_exchange(down_term)))
    gate_up_line = line_reduce(gate_up_term.reshape(line, 2, owned, 2 * mine_ff))
    kept, given = pick(odd, gate_up_line[0], gate_up_line[1])
    gate_up_pair = by_pair(kept, swap(given, "fsdp", 1))
    wide = lax.all_gather(jnp.stack(gate_up_pair), "seq", axis=0, tiled=False)
    wide = wide.reshape(seq_count, 2, owned, 2, group, owned_hidden)
    gate_up_grad = jnp.concatenate(
        [
            wide[k, pair, :, part, member]
            for part in range(2)
            for k in range(seq_count)
            for member in range(group)
            for pair in range(2)
        ],
        axis=-1,
    ).astype(F32)
    proj_sum = pair_sum(proj_term.reshape(group, 2, owned, width)).reshape(group * owned, width)
    proj_grad = from_quarters(line_reduce(col_exchange(proj_sum)))
    qkv_sum = line_reduce(pair_sum(qkv_term.reshape(line, 2, owned, cols)))
    wide = lax.all_gather(qkv_sum, "seq", axis=0, tiled=False)
    qkv_grad = jnp.concatenate(
        [wide[k, :, :head_cols] for k in range(seq_count)]
        + [wide[k, :, head_cols:] for k in range(0, seq_count, 2)]
        + [wide[k, :, head_cols:] for k in range(1, seq_count, 2)],
        axis=-1,
    ).astype(F32)

    bias_term = jnp.zeros(qkv_weight.shape[1], F32)
    bias_term = lax.dynamic_update_slice_in_dim(
        bias_term, bias_part[:head_cols], place * head_cols, 0
    )
    bias_term = lax.dynamic_update_slice_in_dim(bias_term, bias_part[head_cols:], kv_first, 0)
    vector_sum = lax.psum(
        jnp.concatenate([gain_one_term, gain_two_term, bias_term]), ("seq", "fsdp")
    )
    at = lax.axis_index("fsdp")
    attn_gain_grad = lax.dynamic_slice_in_dim(vector_sum, at * owned, owned)
    mlp_gain_grad = lax.dynamic_slice_in_dim(vector_sum, width + at * owned, owned)
    owned_bias = qkv_bias.shape[0]
    bias_grad = lax.dynamic_slice_in_dim(vector_sum, 2 * width + at * owned_bias, owned_bias)
    return (
        block_out[None],
        tokens_grad[None],
        attn_gain_grad,
        qkv_grad,
        bias_grad,
        proj_grad,
        mlp_gain_grad,
        gate_up_grad,
        down_grad,
    )


def solution(mesh):
    in_specs = (
        P("fsdp", "seq", None),
        P("fsdp", None),
        P("fsdp"),
        P("fsdp", None),
        P("fsdp"),
        P("fsdp", None),
        P("fsdp"),
        P("fsdp", None),
        P("fsdp", None),
        P("fsdp", "seq", None),
    )
    out_specs = (
        P("fsdp", "seq", None),
        P("fsdp", "seq", None),
        P("fsdp"),
        P("fsdp", None),
        P("fsdp"),
        P("fsdp", None),
        P("fsdp"),
        P("fsdp", None),
        P("fsdp", None),
    )
    return jax.shard_map(local, mesh=mesh, in_specs=in_specs, out_specs=out_specs, check_vma=False)
```

```python
import functools

import jax
import jax.numpy as jnp
from jax import lax
from jax.experimental import pallas as pl
from jax.experimental.pallas import tpu as pltpu
from jax.sharding import PartitionSpec as P

H = 12
KV = 2
HD = 128
EPSILON = 1e-06
THETA = 1000000.0
FLOOR = -1e30
LOW = jnp.bfloat16
F32 = jnp.float32


def inverse_rms(value):
    return lax.rsqrt(jnp.mean(value * value, axis=-1, keepdims=True) + EPSILON)


def turned(value):
    halfway = value.shape[-1] // 2
    return jnp.concatenate([-value[..., halfway:], value[..., :halfway]], axis=-1)


def turned_back(value):
    halfway = value.shape[-1] // 2
    return jnp.concatenate([value[..., halfway:], -value[..., :halfway]], axis=-1)


def norm_back(value, factor, gain, upstream):
    weighted = upstream * gain
    gain_term = jnp.sum(upstream * value * factor, axis=0)
    through = factor * weighted - value * factor**3 * jnp.mean(
        weighted * value, axis=-1, keepdims=True
    )
    return (through, gain_term)


def dot(left, right):
    return jnp.dot(left, right, preferred_element_type=F32)


def column_product(left, right):
    return lax.dot_general(left, right, (((0,), (0,)), ((), ())), preferred_element_type=F32)


def times_transpose(left, right):
    return lax.dot_general(left, right, (((1,), (1,)), ((), ())), preferred_element_type=F32)


def swap(value, axis, distance):
    return lax.ppermute(value, axis, [(i, i ^ distance) for i in range(lax.axis_size(axis))])


def lines():
    size = lax.axis_size("fsdp")
    return [list(range(first, size, 2)) for first in range(2)]


def line_reduce(value):
    return lax.psum_scatter(
        value, "fsdp", scatter_dimension=0, axis_index_groups=lines(), tiled=False
    )


def by_pair(own, other):
    second = lax.axis_index("fsdp") % 2 == 1
    return (jnp.where(second, other, own), jnp.where(second, own, other))


def pick(flag, first, second):
    return (jnp.where(flag, second, first), jnp.where(flag, first, second))


def after(value, *earlier):
    return lax.optimization_barrier((value, *earlier))[0]


def seq_blocks(value):
    across = swap(value, "seq", 2)
    return [value, swap(value, "seq", 1), across, swap(across, "seq", 1)]


def seq_reduce(parts):
    arrived = swap(jnp.stack([parts[1], parts[3]]), "seq", 1)
    across = (parts[2].astype(F32) + arrived[1].astype(F32)).astype(LOW)
    here = parts[0].astype(F32) + arrived[0].astype(F32)
    return here + swap(across, "seq", 2).astype(F32)


def in_order(blocks):
    me = lax.axis_index("seq")
    bits = 1
    while bits < len(blocks):
        flip = (me & bits) != 0
        blocks = [jnp.where(flip, blocks[k ^ bits], blocks[k]) for k in range(len(blocks))]
        bits *= 2
    return blocks


def relative(value):
    size = lax.axis_size("seq")
    me = lax.axis_index("seq")
    cut = value.reshape(size, value.shape[0] // size, *value.shape[1:])
    return [lax.dynamic_index_in_dim(cut, me ^ k, 0, keepdims=False) for k in range(size)]


def seq_exchange(pieces):
    taken = [part[0] for part in relative(pieces)]
    return in_order([taken[0]] + [swap(taken[k], "seq", k) for k in range(1, len(taken))])


MESH = pl.DeviceIdType.MESH


def neighbours():
    me, owner = lax.axis_index("seq"), lax.axis_index("fsdp")
    sibling = me + 1 - 2 * (me % 2)
    across = me + 2 - 4 * (me // 2 % 2)
    partner = owner + 1 - 2 * (owner % 2)
    return (me, sibling, across), ({"seq": sibling}, {"seq": across}, {"fsdp": partner})


def greet(devices):
    barrier = pltpu.get_barrier_semaphore()
    for device in devices:
        pl.semaphore_signal(barrier, inc=1, device_id=device, device_id_type=MESH)
    pl.semaphore_wait(barrier, len(devices))


class Sender:
    def __init__(self, send_sems, recv_sems):
        self.sems = (send_sems, recv_sems)
        self.copies = []

    def send(self, source, target, device):
        number = len(self.copies)
        copy = pltpu.make_async_remote_copy(
            src_ref=source,
            dst_ref=target,
            send_sem=self.sems[0].at[number],
            recv_sem=self.sems[1].at[number],
            device_id=device,
            device_id_type=MESH,
        )
        copy.start()
        self.copies.append(copy)
        return copy

    def finish(self):
        for copy in self.copies:
            copy.wait_send()


def whole_call(kernel, out_shapes, scratch, copies, number, args):
    sems = [pltpu.SemaphoreType.DMA((copies,))] * 2
    return pl.pallas_call(
        kernel,
        out_shape=out_shapes,
        in_specs=[pl.BlockSpec(memory_space=pltpu.VMEM)] * len(args),
        out_specs=[pl.BlockSpec(memory_space=pltpu.VMEM)] * len(out_shapes),
        scratch_shapes=[*scratch, *sems],
        compiler_params=pltpu.CompilerParams(
            collective_id=number, has_side_effects=True, vmem_limit_bytes=40 << 20
        ),
    )(*args)


def plane_gather(link, blocks, ids):
    core, over_x, over_y = ids
    rows = blocks.shape[1]
    halves = (pl.ds(0, rows // 2), pl.ds(rows // 2, rows // 2))
    to_x = [link.send(blocks.at[0, half], blocks.at[2, half], over_x) for half in halves]
    to_y = [link.send(blocks.at[0, half], blocks.at[4, half], over_y) for half in halves[::-1]]
    last = [link.send(blocks.at[0], blocks.at[1], core)]
    yield
    to_x[0].wait_recv()
    diagonal = [link.send(blocks.at[2, halves[0]], blocks.at[6, halves[0]], over_y)]
    last.append(link.send(blocks.at[2, halves[0]], blocks.at[3, halves[0]], core))
    to_y[0].wait_recv()
    diagonal.append(link.send(blocks.at[4, halves[1]], blocks.at[6, halves[1]], over_x))
    last.append(link.send(blocks.at[4, halves[1]], blocks.at[5, halves[1]], core))
    to_x[1].wait_recv()
    last.append(link.send(blocks.at[2, halves[1]], blocks.at[3, halves[1]], core))
    to_y[1].wait_recv()
    last.append(link.send(blocks.at[4, halves[0]], blocks.at[5, halves[0]], core))
    for copy, half in zip(diagonal, halves):
        copy.wait_recv()
        last.append(link.send(blocks.at[6, half], blocks.at[7, half], core))
    for copy in last:
        copy.wait_recv()
    yield


def opening_kernel(
    shape,
    tokens,
    cotangent,
    qkv,
    proj,
    ff_first,
    ff_second,
    cosines,
    sines,
    seg_col,
    seg_row,
    tokens_all,
    qkv_all,
    proj_mine,
    first_all,
    second_all,
    first_rows,
    second_rows,
    normed,
    queries,
    keys,
    values,
    merged,
    logsum,
    hidden,
    mids,
    cots,
    proj_all,
    weight,
    vectors,
    kv,
    part,
    arrived,
    summed,
    across_in,
    send_sems,
    recv_sems,
    local_sems,
):
    owned, vector_size, per_dev, group = shape
    (me, sibling, across), ids = neighbours()
    core, over_x, over_y = ids
    far = across + 1 - 2 * (across % 2)
    line = qkv_all.shape[0]
    size = 2 * line
    owner = lax.axis_index("fsdp")
    at, pair = owner // 2, owner % 2
    below, above = ({"fsdp": (owner + size - 2) % size}, {"fsdp": (owner + 2) % size})
    rows, width = tokens.shape
    seq_count = tokens_all.shape[0]
    seq_len = seq_count * rows
    halves = (pl.ds(0, rows // 2), pl.ds(rows // 2, rows // 2))
    others = (sibling, across, far)
    greet((*ids, {"seq": far}, below, above))
    link = Sender(send_sems, recv_sems)

    own_copies = []
    for number, (own, whole) in enumerate(((ff_first, first_all), (ff_second, second_all))):
        for place, source in enumerate((pair, 2)):
            copy = pltpu.make_async_copy(
                own.at[source], whole.at[at, source], local_sems.at[2 * number + place]
            )
            copy.start()
            own_copies.append(copy)
    tokens_all[me] = tokens[...]
    qkv_all[at, pair] = qkv[...]
    proj_all[at, pair] = proj[...]

    last = []

    def step(array, k):
        here = array.at[(at + k) % line, pair]
        onward = link.send(here, here, below) if k < line - 1 else None
        last.append(link.send(here, here, over_y))
        return onward

    onward = [step(array, 0) for array in (qkv_all, proj_all)]
    to_x = [link.send(tokens_all.at[me, half], tokens_all.at[me, half], over_x) for half in halves]
    last.append(link.send(tokens_all.at[me], tokens_all.at[me], core))
    for k in range(1, line):
        for number, array in enumerate((qkv_all, proj_all)):
            onward[number].wait_recv()
            onward[number] = step(array, k)

    turned_over = [
        link.send(own.at[1 - pair], whole.at[at, pair], over_y)
        for own, whole in ((ff_first, first_all), (ff_second, second_all))
    ]
    arrivals = []

    def ring_steps():
        for number, (own, whole) in enumerate(((ff_first, first_all), (ff_second, second_all))):
            before = None
            for k in range(line - 1):
                block, now = whole.at[(at + k) % line], []
                for place, part_of in enumerate((pair, 2, 1 - pair)):
                    if k > 0:
                        before[place].wait_recv()
                    elif place == 2:
                        turned_over[number].wait_recv()
                    source = own if k == 0 and place < 2 else block
                    now.append(link.send(source.at[part_of], block.at[part_of], below))
                before = now
                yield
            arrivals.append(before)

    ring = ring_steps()

    def pump(count=1):
        for _ in range(count):
            next(ring, None)

    def exchange_rows(number, whole, rows_mine):
        while len(arrivals) <= number:
            next(ring, None)
        for copy in arrivals[number]:
            copy.wait_recv()
        for copy in own_copies[2 * number : 2 * number + 2]:
            copy.wait()
        mine = whole.at[pl.ds(me * group, group), 2]
        copy = pltpu.make_async_copy(mine, rows_mine.at[me], local_sems.at[4 + number])
        copy.start()
        sent = [copy]
        for target in others:
            source = whole.at[pl.ds(target * group, group), 2]
            sent.append(link.send(source, rows_mine.at[me], {"seq": target}))
        return sent

    pump()
    for copy, half in zip(to_x, halves):
        copy.wait_recv()
        last.append(link.send(tokens_all.at[across, half], tokens_all.at[across, half], core))
    for copy in last:
        copy.wait_recv()
    cots[0] = cotangent[...]
    gather_cots = plane_gather(link, cots, ids)
    next(gather_cots)

    for z in range(line):
        for y in range(2):
            owner_row = 2 * z + y
            weight[pl.ds(owner_row * owned, owned), :] = qkv_all[z, y, :owned, :]
            done = 0
            cols = qkv_all.shape[3]
            for start, count, target in (
                (0, owned, 0),
                (owned, owned, 1),
                (2 * owned, vector_size - 2 * owned, 2),
            ):
                while count > 0:
                    row, col = start // cols, start % cols
                    span = min(count, cols - col)
                    length = (owned, owned, vector_size - 2 * owned)[target]
                    to = owner_row * length + (length - count)
                    vectors[target : target + 1, to : to + span] = qkv_all[
                        z, y, owned + row : owned + row + 1, col : col + span
                    ].astype(F32)
                    start, count = start + span, count - span
    exchange = [
        link.send(proj_all.at[pl.ds(target * group, group)], proj_mine.at[me], {"seq": target})
        for target in others
    ]
    proj_mine[me] = proj_all[pl.ds(me * group, group)]

    head_cols = per_dev * HD
    holds_values = me % 2 == 1
    kv_first = (H + KV * (me % 2) + me // 2) * HD
    bias = jnp.concatenate(
        [
            vectors[2:3, pl.ds(pl.multiple_of(me * head_cols, HD), head_cols)],
            vectors[2:3, pl.ds(pl.multiple_of(kv_first, HD), HD)],
        ],
        axis=1,
    )
    for block in range(seq_count):
        here = pl.ds(block * rows, rows)
        value = tokens_all[block].astype(F32)
        normal = (value * inverse_rms(value) * vectors[0:1, :width]).astype(LOW)
        normed[block] = normal
        projected = dot(normal, weight[...]) + bias
        cosine, sine = cosines[here, :], sines[here, :]

        def rotate(head):
            return head * cosine + pltpu.roll(head, HD // 2, 1) * sine

        for head in range(per_dev):
            queries[head, here, :] = rotate(projected[:, head * HD : (head + 1) * HD]).astype(LOW)
        plain = projected[:, head_cols:]
        kv[0, here, :] = jnp.where(holds_values, plain, rotate(plain)).astype(LOW)
    swapped = link.send(kv.at[0], kv.at[1], core)
    pump()
    swapped.wait_recv()
    keys[...] = jnp.where(holds_values, kv[1], kv[0])
    values[...] = jnp.where(holds_values, kv[0], kv[1])

    for block in range(seq_count):
        here, last_key = pl.ds(block * rows, rows), (block + 1) * rows
        row_index = block * rows + lax.broadcasted_iota(jnp.int32, (rows, last_key), 0)
        key_index = lax.broadcasted_iota(jnp.int32, (rows, last_key), 1)
        allowed = (key_index <= row_index) & (seg_col[here, :] == seg_row[:, :last_key])
        for head in range(per_dev):
            scores = times_transpose(queries[head, here, :], keys[:last_key, :]) * HD ** (-0.5)
            scores = jnp.where(allowed, scores, FLOOR)
            highest = jnp.max(scores, axis=-1, keepdims=True)
            exponent = jnp.exp(scores - highest)
            total = jnp.sum(exponent, axis=-1, keepdims=True)
            mixture = dot((exponent / total).astype(LOW), values[:last_key, :])
            merged[here, head * HD : (head + 1) * HD] = mixture.astype(LOW)
            logsum[head, here, :] = highest + jnp.log(total)
    for copy in exchange:
        copy.wait_recv()
    quarter = proj.shape[1]
    for block in range(seq_count):
        for k in range(seq_count):
            columns = proj_mine[k].reshape(-1, quarter)
            part[block, :, k * quarter : (k + 1) * quarter] = dot(
                merged[block * rows : (block + 1) * rows, :], columns
            ).astype(LOW)

    first = link.send(part.at[far], arrived.at[0], core)
    second = link.send(part.at[sibling], arrived.at[1], core)
    first.wait_recv()
    summed[...] = (part[across].astype(F32) + arrived[0].astype(F32)).astype(LOW)
    third = link.send(summed, across_in, over_x)
    second.wait_recv()
    hidden[...] = tokens[...].astype(F32) + (part[me].astype(F32) + arrived[1].astype(F32))
    pump(2)
    third.wait_recv()
    total = hidden[...] + across_in[...].astype(F32)
    hidden[...] = total
    mids[0] = (total * inverse_rms(total) * vectors[1:2, :width]).astype(LOW)
    for _ in plane_gather(link, mids, ids):
        pass
    exchanged = [exchange_rows(0, first_all, first_rows)]
    pump()
    next(gather_cots)
    exchanged.append(exchange_rows(1, second_all, second_rows))
    for kept, *sent in exchanged:
        kept.wait()
        for copy in sent:
            copy.wait_recv()
    link.finish()


def opening(tokens, cotangent, qkv, proj, ff_first, ff_second, tables, segments, sizes):
    owned, vector_size, per_dev, group, line = sizes
    rows, width = tokens.shape
    block = (rows, width)
    seq_len = 4 * rows
    cols = qkv.shape[1]
    heads = (seq_len, HD)
    vmem, hbm = (pl.BlockSpec(memory_space=pltpu.VMEM), pl.BlockSpec(memory_space=pl.ANY))

    def like(*shape, dtype=LOW):
        return jax.ShapeDtypeStruct(shape, dtype)

    outs = [
        (like(4, *block), vmem),
        (like(line, 2, *qkv.shape), vmem),
        (like(4, group, 2, *proj.shape), vmem),
        (like(line, *ff_first.shape), hbm),
        (like(line, *ff_second.shape), hbm),
        (like(4, group, *ff_first.shape[1:]), vmem),
        (like(4, group, *ff_second.shape[1:]), vmem),
        (like(4, *block), vmem),
        (like(per_dev, *heads), vmem),
        (like(*heads), vmem),
        (like(*heads), vmem),
        (like(seq_len, per_dev * HD), vmem),
        (like(per_dev, seq_len, 1, dtype=F32), vmem),
        (like(*block, dtype=F32), vmem),
        (like(8, *block), vmem),
        (like(8, *block), vmem),
    ]
    copies = 10 * line + 40
    return pl.pallas_call(
        functools.partial(opening_kernel, (owned, vector_size, per_dev, group)),
        out_shape=[shape for shape, _ in outs],
        in_specs=[vmem] * 10,
        out_specs=[place for _, place in outs],
        scratch_shapes=[
            pltpu.VMEM((line, 2, *proj.shape), LOW),
            pltpu.VMEM((width, cols), LOW),
            pltpu.VMEM((3, max(width, 2048)), F32),
            pltpu.VMEM((2, *heads), LOW),
            pltpu.VMEM((4, *block), LOW),
            pltpu.VMEM((2, *block), LOW),
            pltpu.VMEM(block, LOW),
            pltpu.VMEM(block, LOW),
            pltpu.SemaphoreType.DMA((copies,)),
            pltpu.SemaphoreType.DMA((copies,)),
            pltpu.SemaphoreType.DMA((6,)),
        ],
        compiler_params=pltpu.CompilerParams(
            collective_id=0, has_side_effects=True, vmem_limit_bytes=56 << 20
        ),
    )(tokens, cotangent, qkv, proj, ff_first, ff_second, *tables, *segments)


def return_kernel(
    part,
    hidden,
    upstream,
    gain,
    grad_hidden,
    gain_term,
    gathered,
    arrived,
    held,
    from_x,
    from_y,
    corner,
    send_sems,
    recv_sems,
):
    (me, _, across), (core, over_x, over_y) = neighbours()
    rows = hidden.shape[0]
    low, high = (pl.ds(0, rows // 2), pl.ds(rows // 2, rows // 2))
    greet((core, over_x, over_y))
    link = Sender(send_sems, recv_sems)
    halved = {k: link.send(part.at[k + 1], arrived.at[k // 2], core) for k in (6, 2, 4, 0)}

    def chip_sum(k):
        halved[k].wait_recv()
        return part[k].astype(F32) + arrived[k // 2].astype(F32)

    held[2] = chip_sum(6).astype(LOW)
    turn_y = link.send(held.at[2, low], corner.at[0], over_x)
    turn_x = link.send(held.at[2, high], corner.at[1], over_y)
    held[0] = chip_sum(2).astype(LOW)
    direct_x = link.send(held.at[0, low], from_x.at[low], over_x)
    held[1] = chip_sum(4).astype(LOW)
    direct_y = link.send(held.at[1, high], from_y.at[high], over_y)
    grad_hidden[...] = chip_sum(0)
    turn_x.wait_recv()
    held[0, high] = (held[0, high].astype(F32) + corner[1].astype(F32)).astype(LOW)
    late_x = link.send(held.at[0, high], from_x.at[high], over_x)
    turn_y.wait_recv()
    held[1, low] = (held[1, low].astype(F32) + corner[0].astype(F32)).astype(LOW)
    late_y = link.send(held.at[1, low], from_y.at[low], over_y)
    for copy in (direct_x, direct_y, late_x, late_y):
        copy.wait_recv()
    grad_mid = grad_hidden[...] + from_x[...].astype(F32) + from_y[...].astype(F32)
    through, term = norm_back(hidden[...], inverse_rms(hidden[...]), gain[...], grad_mid)
    gain_term[...] = term[None]
    total = upstream[...].astype(F32) + through
    grad_hidden[...] = total
    gathered[me] = total.astype(LOW)
    to_core = link.send(gathered.at[me], gathered.at[me], core)
    to_x = [link.send(gathered.at[me, half], gathered.at[me, half], over_x) for half in (low, high)]
    last = [to_core]
    for copy, half in zip(to_x, (low, high)):
        copy.wait_recv()
        last.append(link.send(gathered.at[across, half], gathered.at[across, half], core))
    for copy in last:
        copy.wait_recv()
    link.finish()


def return_call(part, hidden, upstream, gain):
    _, rows, width = part.shape
    block = (rows, width)
    return whole_call(
        return_kernel,
        [
            jax.ShapeDtypeStruct(block, F32),
            jax.ShapeDtypeStruct((1, width), F32),
            jax.ShapeDtypeStruct((4, *block), LOW),
        ],
        [
            pltpu.VMEM((4, *block), LOW),
            pltpu.VMEM((3, *block), LOW),
            pltpu.VMEM(block, LOW),
            pltpu.VMEM(block, LOW),
            pltpu.VMEM((2, rows // 2, width), LOW),
        ],
        15,
        2,
        (part, hidden, upstream, gain),
    )


def columns_kernel(place, *refs):
    *pieces, out = refs
    row = 0
    for piece in pieces:
        count, rows, quarter = piece.shape
        for k in range(count):
            here = place[0] + k - 2 * ((place[0] % 2) * (k % 2)) - 4 * (
                (place[0] // 2 % 2) * (k // 2 % 2)
            )
            out[pl.ds(row, rows), pl.ds(k * quarter, quarter)] = piece[here].astype(F32)
        row += rows


def columns_call(place, pieces):
    rows = sum(piece.shape[1] for piece in pieces)
    width = pieces[0].shape[0] * pieces[0].shape[2]
    return pl.pallas_call(
        columns_kernel,
        out_shape=jax.ShapeDtypeStruct((rows, width), F32),
        in_specs=[pl.BlockSpec(memory_space=pltpu.SMEM)]
        + [pl.BlockSpec(memory_space=pltpu.VMEM)] * len(pieces),
        out_specs=pl.BlockSpec(memory_space=pltpu.VMEM),
        compiler_params=pltpu.CompilerParams(vmem_limit_bytes=40 << 20),
    )(place, *pieces)


def down_kernel(fold, place, *refs):
    *pieces, out = refs
    row = 0
    for piece in pieces:
        count, owned, width = piece.shape
        span = width // fold
        for k in range(count):
            here = place[0] + k - 2 * ((place[0] % 2) * (k % 2)) - 4 * (
                (place[0] // 2 % 2) * (k // 2 % 2)
            )
            whole = piece[here].astype(F32)
            for j in range(fold):
                whole_part = whole[:, j * span : (j + 1) * span]
                out[pl.ds(row, span), pl.ds((k * fold + j) * owned, owned)] = whole_part.T
        row += span


def down_call(place, pieces, fold):
    rows = sum(piece.shape[2] // fold for piece in pieces)
    width = pieces[0].shape[0] * pieces[0].shape[1] * fold
    return pl.pallas_call(
        functools.partial(down_kernel, fold),
        out_shape=jax.ShapeDtypeStruct((rows, width), F32),
        in_specs=[pl.BlockSpec(memory_space=pltpu.SMEM)]
        + [pl.BlockSpec(memory_space=pltpu.VMEM)] * len(pieces),
        out_specs=pl.BlockSpec(memory_space=pltpu.VMEM),
        compiler_params=pltpu.CompilerParams(vmem_limit_bytes=40 << 20),
    )(place, *pieces)


def hidden_kernel(cuts, group, place, *refs):
    *pieces, out = refs
    units = cuts[-1][1]
    count = pieces[0].shape[0] // 2
    for k in range(count):
        here = place[0] + k - 2 * ((place[0] % 2) * (k % 2)) - 4 * (
            (place[0] // 2 % 2) * (k // 2 % 2)
        )
        for pair in range(2):
            entry = (pair + place[1] - 2 * pair * place[1]) * count + here
            for part in range(2):
                for member in range(group):
                    first = (((part * count + k) * group + member) * 2 + pair) * units
                    for piece, (low, high) in zip(pieces, cuts):
                        span = high - low
                        at = (part * group + member) * span
                        out[:, first + low : first + high] = piece[entry][
                            :, at : at + span
                        ].astype(F32)


def hidden_call(place, pieces, cuts, group):
    rows = pieces[0].shape[1]
    units = cuts[-1][1]
    width = 2 * 8 * group * units
    step = 16
    return pl.pallas_call(
        functools.partial(hidden_kernel, cuts, group),
        grid=(rows // step,),
        out_shape=jax.ShapeDtypeStruct((rows, width), F32),
        in_specs=[pl.BlockSpec(memory_space=pltpu.SMEM)]
        + [pl.BlockSpec((8, step, piece.shape[2]), lambda i: (0, i, 0)) for piece in pieces],
        out_specs=pl.BlockSpec((step, width), lambda i: (i, 0)),
        compiler_params=pltpu.CompilerParams(vmem_limit_bytes=40 << 20),
    )(place, *pieces)


def local(
    tokens,
    segment_ids,
    attn_gain,
    qkv_weight,
    qkv_bias,
    proj_weight,
    mlp_gain,
    gate_up_weight,
    down_weight,
    cotangent,
):
    seq_count = lax.axis_size("seq")
    fsdp_count = lax.axis_size("fsdp")
    line = fsdp_count // 2
    place = lax.axis_index("seq")
    odd = lax.axis_index("fsdp") % 2 == 1
    tok_rows, width = tokens.shape[1:]
    seq_len = tok_rows * seq_count
    owned = qkv_weight.shape[0]
    owned_hidden = down_weight.shape[0]
    hidden = owned_hidden * fsdp_count
    quarter = width // seq_count
    per_dev = H // seq_count
    head_cols = per_dev * HD
    score_scale = HD ** (-0.5)
    group = line // seq_count
    cut_at = owned_hidden // 2 // 128 * 128
    cuts = [(0, cut_at), (cut_at, owned_hidden)]

    holds_values = place % 2 == 1
    kv_first = (H + KV * (place % 2) + place // 2) * HD
    qkv_own = jnp.concatenate(
        [
            lax.dynamic_slice_in_dim(qkv_weight, place * head_cols, head_cols, 1),
            lax.dynamic_slice_in_dim(qkv_weight, kv_first, HD, 1),
        ],
        axis=1,
    )
    cols = head_cols + HD
    vector = jnp.concatenate([attn_gain, mlp_gain, qkv_bias])
    vector_size = vector.shape[0]
    vector_rows = -(-vector_size // (16 * cols)) * 16
    vector = jnp.pad(vector, (0, vector_rows * cols - vector_size)).reshape(vector_rows, cols)
    proj_cols = lax.dynamic_slice_in_dim(proj_weight, place * quarter, quarter, 1)
    down_cols = lax.dynamic_slice_in_dim(down_weight, place * quarter, quarter, 1)
    ff_all = jnp.stack(
        [
            lax.dynamic_slice_in_dim(
                gate_up_weight,
                first + place * group * 2 * owned_hidden,
                group * 2 * owned_hidden,
                1,
            ).reshape(owned, group, 2, owned_hidden)
            for first in (0, hidden)
        ]
    )
    fold = quarter // owned

    def folded(value):
        return jnp.concatenate(
            [value[..., j * owned : (j + 1) * owned, :] for j in range(fold)], axis=-1
        )

    def unfolded(value):
        span = value.shape[-1] // fold
        return jnp.concatenate(
            [value[..., j * span : (j + 1) * span] for j in range(fold)], axis=-2
        )

    ff_sent = []
    for low, high in cuts:
        ff_part = ff_all[:, :, :, :, low:high]
        by_owner = [
            jnp.concatenate(
                [ff_part[part, :, m, pair] for part in range(2) for m in range(group)], axis=1
            )
            for pair in range(2)
        ]
        ff_sent.append(jnp.stack([*by_owner, folded(jnp.transpose(down_cols[low:high]))]))

    segment_row = segment_ids[0]
    doc_starts = jnp.sum((segment_row[None, :] < segment_row[:, None]).astype(jnp.int32), axis=1)
    places = jnp.arange(seq_len, dtype=jnp.int32) - doc_starts
    inverse = THETA ** (-2.0 * jnp.arange(HD // 2, dtype=F32) / HD)
    angles = places.astype(F32)[:, None] * inverse[None, :]
    angles = jnp.concatenate([angles, angles], axis=-1)
    cosines = jnp.cos(angles)
    sines = jnp.sin(angles)

    signs = jnp.where(jnp.arange(HD) < HD // 2, -1.0, 1.0).astype(F32)
    (
        tokens_all,
        qkv_both,
        proj_mine,
        first_all,
        second_all,
        first_rows,
        second_rows,
        normed_in,
        queries,
        head_keys,
        head_values,
        merged,
        logsum,
        hidden_in,
        mids,
        cots,
    ) = opening(
        tokens[0],
        cotangent[0],
        jnp.concatenate([qkv_own, vector], axis=0),
        lax.dynamic_slice_in_dim(proj_weight, place * quarter, quarter, 1),
        *ff_sent,
        (cosines, sines * signs),
        (segment_row[:, None], segment_row[None]),
        (owned, vector_size, per_dev, group, line),
    )
    qkv_mine = qkv_both[:, :, :owned].reshape(width, cols)
    vectors = qkv_both[:, :, owned:].reshape(fsdp_count, vector_rows * cols)[:, :vector_size]
    gain_one = vectors[:, :owned].reshape(width).astype(F32)
    gain_two = vectors[:, owned : 2 * owned].reshape(width).astype(F32)
    proj_mine = jnp.moveaxis(proj_mine.reshape(seq_count, head_cols, quarter), 0, 1)
    proj_mine = proj_mine.reshape(head_cols, width)
    normed_in = normed_in.reshape(seq_len, width)
    resid = tokens[0].astype(F32)
    resid_all = tokens_all.reshape(seq_len, width).astype(F32)
    factor_all = inverse_rms(resid_all)
    mids = mids.reshape(2 * seq_len, width)
    cots = cots.reshape(2 * seq_len, width)
    gate_up_mine = [whole[:, :2].reshape(width, -1) for whole in (first_all, second_all)]
    down_mine = [
        jnp.moveaxis(unfolded(whole), 1, 2).reshape(width, -1)
        for whole in (first_rows, second_rows)
    ]
    block_rows = min(512, seq_len)
    blocks = seq_len // block_rows

    def scores_of(index):
        first, last = index * block_rows, (index + 1) * block_rows
        row_index = first + jnp.arange(block_rows, dtype=jnp.int32)
        key_index = jnp.arange(last, dtype=jnp.int32)
        allowed = (key_index[None, :] <= row_index[:, None]) & (
            segment_row[None, :last] == segment_row[first:last, None]
        )
        scores = (
            jnp.einsum(
                "hqd,kd->hqk", queries[:, first:last], head_keys[:last], preferred_element_type=F32
            )
            * score_scale
        )
        return (jnp.where(allowed[None], scores, FLOOR), allowed)

    def plane_reduce(total):
        parts = [total[k * tok_rows : (k + 1) * tok_rows] for k in range(2 * seq_count)]
        away = seq_reduce(parts[seq_count:]).astype(LOW)
        return seq_reduce(parts[:seq_count]) + swap(away, "fsdp", 1).astype(F32)

    outs, grad_mids, terms = [], [], []
    for gate_up_part, down_part in zip(gate_up_mine, down_mine):
        units = down_part.shape[1]
        gate_up = dot(after(mids, *terms[-1:]), gate_up_part)
        gate, upward = gate_up[:, :units], gate_up[:, units:]
        sigmoid_gate = jax.nn.sigmoid(gate)
        act = (gate * sigmoid_gate * upward).astype(LOW)
        grad_act = dot(cots, down_part)
        grad_gate = grad_act * upward * sigmoid_gate * (1.0 + gate * (1.0 - sigmoid_gate))
        grad_up = grad_act * gate * sigmoid_gate
        grad = jnp.concatenate([grad_gate, grad_up], axis=-1).astype(LOW)
        gate_up_term = column_product(mids, grad).astype(LOW).reshape(line, 2, owned, -1)
        down_term = column_product(cots, act).astype(LOW)
        down_term = jnp.moveaxis(down_term.reshape(seq_count, quarter, group, -1), 2, 1)
        down_term = jnp.stack(seq_exchange(down_term)).reshape(line, 1, quarter, -1)
        terms.append(jnp.concatenate([gate_up_term, folded(down_term)], axis=1))
        outs.append(times_transpose(act, down_part))
        grad_mids.append(times_transpose(grad, gate_up_part))
    grad_mid = after(sum(grad_mids).astype(LOW), *terms[-1:])
    grad_mid = grad_mid.reshape(2 * seq_count, tok_rows, width)
    grad_hidden, gain_two_term, grad_attended = return_call(
        grad_mid, hidden_in, cotangent[0], gain_two[None]
    )
    grad_attended = grad_attended.reshape(seq_len, width)
    block_out = (hidden_in + plane_reduce(sum(outs).astype(LOW))).astype(LOW)

    places_here = jnp.stack([place, lax.axis_index("fsdp") % 2]).astype(jnp.int32)
    down_pieces, hidden_pieces, sums = [], [], []
    for term in terms:
        summed = line_reduce(term)
        sums.append(summed)
        kept, given = pick(odd, summed[0], summed[1])
        here = seq_blocks(jnp.stack([kept, summed[2]]))
        hidden_pieces.append(
            jnp.stack([pair[0] for pair in here] + seq_blocks(swap(given, "fsdp", 1)))
        )
        down_pieces.append(jnp.stack([pair[1] for pair in here]))

    proj_term = column_product(merged, grad_attended).astype(LOW)
    grad_merged = times_transpose(grad_attended, proj_mine).astype(LOW)
    grad_heads = grad_merged.reshape(seq_len, per_dev, HD)
    grad_key = jnp.zeros((seq_len, HD), F32)
    grad_value = jnp.zeros((seq_len, HD), F32)
    grad_queries = []
    for index in range(blocks):
        first, last = index * block_rows, (index + 1) * block_rows
        scores, allowed = scores_of(index)
        probs = jnp.where(allowed[None], jnp.exp(scores - logsum[:, first:last]), 0.0)
        grad_block = grad_heads[first:last]
        grad_probs = jnp.einsum(
            "qhd,kd->hqk", grad_block, head_values[:last], preferred_element_type=F32
        )
        inner = jnp.sum(probs * grad_probs, axis=-1, keepdims=True)
        grad_scores = (probs * (grad_probs - inner)).astype(LOW)
        grad_queries.append(
            (
                jnp.einsum(
                    "hqk,kd->qhd", grad_scores, head_keys[:last], preferred_element_type=F32
                )
                * score_scale
            ).astype(LOW)
        )
        key_term = (
            jnp.einsum(
                "hqk,hqd->kd", grad_scores, queries[:, first:last], preferred_element_type=F32
            )
            * score_scale
        )
        value_term = jnp.einsum(
            "hqk,qhd->kd", probs.astype(LOW), grad_block, preferred_element_type=F32
        )
        grad_key = grad_key + jnp.pad(key_term, ((0, seq_len - last), (0, 0)))
        grad_value = grad_value + jnp.pad(value_term, ((0, seq_len - last), (0, 0)))
    kept_kv, given_kv = pick(holds_values, grad_key.astype(LOW), grad_value.astype(LOW))
    grad_kv = kept_kv.astype(F32) + swap(given_kv, "seq", 1).astype(F32)
    grad_q = jnp.concatenate(grad_queries, axis=0).astype(F32)
    grad_rot = jnp.concatenate([grad_q, grad_kv[:, None]], axis=1)
    unturned = grad_rot * cosines[:, None] + turned_back(grad_rot * sines[:, None])
    grad_projected = (
        jnp.concatenate(
            [
                unturned[:, :per_dev],
                jnp.where(holds_values, grad_kv[:, None], unturned[:, per_dev:]),
            ],
            axis=1,
        )
        .reshape(seq_len, cols)
        .astype(LOW)
    )
    grad_projected = after(grad_projected, sums[-1], hidden_pieces[0], down_pieces[0])
    bias_part = jnp.sum(grad_projected.astype(F32), axis=0)
    grad_in_part = times_transpose(grad_projected, qkv_mine)
    gain_one_part = jnp.sum(grad_in_part * resid_all * factor_all, axis=0)
    grad_in = seq_reduce(relative(grad_in_part.astype(LOW)))
    qkv_term = column_product(normed_in, grad_projected).astype(LOW)
    through_one, _ = norm_back(resid, inverse_rms(resid), gain_one, grad_in)
    tokens_grad = grad_hidden + through_one

    def pair_sum(value):
        kept_rows, given_rows = pick(odd, value[:, 0], value[:, 1])
        arrived = swap(given_rows, "fsdp", 1)
        return (kept_rows.astype(F32) + arrived.astype(F32)).astype(LOW)

    def col_exchange(value):
        rows = value.shape[0]
        cut = jnp.stack([value[:, k * quarter : (k + 1) * quarter] for k in range(seq_count)])
        return jnp.stack(seq_exchange(cut)).reshape(line, rows // group, quarter)

    down_grad = down_call(places_here, down_pieces, fold)
    gate_up_grad = hidden_call(places_here, hidden_pieces, cuts, group)
    proj_sum = pair_sum(proj_term.reshape(group, 2, owned, width)).reshape(group * owned, width)
    proj_sum = col_exchange(proj_sum)

    bias_term = jnp.zeros(qkv_weight.shape[1], F32)
    bias_term = lax.dynamic_update_slice_in_dim(
        bias_term, bias_part[:head_cols], place * head_cols, 0
    )
    bias_term = lax.dynamic_update_slice_in_dim(bias_term, bias_part[head_cols:], kv_first, 0)
    vector_terms = jnp.concatenate(
        [term.reshape(fsdp_count, -1) for term in (gain_one_part, gain_two_term, bias_term)],
        axis=1,
    )
    vector_terms = jnp.pad(vector_terms, ((0, 0), (0, vector_rows * cols - vector_size)))
    qkv_packed = jnp.concatenate(
        [
            qkv_term.reshape(line, 2, owned, cols),
            vector_terms.astype(LOW).reshape(line, 2, vector_rows, cols),
        ],
        axis=2,
    )
    qkv_packed = pair_sum(qkv_packed)
    proj_sum = jnp.pad(proj_sum, ((0, 0), (0, vector_rows), (0, 0)))
    attn_sums = seq_blocks(line_reduce(jnp.concatenate([qkv_packed, proj_sum], axis=-1)))
    proj_grad = columns_call(
        places_here, [jnp.stack([part[:owned, cols:] for part in attn_sums])]
    )
    qkv_sums = in_order([part[:, :cols] for part in attn_sums])
    qkv_grad = jnp.concatenate(
        [part[:owned, :head_cols] for part in qkv_sums]
        + [part[:owned, head_cols:] for part in qkv_sums[0::2]]
        + [part[:owned, head_cols:] for part in qkv_sums[1::2]],
        axis=-1,
    ).astype(F32)
    vector_sum = sum(part[owned:].astype(F32) for part in qkv_sums).reshape(-1)
    return (
        block_out[None],
        tokens_grad[None],
        vector_sum[:owned],
        qkv_grad,
        vector_sum[2 * owned : vector_size],
        proj_grad,
        vector_sum[owned : 2 * owned],
        gate_up_grad,
        down_grad,
    )


def solution(mesh):
    in_specs = (
        P("fsdp", "seq", None),
        P("fsdp", None),
        P("fsdp"),
        P("fsdp", None),
        P("fsdp"),
        P("fsdp", None),
        P("fsdp"),
        P("fsdp", None),
        P("fsdp", None),
        P("fsdp", "seq", None),
    )
    out_specs = (
        P("fsdp", "seq", None),
        P("fsdp", "seq", None),
        P("fsdp"),
        P("fsdp", None),
        P("fsdp"),
        P("fsdp", None),
        P("fsdp"),
        P("fsdp", None),
        P("fsdp", None),
    )
    return jax.shard_map(local, mesh=mesh, in_specs=in_specs, out_specs=out_specs, check_vma=False)
```

```python
import functools

import jax
import jax.numpy as jnp
from jax import lax
from jax.experimental import pallas as pl
from jax.experimental.pallas import tpu as pltpu
from jax.sharding import PartitionSpec as P

H = 12
KV = 2
HD = 128
EPSILON = 1e-06
THETA = 1000000.0
FLOOR = -1e30
LOW = jnp.bfloat16
F32 = jnp.float32


def inverse_rms(value):
    return lax.rsqrt(jnp.mean(value * value, axis=-1, keepdims=True) + EPSILON)


def turned(value):
    halfway = value.shape[-1] // 2
    return jnp.concatenate([-value[..., halfway:], value[..., :halfway]], axis=-1)


def turned_back(value):
    halfway = value.shape[-1] // 2
    return jnp.concatenate([value[..., halfway:], -value[..., :halfway]], axis=-1)


def norm_back(value, factor, gain, upstream):
    weighted = upstream * gain
    gain_term = jnp.sum(upstream * value * factor, axis=0)
    through = factor * weighted - value * factor**3 * jnp.mean(
        weighted * value, axis=-1, keepdims=True
    )
    return (through, gain_term)


def dot(left, right):
    return jnp.dot(left, right, preferred_element_type=F32)


def column_product(left, right):
    return lax.dot_general(left, right, (((0,), (0,)), ((), ())), preferred_element_type=F32)


def times_transpose(left, right):
    return lax.dot_general(left, right, (((1,), (1,)), ((), ())), preferred_element_type=F32)


def swap(value, axis, distance):
    return lax.ppermute(value, axis, [(i, i ^ distance) for i in range(lax.axis_size(axis))])


def lines():
    size = lax.axis_size("fsdp")
    return [list(range(first, size, 2)) for first in range(2)]


def line_gather(value):
    return lax.all_gather(value, "fsdp", axis=0, axis_index_groups=lines(), tiled=False)


def line_reduce(value):
    return lax.psum_scatter(
        value, "fsdp", scatter_dimension=0, axis_index_groups=lines(), tiled=False
    )


def by_pair(own, other):
    second = lax.axis_index("fsdp") % 2 == 1
    return (jnp.where(second, other, own), jnp.where(second, own, other))


def pick(flag, first, second):
    return (jnp.where(flag, second, first), jnp.where(flag, first, second))


def nought(value):
    return jnp.minimum(jnp.abs(value), 0.0).astype(LOW)


def seq_blocks(value):
    across = swap(value, "seq", 2)
    return [value, swap(value, "seq", 1), across, swap(across, "seq", 1)]


def seq_reduce(parts):
    arrived = swap(jnp.stack([parts[1], parts[3]]), "seq", 1)
    across = (parts[2].astype(F32) + arrived[1].astype(F32)).astype(LOW)
    here = parts[0].astype(F32) + arrived[0].astype(F32)
    return here + swap(across, "seq", 2).astype(F32)


def in_order(blocks):
    me = lax.axis_index("seq")
    bits = 1
    while bits < len(blocks):
        flip = (me & bits) != 0
        blocks = [jnp.where(flip, blocks[k ^ bits], blocks[k]) for k in range(len(blocks))]
        bits *= 2
    return blocks


def relative(value):
    size = lax.axis_size("seq")
    me = lax.axis_index("seq")
    cut = value.reshape(size, value.shape[0] // size, *value.shape[1:])
    return [lax.dynamic_index_in_dim(cut, me ^ k, 0, keepdims=False) for k in range(size)]


def seq_exchange(pieces):
    taken = [part[0] for part in relative(pieces)]
    return in_order([taken[0]] + [swap(taken[k], "seq", k) for k in range(1, len(taken))])


MESH = pl.DeviceIdType.MESH


def neighbours():
    me, owner = lax.axis_index("seq"), lax.axis_index("fsdp")
    sibling = me + 1 - 2 * (me % 2)
    across = me + 2 - 4 * (me // 2 % 2)
    partner = owner + 1 - 2 * (owner % 2)
    return (me, sibling, across), ({"seq": sibling}, {"seq": across}, {"fsdp": partner})


def greet(devices):
    barrier = pltpu.get_barrier_semaphore()
    for device in devices:
        pl.semaphore_signal(barrier, inc=1, device_id=device, device_id_type=MESH)
    pl.semaphore_wait(barrier, len(devices))


class Sender:
    def __init__(self, send_sems, recv_sems):
        self.sems = (send_sems, recv_sems)
        self.count, self.open = 0, []

    def send(self, source, target, device):
        number = self.count
        copy = pltpu.make_async_remote_copy(
            src_ref=source,
            dst_ref=target,
            send_sem=self.sems[0].at[number],
            recv_sem=self.sems[1].at[number],
            device_id=device,
            device_id_type=MESH,
        )
        copy.start()
        self.count += 1
        self.open.append(copy)
        return copy

    def release(self, *copies):
        for copy in copies:
            copy.wait_send()
            self.open = [other for other in self.open if other is not copy]

    def finish(self):
        self.release(*self.open)


def plane_gather(link, blocks, ids):
    core, over_x, over_y = ids
    rows = blocks.shape[1]
    halves = (pl.ds(0, rows // 2), pl.ds(rows // 2, rows // 2))
    to_x = [link.send(blocks.at[0, half], blocks.at[2, half], over_x) for half in halves]
    to_y = [link.send(blocks.at[0, half], blocks.at[4, half], over_y) for half in halves[::-1]]
    last = [link.send(blocks.at[0], blocks.at[1], core)]
    yield
    to_x[0].wait_recv()
    diagonal = [link.send(blocks.at[2, halves[0]], blocks.at[6, halves[0]], over_y)]
    last.append(link.send(blocks.at[2, halves[0]], blocks.at[3, halves[0]], core))
    to_y[0].wait_recv()
    diagonal.append(link.send(blocks.at[4, halves[1]], blocks.at[6, halves[1]], over_x))
    last.append(link.send(blocks.at[4, halves[1]], blocks.at[5, halves[1]], core))
    to_x[1].wait_recv()
    last.append(link.send(blocks.at[2, halves[1]], blocks.at[3, halves[1]], core))
    to_y[1].wait_recv()
    last.append(link.send(blocks.at[4, halves[0]], blocks.at[5, halves[0]], core))
    for copy, half in zip(diagonal, halves):
        copy.wait_recv()
        last.append(link.send(blocks.at[6, half], blocks.at[7, half], core))
    for copy in last:
        copy.wait_recv()
    yield


def opening_kernel(
    shape,
    tokens,
    cotangent,
    qkv,
    proj,
    ff_own,
    ff_down,
    cosines,
    sines,
    seg_col,
    seg_row,
    tokens_all,
    weight,
    vectors,
    proj_mine,
    ff_all,
    ff_rows,
    normed,
    queries,
    keys,
    values,
    merged,
    logsum,
    part,
    cots,
    qkv_all,
    proj_all,
    ff_line,
    kv,
    send_sems,
    recv_sems,
    hand_send,
    hand_recv,
    local_sem,
):
    owned, vector_size, per_dev, group = shape
    (me, sibling, across), ids = neighbours()
    core, over_x, over_y = ids
    far = across + 1 - 2 * (across % 2)
    line = qkv_all.shape[0]
    size = 2 * line
    owner = lax.axis_index("fsdp")
    at, pair = owner // 2, owner % 2
    below, above = ({"fsdp": (owner + size - 2) % size}, {"fsdp": (owner + 2) % size})
    rows, width = tokens.shape
    seq_count = tokens_all.shape[0]
    seq_len = seq_count * rows
    halves = (pl.ds(0, rows // 2), pl.ds(rows // 2, rows // 2))
    others = (sibling, across, far)
    greet((*ids, {"seq": far}, below, above))
    link = Sender(send_sems, recv_sems)

    own_copy = pltpu.make_async_copy(ff_own.at[pair], ff_all.at[at, pair], local_sem)
    own_copy.start()
    ff_line[at] = ff_down[...]
    tokens_all[me] = tokens[...]
    qkv_all[at, pair] = qkv[...]
    proj_all[at, pair] = proj[...]

    turned, handed = [], []

    def hand_on(k):
        z = (at + k) % line
        target, member = z // group, z % group
        copy = pltpu.make_async_remote_copy(
            src_ref=ff_line.at[z],
            dst_ref=ff_rows.at[me, member],
            send_sem=hand_send.at[k],
            recv_sem=hand_recv.at[me * group + member],
            device_id={"seq": target},
            device_id_type=MESH,
        )

        @pl.when(target != me)
        def _():
            copy.start()

        @pl.when(target == me)
        def _():
            ff_rows[me, member] = ff_line[z]

        handed.append((copy, target))

    def ring_steps():
        before = [None] * 3
        for k in range(line):
            z = (at + k) % line
            here = (ff_line.at[z], ff_all.at[z, pair], ff_all.at[z, 1 - pair])
            for place, target in enumerate(here):
                source = ff_own.at[pair] if k == 0 and place == 1 else target
                if k > 0:
                    before[place].wait_recv()
                elif place == 2:
                    turned[0].wait_recv()
                if k < line - 1:
                    before[place] = link.send(source, target, below)
                if place == 0:
                    hand_on(k)
                yield

    ring = ring_steps()

    def pump(count):
        for _ in range(count):
            next(ring, None)

    def along_line(array, k):
        here = array.at[(at + k) % line, pair]
        return link.send(here, here, below)

    def to_partner(array, k):
        here = array.at[(at + k) % line, pair]
        return link.send(here, here, over_y)

    onward = along_line(qkv_all, 0)
    last = [to_partner(qkv_all, 0)]
    to_x = [link.send(tokens_all.at[me, half], tokens_all.at[me, half], over_x) for half in halves]
    last.append(link.send(tokens_all.at[me], tokens_all.at[me], core))
    proj_onward = along_line(proj_all, 0)
    for k in range(1, line):
        onward.wait_recv()
        if k < line - 1:
            onward = along_line(qkv_all, k)
        last.append(to_partner(qkv_all, k))
        proj_onward.wait_recv()
        if k < line - 1:
            proj_onward = along_line(proj_all, k)
    turned.append(link.send(ff_own.at[1 - pair], ff_all.at[at, pair], over_y))
    pump(2)
    for copy, half in zip(to_x, halves):
        copy.wait_recv()
        last.append(link.send(tokens_all.at[across, half], tokens_all.at[across, half], core))
    for copy in last:
        copy.wait_recv()
    proj_over = [to_partner(proj_all, k) for k in range(line)]
    cots[0] = cotangent[...]

    for z in range(line):
        for y in range(2):
            owner_row = 2 * z + y
            weight[pl.ds(owner_row * owned, owned), :] = qkv_all[z, y, :owned, :]
            done = 0
            cols = qkv_all.shape[3]
            for start, count, target in (
                (0, owned, 0),
                (owned, owned, 1),
                (2 * owned, vector_size - 2 * owned, 2),
            ):
                while count > 0:
                    row, col = start // cols, start % cols
                    span = min(count, cols - col)
                    length = (owned, owned, vector_size - 2 * owned)[target]
                    to = owner_row * length + (length - count)
                    vectors[target : target + 1, to : to + span] = qkv_all[
                        z, y, owned + row : owned + row + 1, col : col + span
                    ].astype(F32)
                    start, count = start + span, count - span

    head_cols = per_dev * HD
    holds_values = me % 2 == 1
    kv_first = (H + KV * (me % 2) + me // 2) * HD
    bias = jnp.concatenate(
        [
            vectors[2:3, pl.ds(pl.multiple_of(me * head_cols, HD), head_cols)],
            vectors[2:3, pl.ds(pl.multiple_of(kv_first, HD), HD)],
        ],
        axis=1,
    )
    for block in range(seq_count):
        here = pl.ds(block * rows, rows)
        value = tokens_all[block].astype(F32)
        normal = (value * inverse_rms(value) * vectors[0:1, :width]).astype(LOW)
        normed[block] = normal
        projected = dot(normal, weight[...]) + bias
        cosine, sine = cosines[here, :], sines[here, :]

        def rotate(head):
            return head * cosine + pltpu.roll(head, HD // 2, 1) * sine

        for head in range(per_dev):
            queries[head, here, :] = rotate(projected[:, head * HD : (head + 1) * HD]).astype(LOW)
        plain = projected[:, head_cols:]
        kv[0, here, :] = jnp.where(holds_values, plain, rotate(plain)).astype(LOW)
    swapped = link.send(kv.at[0], kv.at[1], core)
    pump(3)
    swapped.wait_recv()
    keys[...] = jnp.where(holds_values, kv[1], kv[0])
    values[...] = jnp.where(holds_values, kv[0], kv[1])

    for copy in proj_over:
        copy.wait_recv()
    exchange = [
        link.send(proj_all.at[pl.ds(target * group, group)], proj_mine.at[me], {"seq": target})
        for target in others
    ]
    gather_cots = plane_gather(link, cots, ids)
    next(gather_cots)
    proj_mine[me] = proj_all[pl.ds(me * group, group)]

    for block in range(seq_count):
        here, last_key = pl.ds(block * rows, rows), (block + 1) * rows
        row_index = block * rows + lax.broadcasted_iota(jnp.int32, (rows, last_key), 0)
        key_index = lax.broadcasted_iota(jnp.int32, (rows, last_key), 1)
        allowed = (key_index <= row_index) & (seg_col[here, :] == seg_row[:, :last_key])
        for head in range(per_dev):
            scores = times_transpose(queries[head, here, :], keys[:last_key, :]) * HD ** (-0.5)
            scores = jnp.where(allowed, scores, FLOOR)
            highest = jnp.max(scores, axis=-1, keepdims=True)
            exponent = jnp.exp(scores - highest)
            total = jnp.sum(exponent, axis=-1, keepdims=True)
            mixture = dot((exponent / total).astype(LOW), values[:last_key, :])
            merged[here, head * HD : (head + 1) * HD] = mixture.astype(LOW)
            logsum[head, here, :] = highest + jnp.log(total)
        pump(1)
    for copy in exchange:
        copy.wait_recv()
    quarter = proj.shape[1]
    for block in range(seq_count):
        for k in range(seq_count):
            columns = proj_mine[k].reshape(-1, quarter)
            part[block, :, k * quarter : (k + 1) * quarter] = dot(
                merged[block * rows : (block + 1) * rows, :], columns
            ).astype(LOW)

    pump(6)
    next(gather_cots)
    pump(3 * line)
    own_copy.wait()
    for source in others:
        for member in range(group):
            pltpu.make_async_remote_copy(
                src_ref=ff_line.at[0],
                dst_ref=ff_rows.at[source, member],
                send_sem=hand_send.at[0],
                recv_sem=hand_recv.at[source * group + member],
                device_id=core,
                device_id_type=MESH,
            ).wait_recv()
    for copy, target in handed:

        @pl.when(target != me)
        def _():
            copy.wait_send()

    link.finish()


def opening(tokens, cotangent, qkv, proj, ff, tables, segments, sizes):
    owned, vector_size, per_dev, group, line = sizes
    rows, width = tokens.shape
    block = (rows, width)
    seq_len = 4 * rows
    cols = qkv.shape[1]
    heads = (seq_len, HD)
    vmem, hbm = (pl.BlockSpec(memory_space=pltpu.VMEM), pl.BlockSpec(memory_space=pl.ANY))

    def like(*shape, dtype=LOW):
        return jax.ShapeDtypeStruct(shape, dtype)

    outs = [
        (like(4, *block), vmem),
        (like(width, cols), vmem),
        (like(3, max(width, 2048), dtype=F32), vmem),
        (like(4, group, 2, *proj.shape), vmem),
        (like(line, *ff[0].shape), hbm),
        (like(4, group, *ff[1].shape), vmem),
        (like(4, *block), vmem),
        (like(per_dev, *heads), vmem),
        (like(*heads), vmem),
        (like(*heads), vmem),
        (like(seq_len, per_dev * HD), vmem),
        (like(per_dev, seq_len, 1, dtype=F32), vmem),
        (like(4, *block), vmem),
        (like(8, *block), vmem),
    ]
    copies = 10 * line + 40
    return pl.pallas_call(
        functools.partial(opening_kernel, (owned, vector_size, per_dev, group)),
        out_shape=[shape for shape, _ in outs],
        in_specs=[vmem] * 10,
        out_specs=[place for _, place in outs],
        scratch_shapes=[
            pltpu.VMEM((line, 2, *qkv.shape), LOW),
            pltpu.VMEM((line, 2, *proj.shape), LOW),
            pltpu.VMEM((line, *ff[1].shape), LOW),
            pltpu.VMEM((2, *heads), LOW),
            pltpu.SemaphoreType.DMA((copies,)),
            pltpu.SemaphoreType.DMA((copies,)),
            pltpu.SemaphoreType.DMA((line,)),
            pltpu.SemaphoreType.DMA((4 * group,)),
            pltpu.SemaphoreType.DMA,
        ],
        cost_estimate=pl.CostEstimate(
            flops=100_000_000_000, bytes_accessed=40_000_000, transcendentals=4_000_000
        ),
        compiler_params=pltpu.CompilerParams(
            collective_id=0, has_side_effects=True, vmem_limit_bytes=56 << 20
        ),
    )(tokens, cotangent, qkv, proj, *ff, *tables, *segments)


def middle_kernel(
    part, tokens, vectors, hidden, mids, arrived, summed, across_in, send_sems, recv_sems
):
    (me, sibling, across), ids = neighbours()
    far = across + 1 - 2 * (across % 2)
    width = tokens.shape[1]
    greet(ids)
    link = Sender(send_sems, recv_sems)
    first = link.send(part.at[far], arrived.at[0], ids[0])
    second = link.send(part.at[sibling], arrived.at[1], ids[0])
    first.wait_recv()
    summed[...] = (part[across].astype(F32) + arrived[0].astype(F32)).astype(LOW)
    third = link.send(summed, across_in, ids[1])
    second.wait_recv()
    hidden[...] = tokens[...].astype(F32) + (part[me].astype(F32) + arrived[1].astype(F32))
    third.wait_recv()
    total = hidden[...] + across_in[...].astype(F32)
    hidden[...] = total
    mids[0] = (total * inverse_rms(total) * vectors[1:2, :width]).astype(LOW)
    for _ in plane_gather(link, mids, ids):
        pass
    link.finish()


def middle(part, tokens, vectors):
    block = tokens.shape
    vmem = pl.BlockSpec(memory_space=pltpu.VMEM)
    return pl.pallas_call(
        middle_kernel,
        out_shape=[jax.ShapeDtypeStruct(block, F32), jax.ShapeDtypeStruct((8, *block), LOW)],
        in_specs=[vmem] * 3,
        out_specs=[vmem] * 2,
        scratch_shapes=[
            pltpu.VMEM((2, *block), LOW),
            pltpu.VMEM(block, LOW),
            pltpu.VMEM(block, LOW),
            pltpu.SemaphoreType.DMA((16,)),
            pltpu.SemaphoreType.DMA((16,)),
        ],
        compiler_params=pltpu.CompilerParams(
            collective_id=1, has_side_effects=True, vmem_limit_bytes=32 << 20
        ),
    )(part, tokens, vectors)


def cut_kernel(shape, *refs):
    follows, group, units = shape
    if follows:
        mids_in, cots_in, whole_in, out_before, mid_before, *refs = refs
    else:
        mids_in, cots_in, weight_in, rows_in, *refs = refs
    term, out, mid, mids, cots, weight, rows, down, act, grad, part, stage, *refs = refs
    before, load_sems, weight_sems, stage_sems, before_sems, send_sems, recv_sems = refs
    (me, sibling, across), ids = neighbours()
    far = across + 1 - 2 * (across % 2)
    others = (sibling, across, far)
    line, _, owned, cols = weight.shape
    count, block, width = mids.shape
    quarter = width // 4
    fold = quarter // owned
    greet((ids[0], ids[1], {"seq": far}))
    link = Sender(send_sems, recv_sems)

    def load(source, target, sem):
        copy = pltpu.make_async_copy(source, target, sem)
        copy.start()
        return copy

    if follows:
        sent = [
            link.send(whole_in.at[pl.ds(k * group, group), 2], rows.at[me], {"seq": k})
            for k in others
        ]
        loads = [load(whole_in.at[pl.ds(me * group, group), 2], rows.at[me], weight_sems.at[line])]
        loads += [
            load(whole_in.at[z, pl.ds(0, 2)], weight.at[z], weight_sems.at[z]) for z in range(line)
        ]
    else:
        sent = []
        loads = [load(rows_in, rows, weight_sems.at[line]), load(weight_in, weight, weight_sems.at[0])]
    for t in range(count):
        load(mids_in.at[t], mids.at[t], load_sems.at[0, t])
        load(cots_in.at[t], cots.at[t], load_sems.at[1, t])
    for copy in loads:
        copy.wait()
    for copy in sent:
        copy.wait_recv()
    for k in range(4):
        for member in range(group):
            for j in range(fold):
                first = k * quarter + j * owned
                down[first : first + owned, member * units : (member + 1) * units] = rows[
                    k, member, :, j * units : (j + 1) * units
                ]

    def tokens(t, carry):
        pltpu.make_async_copy(mids_in.at[t], mids.at[t], load_sems.at[0, t]).wait()
        pltpu.make_async_copy(cots_in.at[t], cots.at[t], load_sems.at[1, t]).wait()
        gate_up = dot(mids[t], weight[...].reshape(width, cols))
        grad_act = dot(cots[t], down[...])
        gate, upward = gate_up[:, : cols // 2], gate_up[:, cols // 2 :]
        sigmoid_gate = jax.nn.sigmoid(gate)
        silu = gate * sigmoid_gate
        act[t] = (silu * upward).astype(LOW)
        grad[t, :, : cols // 2] = (
            grad_act * upward * sigmoid_gate * (1.0 + gate * (1.0 - sigmoid_gate))
        ).astype(LOW)
        grad[t, :, cols // 2 :] = (grad_act * silu).astype(LOW)
        return carry

    lax.fori_loop(0, count, tokens, 0)

    all_act = act[...].reshape(count * block, cols // 2)
    for k in range(4):
        value = column_product(
            cots[:, :, k * quarter : (k + 1) * quarter].reshape(count * block, quarter), all_act
        ).astype(LOW)
        for member in range(group):
            for j in range(fold):
                part[k, member, :, j * units : (j + 1) * units] = value[
                    j * owned : (j + 1) * owned, member * units : (member + 1) * units
                ]
    sent = [
        link.send(part.at[k], term.at[pl.ds(me * group, group), 2], {"seq": k}) for k in others
    ]
    term[pl.ds(me * group, group), 2] = part[me]
    all_grad = grad[...].reshape(count * block, cols)
    for z in range(line):
        value = column_product(
            mids[:, :, 2 * owned * z : 2 * owned * (z + 1)].reshape(count * block, 2 * owned),
            all_grad,
        ).astype(LOW)
        for y in range(2):
            term[z, y] = value[y * owned : (y + 1) * owned, :]

    def ask(t, slot):
        for place, source in enumerate((out_before, mid_before)):
            load(source.at[t], before.at[slot, place], before_sems.at[slot, place])

    if follows:
        ask(0, 0)

    def back(t, carry):
        slot = t % 2

        def hand_over(t, place, target):
            return pltpu.make_async_copy(
                stage.at[t % 2, place], target.at[t], stage_sems.at[t % 2, place]
            )

        @pl.when(t >= 2)
        def _():
            hand_over(t - 2, 0, out).wait()
            hand_over(t - 2, 1, mid).wait()

        values = [
            times_transpose(act[t], down[...]),
            times_transpose(grad[t], weight[...].reshape(width, cols)),
        ]
        if follows:

            @pl.when(t + 1 < count)
            def _():
                ask(t + 1, (t + 1) % 2)

            for place, source in enumerate((out_before, mid_before)):
                pltpu.make_async_copy(
                    source.at[t], before.at[slot, place], before_sems.at[slot, place]
                ).wait()
                values[place] = values[place] + before[slot, place].astype(F32)
        for place, target in enumerate((out, mid)):
            stage[slot, place] = values[place].astype(LOW)
            hand_over(t, place, target).start()
        return carry

    lax.fori_loop(0, count, back, 0)
    for t in (count - 2, count - 1):
        for place, target in enumerate((out, mid)):
            pltpu.make_async_copy(
                stage.at[t % 2, place], target.at[t], stage_sems.at[t % 2, place]
            ).wait()
    for copy in sent:
        copy.wait_recv()
    link.finish()


def cut_call(follows, args, sizes):
    group, line, owned, units = sizes
    mids = args[0]
    count, block, width = mids.shape
    cols = 2 * group * units
    hbm, vmem = (pl.BlockSpec(memory_space=pl.ANY), pl.BlockSpec(memory_space=pltpu.VMEM))
    rows = (4, group, owned, cols)
    low_scratch = [
        mids.shape,
        mids.shape,
        (line, 2, owned, cols),
        rows,
        (width, cols // 2),
        (count, block, cols // 2),
        (count, block, cols),
        rows,
        (2, 2, block, width),
        (2, 2, block, width),
    ]
    return pl.pallas_call(
        functools.partial(cut_kernel, (follows, group, units)),
        out_shape=[
            jax.ShapeDtypeStruct((line, 3, owned, cols), LOW),
            jax.ShapeDtypeStruct(mids.shape, LOW),
            jax.ShapeDtypeStruct(mids.shape, LOW),
        ],
        in_specs=[hbm] * len(args),
        out_specs=[vmem, hbm, hbm],
        scratch_shapes=[pltpu.VMEM(shape, LOW) for shape in low_scratch]
        + [
            pltpu.SemaphoreType.DMA((2, count)),
            pltpu.SemaphoreType.DMA((line + 1,)),
            pltpu.SemaphoreType.DMA((2, 2)),
            pltpu.SemaphoreType.DMA((2, 2)),
            pltpu.SemaphoreType.DMA((6,)),
            pltpu.SemaphoreType.DMA((6,)),
        ],
        compiler_params=pltpu.CompilerParams(
            collective_id=4 if follows else 3, has_side_effects=True, vmem_limit_bytes=56 << 20
        ),
        cost_estimate=pl.CostEstimate(
            flops=50_000_000_000, bytes_accessed=40_000_000, transcendentals=2_000_000
        ),
    )(*args)


def spread_blocks(link, ids, pair, ff_sum, hidden_blocks, down_blocks, local_sems):
    core, over_x, over_y = ids
    kept, down = ff_sum.at[pair], ff_sum.at[2]
    local = [
        pltpu.make_async_copy(kept, hidden_blocks.at[0], local_sems.at[0]),
        pltpu.make_async_copy(down, down_blocks.at[0], local_sems.at[1]),
    ]
    for copy in local:
        copy.start()
    over = link.send(ff_sum.at[1 - pair], hidden_blocks.at[4], over_y)
    to_x = [
        link.send(kept, hidden_blocks.at[2], over_x),
        link.send(down, down_blocks.at[2], over_x),
    ]
    last = [
        link.send(kept, hidden_blocks.at[1], core),
        link.send(down, down_blocks.at[1], core),
    ]
    yield
    over.wait_recv()
    far = link.send(hidden_blocks.at[4], hidden_blocks.at[6], over_x)
    last.append(link.send(hidden_blocks.at[4], hidden_blocks.at[5], core))
    for copy, blocks in zip(to_x, (hidden_blocks, down_blocks)):
        copy.wait_recv()
        last.append(link.send(blocks.at[2], blocks.at[3], core))
    yield
    far.wait_recv()
    last.append(link.send(hidden_blocks.at[6], hidden_blocks.at[7], core))
    yield
    for copy in last:
        copy.wait_recv()
    for copy in local:
        copy.wait()
    yield


def closing_kernel(
    shape,
    mid_terms,
    hidden,
    upstream,
    tokens_all,
    normed,
    vectors,
    weight,
    proj_mine,
    queries,
    keys,
    values,
    merged,
    logsum,
    cosines,
    sines,
    seg_col,
    seg_row,
    ff_sum,
    tokens_grad,
    gain_terms,
    attn_sum,
    hidden_blocks,
    down_blocks,
    arrived,
    held,
    from_x,
    from_y,
    corner,
    upper,
    grad_heads,
    grad_queries,
    grad_keys,
    grad_values,
    kv,
    projected,
    proj_part,
    proj_in,
    proj_half,
    bias_row,
    qkv_part,
    qkv_in,
    late,
    late_x,
    send_sems,
    recv_sems,
    local_sems,
):
    owned, per_dev, group = shape
    (me, sibling, across), (core, over_x, over_y) = neighbours()
    far = across + 1 - 2 * (across % 2)
    others = (sibling, across, far)
    pair = lax.axis_index("fsdp") % 2
    rows, width = hidden.shape
    seq_count = tokens_all.shape[0]
    quarter = width // seq_count
    low, high = (pl.ds(0, rows // 2), pl.ds(rows // 2, rows // 2))
    gains = (vectors[0:1, :width], vectors[1:2, :width])
    greet((core, over_x, {"seq": far}, over_y))
    link = Sender(send_sems, recv_sems)

    halved = {k: link.send(mid_terms.at[k + 1], arrived.at[k // 2], core) for k in (6, 2, 4, 0)}

    def chip_sum(k):
        halved[k].wait_recv()
        return mid_terms[k].astype(F32) + arrived[k // 2].astype(F32)

    held[2] = chip_sum(6).astype(LOW)
    turn_y = link.send(held.at[2, low], corner.at[0], over_x)
    turn_x = link.send(held.at[2, high], corner.at[1], over_y)
    held[0] = chip_sum(2).astype(LOW)
    direct_x = link.send(held.at[0, low], from_x.at[low], over_x)
    held[1] = chip_sum(4).astype(LOW)
    direct_y = link.send(held.at[1, high], from_y.at[high], over_y)
    tokens_grad[...] = chip_sum(0)
    turn_x.wait_recv()
    held[0, high] = (held[0, high].astype(F32) + corner[1].astype(F32)).astype(LOW)
    second_x = link.send(held.at[0, high], from_x.at[high], over_x)
    turn_y.wait_recv()
    held[1, low] = (held[1, low].astype(F32) + corner[0].astype(F32)).astype(LOW)
    second_y = link.send(held.at[1, low], from_y.at[low], over_y)
    for copy in (direct_x, direct_y, second_x, second_y):
        copy.wait_recv()

    grad_mid = tokens_grad[...] + from_x[...].astype(F32) + from_y[...].astype(F32)
    through, term = norm_back(hidden[...], inverse_rms(hidden[...]), gains[1], grad_mid)
    gain_terms[1:2, :] = term[None]
    total = upstream[...].astype(F32) + through
    tokens_grad[...] = total
    upper[me] = total.astype(LOW)
    last = [link.send(upper.at[me], upper.at[me], core)]
    to_x = [link.send(upper.at[me, half], upper.at[me, half], over_x) for half in (low, high)]
    for copy, half in zip(to_x, (low, high)):
        copy.wait_recv()
        last.append(link.send(upper.at[across, half], upper.at[across, half], core))
    for copy in last:
        copy.wait_recv()

    head_rows = per_dev * HD
    for block in range(seq_count):
        grad_heads[block * rows : (block + 1) * rows, :] = sum(
            times_transpose(
                upper[block, :, k * quarter : (k + 1) * quarter],
                proj_mine[k].reshape(head_rows, quarter),
            )
            for k in range(seq_count)
        ).astype(LOW)
    for k in range(seq_count):
        term = sum(
            column_product(
                merged[block * rows : (block + 1) * rows, :],
                upper[block, :, k * quarter : (k + 1) * quarter],
            )
            for block in range(seq_count)
        ).astype(LOW)
        for member in range(group):
            for y in range(2):
                first = (2 * member + y) * owned
                proj_part[y, k, member] = term[first : first + owned, :]
    proj_over = link.send(proj_part.at[1 - pair], proj_in, over_y)
    spread = spread_blocks(
        link, (core, over_x, over_y), pair, ff_sum, hidden_blocks, down_blocks, local_sems
    )
    next(spread)

    grad_keys[...] = jnp.zeros_like(grad_keys)
    grad_values[...] = jnp.zeros_like(grad_values)
    scale = HD ** (-0.5)
    for block in range(seq_count):
        here, last_key = pl.ds(block * rows, rows), (block + 1) * rows
        row_index = block * rows + lax.broadcasted_iota(jnp.int32, (rows, last_key), 0)
        key_index = lax.broadcasted_iota(jnp.int32, (rows, last_key), 1)
        allowed = (key_index <= row_index) & (seg_col[here, :] == seg_row[:, :last_key])
        for head in range(per_dev):
            query = queries[head, here, :]
            upper_head = grad_heads[here, head * HD : (head + 1) * HD]
            scores = times_transpose(query, keys[:last_key, :]) * scale
            probs = jnp.where(allowed, jnp.exp(scores - logsum[head, here, :]), 0.0)
            grad_probs = times_transpose(upper_head, values[:last_key, :])
            inner = jnp.sum(probs * grad_probs, axis=-1, keepdims=True)
            grad_scores = (probs * (grad_probs - inner)).astype(LOW)
            grad_queries[head, here, :] = (dot(grad_scores, keys[:last_key, :]) * scale).astype(LOW)
            grad_keys[:last_key, :] += column_product(grad_scores, query)
            grad_values[:last_key, :] += column_product(probs.astype(LOW), upper_head)
    next(spread)
    holds_values = me % 2 == 1
    key_copy = (grad_keys[...] * scale).astype(LOW)
    value_copy = grad_values[...].astype(LOW)
    kv[0] = jnp.where(holds_values, key_copy, value_copy)
    swapped = link.send(kv.at[0], kv.at[1], core)
    grad_keys[...] = jnp.where(holds_values, value_copy, key_copy).astype(F32)
    proj_over.wait_recv()
    proj_half[...] = (proj_part[pair].astype(F32) + proj_in[...].astype(F32)).astype(LOW)
    cols = weight.shape[1]

    def proj_place(device):
        return (pl.ds(device * group, group), pl.ds(0, owned), pl.ds(cols, quarter))

    last = [
        link.send(proj_half.at[k], attn_sum.at[proj_place(me)], {"seq": k}) for k in others
    ]
    attn_sum[proj_place(me)] = proj_half[me]
    swapped.wait_recv()
    grad_kv = grad_keys[...] + kv[1].astype(F32)

    bias_row[...] = jnp.zeros_like(bias_row)
    bias_parts = 0.0
    gain_terms[0:1, :] = jnp.zeros((1, width), F32)
    for block in range(seq_count):
        here = pl.ds(block * rows, rows)
        cosine, sine = cosines[here, :], sines[here, :]

        def rotate_back(head):
            return head * cosine - pltpu.roll(head, HD // 2, 1) * sine

        for head in range(per_dev):
            projected[here, head * HD : (head + 1) * HD] = rotate_back(
                grad_queries[head, here, :].astype(F32)
            ).astype(LOW)
        plain = grad_kv[block * rows : (block + 1) * rows, :]
        projected[here, head_rows:] = jnp.where(holds_values, plain, rotate_back(plain)).astype(LOW)
        grad_block = projected[here, :]
        bias_parts += jnp.sum(grad_block.astype(F32), axis=0, keepdims=True)
        grad_in = times_transpose(grad_block, weight[...])
        value = tokens_all[block].astype(F32)
        gain_terms[0:1, :] += jnp.sum(
            grad_in * value * inverse_rms(value), axis=0, keepdims=True
        )
        arrived[block] = grad_in.astype(LOW)
    first = link.send(arrived.at[far], late.at[0], core)
    second = link.send(arrived.at[sibling], late.at[1], core)
    first.wait_recv()
    link.release(direct_x, second_x)
    held[0] = (arrived[across].astype(F32) + late[0].astype(F32)).astype(LOW)
    third = link.send(held.at[0], late_x, over_x)
    kv_first = (H + KV * (me % 2) + me // 2) * HD
    bias_row[0:1, pl.ds(pl.multiple_of(me * head_rows, HD), head_rows)] = bias_parts[:, :head_rows]
    bias_row[0:1, pl.ds(pl.multiple_of(kv_first, HD), HD)] = bias_parts[:, head_rows:]
    line = qkv_in.shape[0]
    owned_bias = bias_row.shape[1] // (2 * line)
    qkv_part[:, :, owned:, :] = jnp.zeros_like(qkv_part[:, :, owned:, :])
    for z in range(line):
        for y in range(2):
            owner, at = 2 * z + y, 0
            for source, row, length in (
                (gain_terms, 0, owned),
                (gain_terms, 1, owned),
                (bias_row, 0, owned_bias),
            ):
                done = 0
                while done < length:
                    span = min(length - done, cols - at % cols)
                    first_col = owner * length + done
                    qkv_part[
                        y, z, owned + at // cols : owned + at // cols + 1, at % cols : at % cols + span
                    ] = source[row : row + 1, first_col : first_col + span].astype(LOW)
                    done, at = done + span, at + span
    for z in range(line):
        term = sum(
            column_product(
                normed[block, :, 2 * owned * z : 2 * owned * (z + 1)],
                projected[block * rows : (block + 1) * rows, :],
            )
            for block in range(seq_count)
        ).astype(LOW)
        for y in range(2):
            qkv_part[y, z, :owned, :] = term[y * owned : (y + 1) * owned, :]
    qkv_over = link.send(qkv_part.at[1 - pair], qkv_in, over_y)
    next(spread)
    second.wait_recv()
    third.wait_recv()
    grad_in = arrived[me].astype(F32) + late[1].astype(F32) + late_x[...].astype(F32)
    value = tokens_all[me].astype(F32)
    through, _ = norm_back(value, inverse_rms(value), gains[0], grad_in)
    tokens_grad[...] += through
    qkv_over.wait_recv()
    attn_sum[:, :, :cols] = (qkv_part[pair].astype(F32) + qkv_in[...].astype(F32)).astype(LOW)
    attn_sum[:, owned:, cols:] = jnp.zeros_like(attn_sum[:, owned:, cols:])
    for copy in last:
        copy.wait_recv()
    next(spread)
    link.finish()


def closing(args, sizes):
    owned, vector_rows, bias_cols, per_dev, group, line = sizes
    hidden, weight, proj_mine = args[1], args[6], args[7]
    rows, width = hidden.shape
    block = (rows, width)
    cols = weight.shape[1]
    quarter = proj_mine.shape[-1]
    heads = (4 * rows, HD)
    rows_in = (4, group, owned, quarter)
    outs = [
        jax.ShapeDtypeStruct(block, F32),
        jax.ShapeDtypeStruct((2, width), F32),
        jax.ShapeDtypeStruct((line, owned + vector_rows, cols + quarter), LOW),
        jax.ShapeDtypeStruct((8, *args[-1].shape[1:]), LOW),
        jax.ShapeDtypeStruct((4, *args[-1].shape[1:]), LOW),
    ]
    low_scratch = [
        (4, *block),
        (3, *block),
        block,
        block,
        (2, rows // 2, width),
        (4, *block),
        (4 * rows, per_dev * HD),
        (per_dev, *heads),
    ]
    return pl.pallas_call(
        functools.partial(closing_kernel, (owned, per_dev, group)),
        out_shape=outs,
        in_specs=[pl.BlockSpec(memory_space=pltpu.VMEM)] * len(args),
        out_specs=[pl.BlockSpec(memory_space=pltpu.VMEM)] * (len(outs) - 2)
        + [pl.BlockSpec(memory_space=pl.ANY)] * 2,
        scratch_shapes=[pltpu.VMEM(shape, LOW) for shape in low_scratch]
        + [pltpu.VMEM(heads, F32)] * 2
        + [
            pltpu.VMEM(shape, LOW)
            for shape in (
                (2, *heads),
                (4 * rows, cols),
                (2, *rows_in),
                rows_in,
                rows_in,
            )
        ]
        + [pltpu.VMEM((1, bias_cols), F32)]
        + [
            pltpu.VMEM(shape, LOW)
            for shape in (
                (2, line, owned + vector_rows, cols),
                (line, owned + vector_rows, cols),
                (2, *block),
                block,
            )
        ]
        + [pltpu.SemaphoreType.DMA((48,))] * 2
        + [pltpu.SemaphoreType.DMA((2,))],
        compiler_params=pltpu.CompilerParams(
            collective_id=2, has_side_effects=True, vmem_limit_bytes=58 << 20
        ),
        cost_estimate=pl.CostEstimate(
            flops=100_000_000_000, bytes_accessed=40_000_000, transcendentals=4_000_000
        ),
    )(*args)


def columns_kernel(place, *refs):
    *pieces, out = refs
    row = 0
    for piece in pieces:
        count, rows, quarter = piece.shape
        for k in range(count):
            here = place[0] + k - 2 * ((place[0] % 2) * (k % 2)) - 4 * (
                (place[0] // 2 % 2) * (k // 2 % 2)
            )
            out[pl.ds(row, rows), pl.ds(k * quarter, quarter)] = piece[here].astype(F32)
        row += rows


def columns_call(place, pieces):
    rows = sum(piece.shape[1] for piece in pieces)
    width = pieces[0].shape[0] * pieces[0].shape[2]
    return pl.pallas_call(
        columns_kernel,
        out_shape=jax.ShapeDtypeStruct((rows, width), F32),
        in_specs=[pl.BlockSpec(memory_space=pltpu.SMEM)]
        + [pl.BlockSpec(memory_space=pltpu.VMEM)] * len(pieces),
        out_specs=pl.BlockSpec(memory_space=pltpu.VMEM),
        compiler_params=pltpu.CompilerParams(vmem_limit_bytes=40 << 20),
    )(place, *pieces)


def down_kernel(fold, place, *refs):
    *pieces, out = refs
    row = 0
    for piece in pieces:
        count, owned, width = piece.shape
        span = width // fold
        for k in range(count):
            here = place[0] + k - 2 * ((place[0] % 2) * (k % 2)) - 4 * (
                (place[0] // 2 % 2) * (k // 2 % 2)
            )
            whole = piece[here].astype(F32)
            for j in range(fold):
                whole_part = whole[:, j * span : (j + 1) * span]
                out[pl.ds(row, span), pl.ds((k * fold + j) * owned, owned)] = whole_part.T
        row += span


def down_call(place, pieces, fold):
    rows = sum(piece.shape[2] // fold for piece in pieces)
    width = pieces[0].shape[0] * pieces[0].shape[1] * fold
    return pl.pallas_call(
        functools.partial(down_kernel, fold),
        out_shape=jax.ShapeDtypeStruct((rows, width), F32),
        in_specs=[pl.BlockSpec(memory_space=pltpu.SMEM)]
        + [pl.BlockSpec(memory_space=pltpu.VMEM)] * len(pieces),
        out_specs=pl.BlockSpec(memory_space=pltpu.VMEM),
        compiler_params=pltpu.CompilerParams(vmem_limit_bytes=40 << 20),
    )(place, *pieces)


def hidden_kernel(cuts, group, place, *refs):
    *pieces, out = refs
    units = cuts[-1][1]
    count = pieces[0].shape[0] // 2
    for k in range(count):
        here = place[0] + k - 2 * ((place[0] % 2) * (k % 2)) - 4 * (
            (place[0] // 2 % 2) * (k // 2 % 2)
        )
        for pair in range(2):
            entry = (pair + place[1] - 2 * pair * place[1]) * count + here
            for part in range(2):
                for member in range(group):
                    first = (((part * count + k) * group + member) * 2 + pair) * units
                    for piece, (low, high) in zip(pieces, cuts):
                        span = high - low
                        at = (part * group + member) * span
                        out[:, first + low : first + high] = piece[entry][
                            :, at : at + span
                        ].astype(F32)


def hidden_call(place, pieces, cuts, group):
    rows = pieces[0].shape[1]
    units = cuts[-1][1]
    width = 2 * 8 * group * units
    step = 16
    return pl.pallas_call(
        functools.partial(hidden_kernel, cuts, group),
        grid=(rows // step,),
        out_shape=jax.ShapeDtypeStruct((rows, width), F32),
        in_specs=[pl.BlockSpec(memory_space=pltpu.SMEM)]
        + [pl.BlockSpec((8, step, piece.shape[2]), lambda i: (0, i, 0)) for piece in pieces],
        out_specs=pl.BlockSpec((step, width), lambda i: (i, 0)),
        compiler_params=pltpu.CompilerParams(vmem_limit_bytes=40 << 20),
    )(place, *pieces)


def local(
    tokens,
    segment_ids,
    attn_gain,
    qkv_weight,
    qkv_bias,
    proj_weight,
    mlp_gain,
    gate_up_weight,
    down_weight,
    cotangent,
):
    seq_count = lax.axis_size("seq")
    fsdp_count = lax.axis_size("fsdp")
    line = fsdp_count // 2
    place = lax.axis_index("seq")
    odd = lax.axis_index("fsdp") % 2 == 1
    tok_rows, width = tokens.shape[1:]
    seq_len = tok_rows * seq_count
    owned = qkv_weight.shape[0]
    owned_hidden = down_weight.shape[0]
    hidden = owned_hidden * fsdp_count
    quarter = width // seq_count
    per_dev = H // seq_count
    head_cols = per_dev * HD
    score_scale = HD ** (-0.5)
    group = line // seq_count
    cut_at = owned_hidden // 2 // 128 * 128
    cuts = [(0, cut_at), (cut_at, owned_hidden)]

    holds_values = place % 2 == 1
    kv_first = (H + KV * (place % 2) + place // 2) * HD
    qkv_own = jnp.concatenate(
        [
            lax.dynamic_slice_in_dim(qkv_weight, place * head_cols, head_cols, 1),
            lax.dynamic_slice_in_dim(qkv_weight, kv_first, HD, 1),
        ],
        axis=1,
    )
    cols = head_cols + HD
    vector = jnp.concatenate([attn_gain, mlp_gain, qkv_bias])
    vector_size = vector.shape[0]
    vector_rows = -(-vector_size // (16 * cols)) * 16
    vector = jnp.pad(vector, (0, vector_rows * cols - vector_size)).reshape(vector_rows, cols)
    proj_cols = lax.dynamic_slice_in_dim(proj_weight, place * quarter, quarter, 1)
    down_cols = lax.dynamic_slice_in_dim(down_weight, place * quarter, quarter, 1)
    fold = quarter // owned

    def folded(value):
        return jnp.concatenate(
            [value[..., j * owned : (j + 1) * owned, :] for j in range(fold)], axis=-1
        )

    def ff_columns(low, high, pair):
        return jnp.concatenate(
            [
                lax.dynamic_slice_in_dim(
                    gate_up_weight,
                    first + ((place * group + member) * 2 + pair) * owned_hidden + low,
                    high - low,
                    1,
                )
                for first in (0, hidden)
                for member in range(group)
            ],
            axis=1,
        )

    ff_sent = []
    for low, high in cuts:
        by_owner = [ff_columns(low, high, pair) for pair in range(2)]
        ff_sent.append((by_owner, folded(jnp.transpose(down_cols[low:high]))))
    segment_row = segment_ids[0]
    doc_starts = jnp.sum((segment_row[None, :] < segment_row[:, None]).astype(jnp.int32), axis=1)
    places = jnp.arange(seq_len, dtype=jnp.int32) - doc_starts
    inverse = THETA ** (-2.0 * jnp.arange(HD // 2, dtype=F32) / HD)
    angles = places.astype(F32)[:, None] * inverse[None, :]
    angles = jnp.concatenate([angles, angles], axis=-1)
    cosines = jnp.cos(angles)
    signs = jnp.where(jnp.arange(HD) < HD // 2, -1.0, 1.0).astype(F32)
    sines = jnp.sin(angles) * signs

    (
        tokens_all,
        qkv_mine,
        vectors,
        proj_mine,
        first_all,
        first_rows,
        normed_in,
        queries,
        head_keys,
        head_values,
        merged,
        logsum,
        attended,
        cots,
    ) = opening(
        tokens[0],
        cotangent[0],
        jnp.concatenate([qkv_own, vector], axis=0),
        lax.dynamic_slice_in_dim(proj_weight, place * quarter, quarter, 1),
        (jnp.stack(ff_sent[0][0]), ff_sent[0][1]),
        (cosines, sines),
        (segment_row[:, None], segment_row[None]),
        (owned, vector_size, per_dev, group, line),
    )
    (by_owner, second_down) = ff_sent[1]
    kept, given = pick(odd, *by_owner)
    second_sent = jnp.stack([*by_pair(kept, swap(given, "fsdp", 1)), second_down])
    second_all = line_gather(second_sent + nought(vectors[0, 0]))

    hidden_in, mids = middle(attended, tokens[0], vectors)

    def plane_reduce(total):
        parts = [total[k] for k in range(2 * seq_count)]
        away = seq_reduce(parts[seq_count:]).astype(LOW)
        return seq_reduce(parts[:seq_count]) + swap(away, "fsdp", 1).astype(F32)

    spans = [high - low for low, high in cuts]
    first_term, out_first, mid_first = cut_call(
        False, (mids, cots, first_all, first_rows), (group, line, owned, spans[0])
    )
    second_term, out, grad_mid = cut_call(
        True, (mids, cots, second_all, out_first, mid_first), (group, line, owned, spans[1])
    )

    sums = [line_reduce(term) for term in (first_term, second_term)]

    tokens_grad, gain_terms, attn_term, *first_blocks = closing(
        (
            grad_mid,
            hidden_in,
            cotangent[0],
            tokens_all,
            normed_in,
            vectors,
            qkv_mine,
            proj_mine,
            queries,
            head_keys,
            head_values,
            merged,
            logsum,
            cosines,
            sines,
            segment_row[:, None],
            segment_row[None],
            sums[0],
        ),
        (owned, vector_rows, qkv_weight.shape[1], per_dev, group, line),
    )
    block_out = (hidden_in + plane_reduce(out)).astype(LOW)

    places_here = jnp.stack([place, lax.axis_index("fsdp") % 2]).astype(jnp.int32)
    attn_sum = line_reduce(attn_term + nought(sums[1][0, 0, 0]))
    second_sum = sums[1] + nought(attn_sum[0, 0])
    kept, given = pick(odd, second_sum[0], second_sum[1])
    here = seq_blocks(jnp.stack([kept, second_sum[2]]))
    hidden_pieces = [
        first_blocks[0],
        jnp.stack([pair[0] for pair in here] + seq_blocks(swap(given, "fsdp", 1))),
    ]
    down_pieces = [first_blocks[1], jnp.stack([pair[1] for pair in here])]
    down_grad = down_call(places_here, down_pieces, fold)
    gate_up_grad = hidden_call(places_here, hidden_pieces, cuts, group)
    attn_sums = seq_blocks(attn_sum)
    proj_grad = columns_call(
        places_here, [jnp.stack([part[:owned, cols:] for part in attn_sums])]
    )
    qkv_sums = in_order([part[:, :cols] for part in attn_sums])
    qkv_grad = jnp.concatenate(
        [part[:owned, :head_cols] for part in qkv_sums]
        + [part[:owned, head_cols:] for part in qkv_sums[0::2]]
        + [part[:owned, head_cols:] for part in qkv_sums[1::2]],
        axis=-1,
    ).astype(F32)
    vector_sum = sum(part[owned:].astype(F32) for part in qkv_sums).reshape(-1)
    return (
        block_out[None],
        tokens_grad[None],
        vector_sum[:owned],
        qkv_grad,
        vector_sum[2 * owned : vector_size],
        proj_grad,
        vector_sum[owned : 2 * owned],
        gate_up_grad,
        down_grad,
    )


def solution(mesh):
    in_specs = (
        P("fsdp", "seq", None),
        P("fsdp", None),
        P("fsdp"),
        P("fsdp", None),
        P("fsdp"),
        P("fsdp", None),
        P("fsdp"),
        P("fsdp", None),
        P("fsdp", None),
        P("fsdp", "seq", None),
    )
    out_specs = (
        P("fsdp", "seq", None),
        P("fsdp", "seq", None),
        P("fsdp"),
        P("fsdp", None),
        P("fsdp"),
        P("fsdp", None),
        P("fsdp"),
        P("fsdp", None),
        P("fsdp", None),
    )
    return jax.shard_map(local, mesh=mesh, in_specs=in_specs, out_specs=out_specs, check_vma=False)
```

```python
import functools

import jax
import jax.numpy as jnp
from jax import lax
from jax.experimental import pallas as pl
from jax.experimental.pallas import tpu as pltpu
from jax.sharding import PartitionSpec as P

H = 12
KV = 2
HD = 128
EPSILON = 1e-06
THETA = 1000000.0
FLOOR = -1e30
LOW = jnp.bfloat16
F32 = jnp.float32


def inverse_rms(value):
    return lax.rsqrt(jnp.mean(value * value, axis=-1, keepdims=True) + EPSILON)


def turned(value):
    halfway = value.shape[-1] // 2
    return jnp.concatenate([-value[..., halfway:], value[..., :halfway]], axis=-1)


def turned_back(value):
    halfway = value.shape[-1] // 2
    return jnp.concatenate([value[..., halfway:], -value[..., :halfway]], axis=-1)


def norm_back(value, factor, gain, upstream):
    weighted = upstream * gain
    gain_term = jnp.sum(upstream * value * factor, axis=0)
    through = factor * weighted - value * factor**3 * jnp.mean(
        weighted * value, axis=-1, keepdims=True
    )
    return (through, gain_term)


def dot(left, right):
    return jnp.dot(left, right, preferred_element_type=F32)


def column_product(left, right):
    return lax.dot_general(left, right, (((0,), (0,)), ((), ())), preferred_element_type=F32)


def times_transpose(left, right):
    return lax.dot_general(left, right, (((1,), (1,)), ((), ())), preferred_element_type=F32)


def swap(value, axis, distance):
    return lax.ppermute(value, axis, [(i, i ^ distance) for i in range(lax.axis_size(axis))])


def lines():
    size = lax.axis_size("fsdp")
    return [list(range(first, size, 2)) for first in range(2)]


def line_gather(value):
    return lax.all_gather(value, "fsdp", axis=0, axis_index_groups=lines(), tiled=False)


def line_reduce(value):
    return lax.psum_scatter(
        value, "fsdp", scatter_dimension=0, axis_index_groups=lines(), tiled=False
    )


def by_pair(own, other):
    second = lax.axis_index("fsdp") % 2 == 1
    return (jnp.where(second, other, own), jnp.where(second, own, other))


def pick(flag, first, second):
    return (jnp.where(flag, second, first), jnp.where(flag, first, second))


def nought(value):
    return jnp.minimum(jnp.abs(value), 0.0).astype(LOW)


def seq_blocks(value):
    across = swap(value, "seq", 2)
    return [value, swap(value, "seq", 1), across, swap(across, "seq", 1)]


def seq_reduce(parts):
    arrived = swap(jnp.stack([parts[1], parts[3]]), "seq", 1)
    across = (parts[2].astype(F32) + arrived[1].astype(F32)).astype(LOW)
    here = parts[0].astype(F32) + arrived[0].astype(F32)
    return here + swap(across, "seq", 2).astype(F32)


def in_order(blocks):
    me = lax.axis_index("seq")
    bits = 1
    while bits < len(blocks):
        flip = (me & bits) != 0
        blocks = [jnp.where(flip, blocks[k ^ bits], blocks[k]) for k in range(len(blocks))]
        bits *= 2
    return blocks


def relative(value):
    size = lax.axis_size("seq")
    me = lax.axis_index("seq")
    cut = value.reshape(size, value.shape[0] // size, *value.shape[1:])
    return [lax.dynamic_index_in_dim(cut, me ^ k, 0, keepdims=False) for k in range(size)]


def seq_exchange(pieces):
    taken = [part[0] for part in relative(pieces)]
    return in_order([taken[0]] + [swap(taken[k], "seq", k) for k in range(1, len(taken))])


MESH = pl.DeviceIdType.MESH


def neighbours():
    me, owner = lax.axis_index("seq"), lax.axis_index("fsdp")
    sibling = me + 1 - 2 * (me % 2)
    across = me + 2 - 4 * (me // 2 % 2)
    partner = owner + 1 - 2 * (owner % 2)
    return (me, sibling, across), ({"seq": sibling}, {"seq": across}, {"fsdp": partner})


def greet(devices):
    barrier = pltpu.get_barrier_semaphore()
    for device in devices:
        pl.semaphore_signal(barrier, inc=1, device_id=device, device_id_type=MESH)
    pl.semaphore_wait(barrier, len(devices))


class Sender:
    def __init__(self, send_sems, recv_sems):
        self.sems = (send_sems, recv_sems)
        self.count, self.open = 0, []

    def send(self, source, target, device):
        number = self.count
        copy = pltpu.make_async_remote_copy(
            src_ref=source,
            dst_ref=target,
            send_sem=self.sems[0].at[number],
            recv_sem=self.sems[1].at[number],
            device_id=device,
            device_id_type=MESH,
        )
        copy.start()
        self.count += 1
        self.open.append(copy)
        return copy

    def release(self, *copies):
        for copy in copies:
            copy.wait_send()
            self.open = [other for other in self.open if other is not copy]

    def finish(self):
        self.release(*self.open)


def plane_gather(link, blocks, ids):
    core, over_x, over_y = ids
    rows = blocks.shape[1]
    halves = (pl.ds(0, rows // 2), pl.ds(rows // 2, rows // 2))
    to_x = [link.send(blocks.at[0, half], blocks.at[2, half], over_x) for half in halves]
    last = [link.send(blocks.at[0], blocks.at[1], core)]
    yield
    to_y = [link.send(blocks.at[0, half], blocks.at[4, half], over_y) for half in halves[::-1]]
    yield
    to_x[0].wait_recv()
    diagonal = [link.send(blocks.at[2, halves[0]], blocks.at[6, halves[0]], over_y)]
    last.append(link.send(blocks.at[2, halves[0]], blocks.at[3, halves[0]], core))
    to_y[0].wait_recv()
    diagonal.append(link.send(blocks.at[4, halves[1]], blocks.at[6, halves[1]], over_x))
    last.append(link.send(blocks.at[4, halves[1]], blocks.at[5, halves[1]], core))
    to_x[1].wait_recv()
    last.append(link.send(blocks.at[2, halves[1]], blocks.at[3, halves[1]], core))
    to_y[1].wait_recv()
    last.append(link.send(blocks.at[4, halves[0]], blocks.at[5, halves[0]], core))
    for copy, half in zip(diagonal, halves):
        copy.wait_recv()
        last.append(link.send(blocks.at[6, half], blocks.at[7, half], core))
    for copy in last:
        copy.wait_recv()
    yield


def opening_kernel(
    shape,
    tokens,
    cotangent,
    qkv,
    proj,
    ff_own,
    ff_down,
    second,
    cosines,
    sines,
    seg_col,
    seg_row,
    tokens_all,
    weight,
    vectors,
    proj_mine,
    ff_all,
    ff_rows,
    second_out,
    normed,
    queries,
    keys,
    values,
    merged,
    logsum,
    part,
    cots,
    qkv_all,
    proj_all,
    ff_line,
    kv,
    send_sems,
    recv_sems,
    hand_send,
    hand_recv,
    local_sem,
):
    owned, vector_size, per_dev, group = shape
    (me, sibling, across), ids = neighbours()
    core, over_x, over_y = ids
    far = across + 1 - 2 * (across % 2)
    line = qkv_all.shape[0]
    size = 2 * line
    owner = lax.axis_index("fsdp")
    at, pair = owner // 2, owner % 2
    below, above = ({"fsdp": (owner + size - 2) % size}, {"fsdp": (owner + 2) % size})
    rows, width = tokens.shape
    seq_count = tokens_all.shape[0]
    seq_len = seq_count * rows
    halves = (pl.ds(0, rows // 2), pl.ds(rows // 2, rows // 2))
    others = (sibling, across, far)
    greet((*ids, {"seq": far}, below, above))
    link = Sender(send_sems, recv_sems)

    own_copy = pltpu.make_async_copy(ff_own.at[pair], ff_all.at[at, pair], local_sem.at[0])
    own_copy.start()
    second_copy = pltpu.make_async_copy(second, second_out, local_sem.at[1])
    second_copy.start()
    ff_line[at] = ff_down[...]
    tokens_all[me] = tokens[...]
    qkv_all[at, pair] = qkv[...]
    proj_all[at, pair] = proj[...]

    turned, handed = [], []

    def hand_on(k):
        z = (at + k) % line
        target, member = z // group, z % group
        copy = pltpu.make_async_remote_copy(
            src_ref=ff_line.at[z],
            dst_ref=ff_rows.at[me, member],
            send_sem=hand_send.at[k],
            recv_sem=hand_recv.at[me * group + member],
            device_id={"seq": target},
            device_id_type=MESH,
        )

        @pl.when(target != me)
        def _():
            copy.start()

        @pl.when(target == me)
        def _():
            ff_rows[me, member] = ff_line[z]

        handed.append((copy, target))

    def ring_steps():
        before = [None] * 3
        for k in range(line):
            z = (at + k) % line
            here = (ff_line.at[z], ff_all.at[z, pair], ff_all.at[z, 1 - pair])
            for place, target in enumerate(here):
                source = ff_own.at[pair] if k == 0 and place == 1 else target
                if k > 0:
                    before[place].wait_recv()
                elif place == 2:
                    turned[0].wait_recv()
                if k < line - 1:
                    before[place] = link.send(source, target, below)
                if place == 0:
                    hand_on(k)
                yield

    ring = ring_steps()

    def pump(count):
        for _ in range(count):
            next(ring, None)

    def along_line(array, k):
        here = array.at[(at + k) % line, pair]
        return link.send(here, here, below)

    def to_partner(array, k):
        here = array.at[(at + k) % line, pair]
        return link.send(here, here, over_y)

    onward = along_line(qkv_all, 0)
    last = [to_partner(qkv_all, 0)]
    to_x = [link.send(tokens_all.at[me, half], tokens_all.at[me, half], over_x) for half in halves]
    last.append(link.send(tokens_all.at[me], tokens_all.at[me], core))
    proj_onward = along_line(proj_all, 0)
    for k in range(1, line):
        onward.wait_recv()
        if k < line - 1:
            onward = along_line(qkv_all, k)
        last.append(to_partner(qkv_all, k))
        proj_onward.wait_recv()
        if k < line - 1:
            proj_onward = along_line(proj_all, k)
        if k == line - 2:
            pump(2)
    turned.append(link.send(ff_own.at[1 - pair], ff_all.at[at, pair], over_y))
    for copy, half in zip(to_x, halves):
        copy.wait_recv()
        last.append(link.send(tokens_all.at[across, half], tokens_all.at[across, half], core))
    for copy in last:
        copy.wait_recv()
    proj_over = [to_partner(proj_all, k) for k in range(line)]
    cots[0] = cotangent[...]
    gather_cots = plane_gather(link, cots, ids)
    next(gather_cots)

    for z in range(line):
        for y in range(2):
            owner_row = 2 * z + y
            weight[pl.ds(owner_row * owned, owned), :] = qkv_all[z, y, :owned, :]
            done = 0
            cols = qkv_all.shape[3]
            for start, count, target in (
                (0, owned, 0),
                (owned, owned, 1),
                (2 * owned, vector_size - 2 * owned, 2),
            ):
                while count > 0:
                    row, col = start // cols, start % cols
                    span = min(count, cols - col)
                    length = (owned, owned, vector_size - 2 * owned)[target]
                    to = owner_row * length + (length - count)
                    vectors[target : target + 1, to : to + span] = qkv_all[
                        z, y, owned + row : owned + row + 1, col : col + span
                    ].astype(F32)
                    start, count = start + span, count - span

    head_cols = per_dev * HD
    holds_values = me % 2 == 1
    kv_first = (H + KV * (me % 2) + me // 2) * HD
    bias = jnp.concatenate(
        [
            vectors[2:3, pl.ds(pl.multiple_of(me * head_cols, HD), head_cols)],
            vectors[2:3, pl.ds(pl.multiple_of(kv_first, HD), HD)],
        ],
        axis=1,
    )
    for block in range(seq_count):
        here = pl.ds(block * rows, rows)
        value = tokens_all[block].astype(F32)
        normal = (value * inverse_rms(value) * vectors[0:1, :width]).astype(LOW)
        normed[block] = normal
        projected = dot(normal, weight[...]) + bias
        cosine, sine = cosines[here, :], sines[here, :]

        def rotate(head):
            return head * cosine + pltpu.roll(head, HD // 2, 1) * sine

        for head in range(per_dev):
            queries[head, here, :] = rotate(projected[:, head * HD : (head + 1) * HD]).astype(LOW)
        plain = projected[:, head_cols:]
        kv[0, here, :] = jnp.where(holds_values, plain, rotate(plain)).astype(LOW)
    swapped = link.send(kv.at[0], kv.at[1], core)
    pump(3)
    swapped.wait_recv()
    keys[...] = jnp.where(holds_values, kv[1], kv[0])
    values[...] = jnp.where(holds_values, kv[0], kv[1])

    for copy in proj_over:
        copy.wait_recv()
    exchange = [
        link.send(proj_all.at[pl.ds(target * group, group)], proj_mine.at[me], {"seq": target})
        for target in others
    ]
    next(gather_cots)
    proj_mine[me] = proj_all[pl.ds(me * group, group)]

    for block in range(seq_count):
        here, last_key = pl.ds(block * rows, rows), (block + 1) * rows
        row_index = block * rows + lax.broadcasted_iota(jnp.int32, (rows, last_key), 0)
        key_index = lax.broadcasted_iota(jnp.int32, (rows, last_key), 1)
        allowed = (key_index <= row_index) & (seg_col[here, :] == seg_row[:, :last_key])
        for head in range(per_dev):
            scores = times_transpose(queries[head, here, :], keys[:last_key, :]) * HD ** (-0.5)
            scores = jnp.where(allowed, scores, FLOOR)
            highest = jnp.max(scores, axis=-1, keepdims=True)
            exponent = jnp.exp(scores - highest)
            total = jnp.sum(exponent, axis=-1, keepdims=True)
            mixture = dot((exponent / total).astype(LOW), values[:last_key, :])
            merged[here, head * HD : (head + 1) * HD] = mixture.astype(LOW)
            logsum[head, here, :] = highest + jnp.log(total)
    pump(2)
    for copy in exchange:
        copy.wait_recv()
    quarter = proj.shape[1]
    for block in range(seq_count):
        for k in range(seq_count):
            columns = proj_mine[k].reshape(-1, quarter)
            part[block, :, k * quarter : (k + 1) * quarter] = dot(
                merged[block * rows : (block + 1) * rows, :], columns
            ).astype(LOW)

    pump(1)
    next(gather_cots)
    pump(3 * line)
    own_copy.wait()
    second_copy.wait()
    for source in others:
        for member in range(group):
            pltpu.make_async_remote_copy(
                src_ref=ff_line.at[0],
                dst_ref=ff_rows.at[source, member],
                send_sem=hand_send.at[0],
                recv_sem=hand_recv.at[source * group + member],
                device_id=core,
                device_id_type=MESH,
            ).wait_recv()
    for copy, target in handed:

        @pl.when(target != me)
        def _():
            copy.wait_send()

    link.finish()


def opening(tokens, cotangent, qkv, proj, ff, tables, segments, sizes):
    owned, vector_size, per_dev, group, line = sizes
    rows, width = tokens.shape
    block = (rows, width)
    seq_len = 4 * rows
    cols = qkv.shape[1]
    heads = (seq_len, HD)
    vmem, hbm = (pl.BlockSpec(memory_space=pltpu.VMEM), pl.BlockSpec(memory_space=pl.ANY))

    def like(*shape, dtype=LOW):
        return jax.ShapeDtypeStruct(shape, dtype)

    outs = [
        (like(4, *block), vmem),
        (like(width, cols), vmem),
        (like(3, max(width, 2048), dtype=F32), vmem),
        (like(4, group, 2, *proj.shape), vmem),
        (like(line, *ff[0].shape), hbm),
        (like(4, group, *ff[1].shape), vmem),
        (like(*ff[2].shape), hbm),
        (like(4, *block), vmem),
        (like(per_dev, *heads), vmem),
        (like(*heads), vmem),
        (like(*heads), vmem),
        (like(seq_len, per_dev * HD), vmem),
        (like(per_dev, seq_len, 1, dtype=F32), vmem),
        (like(4, *block), vmem),
        (like(8, *block), vmem),
    ]
    copies = 10 * line + 40
    return pl.pallas_call(
        functools.partial(opening_kernel, (owned, vector_size, per_dev, group)),
        out_shape=[shape for shape, _ in outs],
        in_specs=[vmem] * 6 + [hbm] + [vmem] * 4,
        out_specs=[place for _, place in outs],
        scratch_shapes=[
            pltpu.VMEM((line, 2, *qkv.shape), LOW),
            pltpu.VMEM((line, 2, *proj.shape), LOW),
            pltpu.VMEM((line, *ff[1].shape), LOW),
            pltpu.VMEM((2, *heads), LOW),
            pltpu.SemaphoreType.DMA((copies,)),
            pltpu.SemaphoreType.DMA((copies,)),
            pltpu.SemaphoreType.DMA((line,)),
            pltpu.SemaphoreType.DMA((4 * group,)),
            pltpu.SemaphoreType.DMA((2,)),
        ],
        cost_estimate=pl.CostEstimate(
            flops=100_000_000_000, bytes_accessed=40_000_000, transcendentals=4_000_000
        ),
        compiler_params=pltpu.CompilerParams(
            collective_id=0, has_side_effects=True, vmem_limit_bytes=56 << 20
        ),
    )(tokens, cotangent, qkv, proj, *ff, *tables, *segments)


def middle_kernel(
    part, tokens, vectors, hidden, mids, arrived, summed, across_in, send_sems, recv_sems
):
    (me, sibling, across), ids = neighbours()
    far = across + 1 - 2 * (across % 2)
    width = tokens.shape[1]
    greet(ids)
    link = Sender(send_sems, recv_sems)
    first = link.send(part.at[far], arrived.at[0], ids[0])
    second = link.send(part.at[sibling], arrived.at[1], ids[0])
    first.wait_recv()
    summed[...] = (part[across].astype(F32) + arrived[0].astype(F32)).astype(LOW)
    third = link.send(summed, across_in, ids[1])
    second.wait_recv()
    hidden[...] = tokens[...].astype(F32) + (part[me].astype(F32) + arrived[1].astype(F32))
    third.wait_recv()
    total = hidden[...] + across_in[...].astype(F32)
    hidden[...] = total
    mids[0] = (total * inverse_rms(total) * vectors[1:2, :width]).astype(LOW)
    for _ in plane_gather(link, mids, ids):
        pass
    link.finish()


def middle(part, tokens, vectors):
    block = tokens.shape
    vmem = pl.BlockSpec(memory_space=pltpu.VMEM)
    return pl.pallas_call(
        middle_kernel,
        out_shape=[jax.ShapeDtypeStruct(block, F32), jax.ShapeDtypeStruct((8, *block), LOW)],
        in_specs=[vmem] * 3,
        out_specs=[vmem] * 2,
        scratch_shapes=[
            pltpu.VMEM((2, *block), LOW),
            pltpu.VMEM(block, LOW),
            pltpu.VMEM(block, LOW),
            pltpu.SemaphoreType.DMA((16,)),
            pltpu.SemaphoreType.DMA((16,)),
        ],
        compiler_params=pltpu.CompilerParams(
            collective_id=1, has_side_effects=True, vmem_limit_bytes=32 << 20
        ),
    )(part, tokens, vectors)


def cut_kernel(shape, *refs):
    follows, group, units = shape
    if follows:
        mids_in, cots_in, whole_in, out_before, mid_before, *refs = refs
    else:
        mids_in, cots_in, weight_in, rows_in, *refs = refs
    term, out, mid, mids, cots, weight, rows, down, act, grad, stage, *refs = refs
    before, ahead, load_sems, weight_sems, stage_sems, before_sems, send_sems, recv_sems = refs
    (me, sibling, across), ids = neighbours()
    far = across + 1 - 2 * (across % 2)
    others = (sibling, across, far)
    line, _, owned, cols = weight.shape
    count, block, width = mids.shape
    quarter = width // 4
    fold = quarter // owned
    greet((ids[0], ids[1], {"seq": far}))
    link = Sender(send_sems, recv_sems)

    def load(source, target, sem):
        copy = pltpu.make_async_copy(source, target, sem)
        copy.start()
        return copy

    if follows:
        sent = [
            link.send(whole_in.at[pl.ds(k * group, group), 2], rows.at[me], {"seq": k})
            for k in others
        ]
        loads = [load(whole_in.at[pl.ds(me * group, group), 2], rows.at[me], weight_sems.at[line])]
        loads += [
            load(whole_in.at[z, pl.ds(0, 2)], weight.at[z], weight_sems.at[z]) for z in range(line)
        ]
    else:
        sent = []
        loads = [load(rows_in, rows, weight_sems.at[line]), load(weight_in, weight, weight_sems.at[0])]
    for t in range(count):
        load(mids_in.at[t], mids.at[t], load_sems.at[0, t])
        load(cots_in.at[t], cots.at[t], load_sems.at[1, t])
    for copy in loads:
        copy.wait()

    def forward(t, carry):
        pltpu.make_async_copy(mids_in.at[t], mids.at[t], load_sems.at[0, t]).wait()
        ahead[t] = dot(mids[t], weight[...].reshape(width, cols))
        return carry

    early = ahead.shape[0]
    if follows:
        lax.fori_loop(0, early, forward, 0)
    for copy in sent:
        copy.wait_recv()
    for k in range(4):
        for member in range(group):
            for j in range(fold):
                first = k * quarter + j * owned
                down[first : first + owned, member * units : (member + 1) * units] = rows[
                    k, member, :, j * units : (j + 1) * units
                ]

    def tokens(first, t, carry):
        if first == 0 and follows:
            gate_up = ahead[t]
        else:
            pltpu.make_async_copy(mids_in.at[t], mids.at[t], load_sems.at[0, t]).wait()
            gate_up = dot(mids[t], weight[...].reshape(width, cols))
        pltpu.make_async_copy(cots_in.at[t], cots.at[t], load_sems.at[1, t]).wait()
        grad_act = dot(cots[t], down[...])
        gate, upward = gate_up[:, : cols // 2], gate_up[:, cols // 2 :]
        sigmoid_gate = jax.nn.sigmoid(gate)
        silu = gate * sigmoid_gate
        act[t] = (silu * upward).astype(LOW)
        grad[t, :, : cols // 2] = (
            grad_act * upward * sigmoid_gate * (1.0 + gate * (1.0 - sigmoid_gate))
        ).astype(LOW)
        grad[t, :, cols // 2 :] = (grad_act * silu).astype(LOW)
        return carry

    if follows:
        lax.fori_loop(0, early, functools.partial(tokens, 0), 0)
        lax.fori_loop(early, count, functools.partial(tokens, early), 0)
    else:
        lax.fori_loop(0, count, functools.partial(tokens, 0), 0)

    all_act = act[...].reshape(count * block, cols // 2)
    for k in range(4):
        value = column_product(
            cots[:, :, k * quarter : (k + 1) * quarter].reshape(count * block, quarter), all_act
        ).astype(LOW)
        for member in range(group):
            for j in range(fold):
                rows[k, member, :, j * units : (j + 1) * units] = value[
                    j * owned : (j + 1) * owned, member * units : (member + 1) * units
                ]
    sent = [
        link.send(rows.at[k], term.at[pl.ds(me * group, group), 2], {"seq": k}) for k in others
    ]
    term[pl.ds(me * group, group), 2] = rows[me]
    all_grad = grad[...].reshape(count * block, cols)
    for z in range(line):
        value = column_product(
            mids[:, :, 2 * owned * z : 2 * owned * (z + 1)].reshape(count * block, 2 * owned),
            all_grad,
        ).astype(LOW)
        for y in range(2):
            term[z, y] = value[y * owned : (y + 1) * owned, :]

    def ask(t, slot):
        for place, source in enumerate((out_before, mid_before)):
            load(source.at[t], before.at[slot, place], before_sems.at[slot, place])

    if follows:
        ask(0, 0)

    def back(t, carry):
        slot = t % 2

        def hand_over(t, place, target):
            return pltpu.make_async_copy(
                stage.at[t % 2, place], target.at[t], stage_sems.at[t % 2, place]
            )

        @pl.when(t >= 2)
        def _():
            hand_over(t - 2, 0, out).wait()
            hand_over(t - 2, 1, mid).wait()

        values = [
            times_transpose(act[t], down[...]),
            times_transpose(grad[t], weight[...].reshape(width, cols)),
        ]
        if follows:

            @pl.when(t + 1 < count)
            def _():
                ask(t + 1, (t + 1) % 2)

            for place, source in enumerate((out_before, mid_before)):
                pltpu.make_async_copy(
                    source.at[t], before.at[slot, place], before_sems.at[slot, place]
                ).wait()
                values[place] = values[place] + before[slot, place].astype(F32)
        for place, target in enumerate((out, mid)):
            stage[slot, place] = values[place].astype(LOW)
            hand_over(t, place, target).start()
        return carry

    lax.fori_loop(0, count, back, 0)
    for t in (count - 2, count - 1):
        for place, target in enumerate((out, mid)):
            pltpu.make_async_copy(
                stage.at[t % 2, place], target.at[t], stage_sems.at[t % 2, place]
            ).wait()
    for copy in sent:
        copy.wait_recv()
    link.finish()


def cut_call(follows, args, sizes):
    group, line, owned, units = sizes
    mids = args[0]
    count, block, width = mids.shape
    cols = 2 * group * units
    hbm, vmem = (pl.BlockSpec(memory_space=pl.ANY), pl.BlockSpec(memory_space=pltpu.VMEM))
    rows = (4, group, owned, cols)
    low_scratch = [
        mids.shape,
        mids.shape,
        (line, 2, owned, cols),
        rows,
        (width, cols // 2),
        (count, block, cols // 2),
        (count, block, cols),
        (2, 2, block, width),
        (2, 2, block, width),
    ]
    return pl.pallas_call(
        functools.partial(cut_kernel, (follows, group, units)),
        out_shape=[
            jax.ShapeDtypeStruct((line, 3, owned, cols), LOW),
            jax.ShapeDtypeStruct(mids.shape, LOW),
            jax.ShapeDtypeStruct(mids.shape, LOW),
        ],
        in_specs=[hbm] * len(args),
        out_specs=[vmem, hbm, hbm],
        scratch_shapes=[pltpu.VMEM(shape, LOW) for shape in low_scratch]
        + [
            pltpu.VMEM((count // 2 if follows else 1, block, cols), F32),
            pltpu.SemaphoreType.DMA((2, count)),
            pltpu.SemaphoreType.DMA((line + 1,)),
            pltpu.SemaphoreType.DMA((2, 2)),
            pltpu.SemaphoreType.DMA((2, 2)),
            pltpu.SemaphoreType.DMA((6,)),
            pltpu.SemaphoreType.DMA((6,)),
        ],
        compiler_params=pltpu.CompilerParams(
            collective_id=4 if follows else 3, has_side_effects=True, vmem_limit_bytes=56 << 20
        ),
        cost_estimate=pl.CostEstimate(
            flops=50_000_000_000, bytes_accessed=40_000_000, transcendentals=2_000_000
        ),
    )(*args)


def spread_blocks(link, ids, pair, ff_sum, hidden_blocks, down_blocks, local_sems):
    core, over_x, over_y = ids
    kept, down = ff_sum.at[pair], ff_sum.at[2]
    local = [
        pltpu.make_async_copy(kept, hidden_blocks.at[0], local_sems.at[0]),
        pltpu.make_async_copy(down, down_blocks.at[0], local_sems.at[1]),
    ]
    for copy in local:
        copy.start()
    over = link.send(ff_sum.at[1 - pair], hidden_blocks.at[4], over_y)
    to_x = [
        link.send(kept, hidden_blocks.at[2], over_x),
        link.send(down, down_blocks.at[2], over_x),
    ]
    last = [
        link.send(kept, hidden_blocks.at[1], core),
        link.send(down, down_blocks.at[1], core),
    ]
    yield
    over.wait_recv()
    far = link.send(hidden_blocks.at[4], hidden_blocks.at[6], over_x)
    last.append(link.send(hidden_blocks.at[4], hidden_blocks.at[5], core))
    for copy, blocks in zip(to_x, (hidden_blocks, down_blocks)):
        copy.wait_recv()
        last.append(link.send(blocks.at[2], blocks.at[3], core))
    yield
    far.wait_recv()
    last.append(link.send(hidden_blocks.at[6], hidden_blocks.at[7], core))
    yield
    for copy in last:
        copy.wait_recv()
    for copy in local:
        copy.wait()
    yield


def output_kernel(
    terms_in,
    hidden,
    ff_sum,
    block_out,
    hidden_blocks,
    down_blocks,
    terms,
    arrived,
    held,
    from_x,
    from_y,
    corner,
    send_sems,
    recv_sems,
    load_sems,
    local_sems,
):
    _, ids = neighbours()
    core, over_x, over_y = ids
    pair = lax.axis_index("fsdp") % 2
    greet(ids)
    link = Sender(send_sems, recv_sems)
    order = (7, 6, 5, 4, 3, 2, 1, 0)
    loads = {k: pltpu.make_async_copy(terms_in.at[k], terms.at[k], load_sems.at[k]) for k in order}
    for k in order:
        loads[k].start()
    spread = spread_blocks(link, ids, pair, ff_sum, hidden_blocks, down_blocks, local_sems)
    next(spread)
    halved = {}
    for k in (6, 4, 2, 0):
        loads[k + 1].wait()
        halved[k] = link.send(terms.at[k + 1], arrived.at[k // 2], core)

    def chip_sum(k):
        loads[k].wait()
        halved[k].wait_recv()
        return terms[k].astype(F32) + arrived[k // 2].astype(F32)

    held[0] = chip_sum(6).astype(LOW)
    turn = link.send(held.at[0], corner, over_y)
    held[1] = chip_sum(4).astype(LOW)
    direct = link.send(held.at[1], from_y, over_y)
    total = chip_sum(2)
    turn.wait_recv()
    held[2] = (total + corner[...].astype(F32)).astype(LOW)
    last = link.send(held.at[2], from_x, over_x)
    next(spread)
    total = hidden[...] + chip_sum(0)
    direct.wait_recv()
    last.wait_recv()
    total = total + from_x[...].astype(F32) + from_y[...].astype(F32)
    block_out[...] = total.astype(LOW)
    next(spread)
    next(spread)
    link.finish()


def spread(ff_sum, terms, hidden):
    hbm, vmem = (pl.BlockSpec(memory_space=pl.ANY), pl.BlockSpec(memory_space=pltpu.VMEM))
    shapes = [jax.ShapeDtypeStruct((count, *ff_sum.shape[1:]), LOW) for count in (8, 4)]
    sems = [pltpu.SemaphoreType.DMA((18,))] * 2
    block = hidden.shape
    return pl.pallas_call(
        output_kernel,
        out_shape=[jax.ShapeDtypeStruct(block, LOW), *shapes],
        in_specs=[hbm, vmem, vmem],
        out_specs=[vmem, hbm, hbm],
        scratch_shapes=[
            pltpu.VMEM(shape, LOW)
            for shape in (terms.shape, (4, *block), (3, *block), block, block, block)
        ]
        + [*sems, pltpu.SemaphoreType.DMA((8,)), pltpu.SemaphoreType.DMA((2,))],
        compiler_params=pltpu.CompilerParams(
            collective_id=5, has_side_effects=True, vmem_limit_bytes=32 << 20
        ),
        cost_estimate=pl.CostEstimate(
            flops=50_000_000_000, bytes_accessed=20_000_000, transcendentals=0
        ),
    )(terms, hidden, ff_sum)


def closing_kernel(
    shape,
    mid_terms,
    hidden,
    upstream,
    tokens_all,
    normed,
    vectors,
    weight,
    proj_mine,
    queries,
    keys,
    values,
    merged,
    logsum,
    cosines,
    sines,
    seg_col,
    seg_row,
    ff_sum,
    tokens_grad,
    gain_terms,
    attn_sum,
    hidden_blocks,
    down_blocks,
    arrived,
    held,
    from_x,
    from_y,
    corner,
    upper,
    grad_heads,
    grad_queries,
    grad_keys,
    grad_values,
    kv,
    projected,
    proj_part,
    proj_in,
    proj_half,
    bias_row,
    qkv_part,
    qkv_in,
    late,
    late_x,
    send_sems,
    recv_sems,
    local_sems,
):
    owned, per_dev, group = shape
    (me, sibling, across), (core, over_x, over_y) = neighbours()
    far = across + 1 - 2 * (across % 2)
    others = (sibling, across, far)
    pair = lax.axis_index("fsdp") % 2
    rows, width = hidden.shape
    seq_count = tokens_all.shape[0]
    quarter = width // seq_count
    low, high = (pl.ds(0, rows // 2), pl.ds(rows // 2, rows // 2))
    gains = (vectors[0:1, :width], vectors[1:2, :width])
    greet((core, over_x, {"seq": far}, over_y))
    link = Sender(send_sems, recv_sems)

    halved = {k: link.send(mid_terms.at[k + 1], arrived.at[k // 2], core) for k in (6, 2, 4, 0)}

    def chip_sum(k):
        halved[k].wait_recv()
        return mid_terms[k].astype(F32) + arrived[k // 2].astype(F32)

    held[2] = chip_sum(6).astype(LOW)
    turn_y = link.send(held.at[2, low], corner.at[0], over_x)
    turn_x = link.send(held.at[2, high], corner.at[1], over_y)
    held[0] = chip_sum(2).astype(LOW)
    direct_x = link.send(held.at[0, low], from_x.at[low], over_x)
    held[1] = chip_sum(4).astype(LOW)
    direct_y = link.send(held.at[1, high], from_y.at[high], over_y)
    tokens_grad[...] = chip_sum(0)
    turn_x.wait_recv()
    held[0, high] = (held[0, high].astype(F32) + corner[1].astype(F32)).astype(LOW)
    second_x = link.send(held.at[0, high], from_x.at[high], over_x)
    turn_y.wait_recv()
    held[1, low] = (held[1, low].astype(F32) + corner[0].astype(F32)).astype(LOW)
    second_y = link.send(held.at[1, low], from_y.at[low], over_y)
    for copy in (direct_x, direct_y, second_x, second_y):
        copy.wait_recv()

    grad_mid = tokens_grad[...] + from_x[...].astype(F32) + from_y[...].astype(F32)
    through, term = norm_back(hidden[...], inverse_rms(hidden[...]), gains[1], grad_mid)
    gain_terms[1:2, :] = term[None]
    total = upstream[...].astype(F32) + through
    tokens_grad[...] = total
    upper[me] = total.astype(LOW)
    last = [link.send(upper.at[me], upper.at[me], core)]
    to_x = [link.send(upper.at[me, half], upper.at[me, half], over_x) for half in (low, high)]
    for copy, half in zip(to_x, (low, high)):
        copy.wait_recv()
        last.append(link.send(upper.at[across, half], upper.at[across, half], core))
    for copy in last:
        copy.wait_recv()

    head_rows = per_dev * HD
    for block in range(seq_count):
        grad_heads[block * rows : (block + 1) * rows, :] = sum(
            times_transpose(
                upper[block, :, k * quarter : (k + 1) * quarter],
                proj_mine[k].reshape(head_rows, quarter),
            )
            for k in range(seq_count)
        ).astype(LOW)
    for k in range(seq_count):
        term = sum(
            column_product(
                merged[block * rows : (block + 1) * rows, :],
                upper[block, :, k * quarter : (k + 1) * quarter],
            )
            for block in range(seq_count)
        ).astype(LOW)
        for member in range(group):
            for y in range(2):
                first = (2 * member + y) * owned
                proj_part[y, k, member] = term[first : first + owned, :]
    proj_over = link.send(proj_part.at[1 - pair], proj_in, over_y)
    spread = spread_blocks(
        link, (core, over_x, over_y), pair, ff_sum, hidden_blocks, down_blocks, local_sems
    )
    next(spread)

    grad_keys[...] = jnp.zeros_like(grad_keys)
    grad_values[...] = jnp.zeros_like(grad_values)
    scale = HD ** (-0.5)
    for block in range(seq_count):
        here, last_key = pl.ds(block * rows, rows), (block + 1) * rows
        row_index = block * rows + lax.broadcasted_iota(jnp.int32, (rows, last_key), 0)
        key_index = lax.broadcasted_iota(jnp.int32, (rows, last_key), 1)
        allowed = (key_index <= row_index) & (seg_col[here, :] == seg_row[:, :last_key])
        for head in range(per_dev):
            query = queries[head, here, :]
            upper_head = grad_heads[here, head * HD : (head + 1) * HD]
            scores = times_transpose(query, keys[:last_key, :]) * scale
            probs = jnp.where(allowed, jnp.exp(scores - logsum[head, here, :]), 0.0)
            grad_probs = times_transpose(upper_head, values[:last_key, :])
            inner = jnp.sum(probs * grad_probs, axis=-1, keepdims=True)
            grad_scores = (probs * (grad_probs - inner)).astype(LOW)
            grad_queries[head, here, :] = (dot(grad_scores, keys[:last_key, :]) * scale).astype(LOW)
            grad_keys[:last_key, :] += column_product(grad_scores, query)
            grad_values[:last_key, :] += column_product(probs.astype(LOW), upper_head)
    next(spread)
    holds_values = me % 2 == 1
    key_copy = (grad_keys[...] * scale).astype(LOW)
    value_copy = grad_values[...].astype(LOW)
    kv[0] = jnp.where(holds_values, key_copy, value_copy)
    swapped = link.send(kv.at[0], kv.at[1], core)
    grad_keys[...] = jnp.where(holds_values, value_copy, key_copy).astype(F32)
    proj_over.wait_recv()
    proj_half[...] = (proj_part[pair].astype(F32) + proj_in[...].astype(F32)).astype(LOW)
    cols = weight.shape[1]

    def proj_place(device):
        return (pl.ds(device * group, group), pl.ds(0, owned), pl.ds(cols, quarter))

    last = [
        link.send(proj_half.at[k], attn_sum.at[proj_place(me)], {"seq": k}) for k in others
    ]
    attn_sum[proj_place(me)] = proj_half[me]
    swapped.wait_recv()
    grad_kv = grad_keys[...] + kv[1].astype(F32)

    bias_row[...] = jnp.zeros_like(bias_row)
    bias_parts = 0.0
    gain_terms[0:1, :] = jnp.zeros((1, width), F32)
    for block in range(seq_count):
        here = pl.ds(block * rows, rows)
        cosine, sine = cosines[here, :], sines[here, :]

        def rotate_back(head):
            return head * cosine - pltpu.roll(head, HD // 2, 1) * sine

        for head in range(per_dev):
            projected[here, head * HD : (head + 1) * HD] = rotate_back(
                grad_queries[head, here, :].astype(F32)
            ).astype(LOW)
        plain = grad_kv[block * rows : (block + 1) * rows, :]
        projected[here, head_rows:] = jnp.where(holds_values, plain, rotate_back(plain)).astype(LOW)
        grad_block = projected[here, :]
        bias_parts += jnp.sum(grad_block.astype(F32), axis=0, keepdims=True)
        grad_in = times_transpose(grad_block, weight[...])
        value = tokens_all[block].astype(F32)
        gain_terms[0:1, :] += jnp.sum(
            grad_in * value * inverse_rms(value), axis=0, keepdims=True
        )
        arrived[block] = grad_in.astype(LOW)
    first = link.send(arrived.at[far], late.at[0], core)
    second = link.send(arrived.at[sibling], late.at[1], core)
    first.wait_recv()
    link.release(direct_x, second_x)
    held[0] = (arrived[across].astype(F32) + late[0].astype(F32)).astype(LOW)
    third = link.send(held.at[0], late_x, over_x)
    kv_first = (H + KV * (me % 2) + me // 2) * HD
    bias_row[0:1, pl.ds(pl.multiple_of(me * head_rows, HD), head_rows)] = bias_parts[:, :head_rows]
    bias_row[0:1, pl.ds(pl.multiple_of(kv_first, HD), HD)] = bias_parts[:, head_rows:]
    line = qkv_in.shape[0]
    owned_bias = bias_row.shape[1] // (2 * line)
    qkv_part[:, :, owned:, :] = jnp.zeros_like(qkv_part[:, :, owned:, :])
    for z in range(line):
        for y in range(2):
            owner, at = 2 * z + y, 0
            for source, row, length in (
                (gain_terms, 0, owned),
                (gain_terms, 1, owned),
                (bias_row, 0, owned_bias),
            ):
                done = 0
                while done < length:
                    span = min(length - done, cols - at % cols)
                    first_col = owner * length + done
                    qkv_part[
                        y, z, owned + at // cols : owned + at // cols + 1, at % cols : at % cols + span
                    ] = source[row : row + 1, first_col : first_col + span].astype(LOW)
                    done, at = done + span, at + span
    for z in range(line):
        term = sum(
            column_product(
                normed[block, :, 2 * owned * z : 2 * owned * (z + 1)],
                projected[block * rows : (block + 1) * rows, :],
            )
            for block in range(seq_count)
        ).astype(LOW)
        for y in range(2):
            qkv_part[y, z, :owned, :] = term[y * owned : (y + 1) * owned, :]
    qkv_over = link.send(qkv_part.at[1 - pair], qkv_in, over_y)
    next(spread)
    second.wait_recv()
    third.wait_recv()
    grad_in = arrived[me].astype(F32) + late[1].astype(F32) + late_x[...].astype(F32)
    value = tokens_all[me].astype(F32)
    through, _ = norm_back(value, inverse_rms(value), gains[0], grad_in)
    tokens_grad[...] += through
    qkv_over.wait_recv()
    attn_sum[:, :, :cols] = (qkv_part[pair].astype(F32) + qkv_in[...].astype(F32)).astype(LOW)
    attn_sum[:, owned:, cols:] = jnp.zeros_like(attn_sum[:, owned:, cols:])
    for copy in last:
        copy.wait_recv()
    next(spread)
    link.finish()


def closing(args, sizes):
    owned, vector_rows, bias_cols, per_dev, group, line = sizes
    hidden, weight, proj_mine = args[1], args[6], args[7]
    rows, width = hidden.shape
    block = (rows, width)
    cols = weight.shape[1]
    quarter = proj_mine.shape[-1]
    heads = (4 * rows, HD)
    rows_in = (4, group, owned, quarter)
    outs = [
        jax.ShapeDtypeStruct(block, F32),
        jax.ShapeDtypeStruct((2, width), F32),
        jax.ShapeDtypeStruct((line, owned + vector_rows, cols + quarter), LOW),
        jax.ShapeDtypeStruct((8, *args[-1].shape[1:]), LOW),
        jax.ShapeDtypeStruct((4, *args[-1].shape[1:]), LOW),
    ]
    low_scratch = [
        (4, *block),
        (3, *block),
        block,
        block,
        (2, rows // 2, width),
        (4, *block),
        (4 * rows, per_dev * HD),
        (per_dev, *heads),
    ]
    return pl.pallas_call(
        functools.partial(closing_kernel, (owned, per_dev, group)),
        out_shape=outs,
        in_specs=[pl.BlockSpec(memory_space=pltpu.VMEM)] * len(args),
        out_specs=[pl.BlockSpec(memory_space=pltpu.VMEM)] * (len(outs) - 2)
        + [pl.BlockSpec(memory_space=pl.ANY)] * 2,
        scratch_shapes=[pltpu.VMEM(shape, LOW) for shape in low_scratch]
        + [pltpu.VMEM(heads, F32)] * 2
        + [
            pltpu.VMEM(shape, LOW)
            for shape in (
                (2, *heads),
                (4 * rows, cols),
                (2, *rows_in),
                rows_in,
                rows_in,
            )
        ]
        + [pltpu.VMEM((1, bias_cols), F32)]
        + [
            pltpu.VMEM(shape, LOW)
            for shape in (
                (2, line, owned + vector_rows, cols),
                (line, owned + vector_rows, cols),
                (2, *block),
                block,
            )
        ]
        + [pltpu.SemaphoreType.DMA((48,))] * 2
        + [pltpu.SemaphoreType.DMA((2,))],
        compiler_params=pltpu.CompilerParams(
            collective_id=2, has_side_effects=True, vmem_limit_bytes=58 << 20
        ),
        cost_estimate=pl.CostEstimate(
            flops=100_000_000_000, bytes_accessed=40_000_000, transcendentals=4_000_000
        ),
    )(*args)


def columns_kernel(place, *refs):
    *pieces, out = refs
    row = 0
    for piece in pieces:
        count, rows, quarter = piece.shape
        for k in range(count):
            here = place[0] + k - 2 * ((place[0] % 2) * (k % 2)) - 4 * (
                (place[0] // 2 % 2) * (k // 2 % 2)
            )
            out[pl.ds(row, rows), pl.ds(k * quarter, quarter)] = piece[here].astype(F32)
        row += rows


def columns_call(place, pieces):
    rows = sum(piece.shape[1] for piece in pieces)
    width = pieces[0].shape[0] * pieces[0].shape[2]
    return pl.pallas_call(
        columns_kernel,
        out_shape=jax.ShapeDtypeStruct((rows, width), F32),
        in_specs=[pl.BlockSpec(memory_space=pltpu.SMEM)]
        + [pl.BlockSpec(memory_space=pltpu.VMEM)] * len(pieces),
        out_specs=pl.BlockSpec(memory_space=pltpu.VMEM),
        compiler_params=pltpu.CompilerParams(vmem_limit_bytes=40 << 20),
    )(place, *pieces)


def down_kernel(fold, place, *refs):
    *pieces, out = refs
    row = 0
    for piece in pieces:
        count, owned, width = piece.shape
        span = width // fold
        for k in range(count):
            here = place[0] + k - 2 * ((place[0] % 2) * (k % 2)) - 4 * (
                (place[0] // 2 % 2) * (k // 2 % 2)
            )
            whole = piece[here].astype(F32)
            for j in range(fold):
                whole_part = whole[:, j * span : (j + 1) * span]
                out[pl.ds(row, span), pl.ds((k * fold + j) * owned, owned)] = whole_part.T
        row += span


def down_call(place, pieces, fold):
    rows = sum(piece.shape[2] // fold for piece in pieces)
    width = pieces[0].shape[0] * pieces[0].shape[1] * fold
    return pl.pallas_call(
        functools.partial(down_kernel, fold),
        out_shape=jax.ShapeDtypeStruct((rows, width), F32),
        in_specs=[pl.BlockSpec(memory_space=pltpu.SMEM)]
        + [pl.BlockSpec(memory_space=pltpu.VMEM)] * len(pieces),
        out_specs=pl.BlockSpec(memory_space=pltpu.VMEM),
        compiler_params=pltpu.CompilerParams(vmem_limit_bytes=40 << 20),
    )(place, *pieces)


def hidden_kernel(cuts, group, place, *refs):
    *pieces, out = refs
    units = cuts[-1][1]
    count = pieces[0].shape[0] // 2
    for k in range(count):
        here = place[0] + k - 2 * ((place[0] % 2) * (k % 2)) - 4 * (
            (place[0] // 2 % 2) * (k // 2 % 2)
        )
        for pair in range(2):
            entry = (pair + place[1] - 2 * pair * place[1]) * count + here
            for part in range(2):
                for member in range(group):
                    first = (((part * count + k) * group + member) * 2 + pair) * units
                    for piece, (low, high) in zip(pieces, cuts):
                        span = high - low
                        at = (part * group + member) * span
                        out[:, first + low : first + high] = piece[entry][
                            :, at : at + span
                        ].astype(F32)


def hidden_call(place, pieces, cuts, group):
    rows = pieces[0].shape[1]
    units = cuts[-1][1]
    width = 2 * 8 * group * units
    step = 16
    return pl.pallas_call(
        functools.partial(hidden_kernel, cuts, group),
        grid=(rows // step,),
        out_shape=jax.ShapeDtypeStruct((rows, width), F32),
        in_specs=[pl.BlockSpec(memory_space=pltpu.SMEM)]
        + [pl.BlockSpec((8, step, piece.shape[2]), lambda i: (0, i, 0)) for piece in pieces],
        out_specs=pl.BlockSpec((step, width), lambda i: (i, 0)),
        compiler_params=pltpu.CompilerParams(vmem_limit_bytes=40 << 20),
    )(place, *pieces)


def local(
    tokens,
    segment_ids,
    attn_gain,
    qkv_weight,
    qkv_bias,
    proj_weight,
    mlp_gain,
    gate_up_weight,
    down_weight,
    cotangent,
):
    seq_count = lax.axis_size("seq")
    fsdp_count = lax.axis_size("fsdp")
    line = fsdp_count // 2
    place = lax.axis_index("seq")
    odd = lax.axis_index("fsdp") % 2 == 1
    tok_rows, width = tokens.shape[1:]
    seq_len = tok_rows * seq_count
    owned = qkv_weight.shape[0]
    owned_hidden = down_weight.shape[0]
    hidden = owned_hidden * fsdp_count
    quarter = width // seq_count
    per_dev = H // seq_count
    head_cols = per_dev * HD
    score_scale = HD ** (-0.5)
    group = line // seq_count
    cut_at = owned_hidden // 2 // 128 * 128
    cuts = [(0, cut_at), (cut_at, owned_hidden)]

    holds_values = place % 2 == 1
    kv_first = (H + KV * (place % 2) + place // 2) * HD
    qkv_own = jnp.concatenate(
        [
            lax.dynamic_slice_in_dim(qkv_weight, place * head_cols, head_cols, 1),
            lax.dynamic_slice_in_dim(qkv_weight, kv_first, HD, 1),
        ],
        axis=1,
    )
    cols = head_cols + HD
    vector = jnp.concatenate([attn_gain, mlp_gain, qkv_bias])
    vector_size = vector.shape[0]
    vector_rows = -(-vector_size // (16 * cols)) * 16
    vector = jnp.pad(vector, (0, vector_rows * cols - vector_size)).reshape(vector_rows, cols)
    proj_cols = lax.dynamic_slice_in_dim(proj_weight, place * quarter, quarter, 1)
    down_cols = lax.dynamic_slice_in_dim(down_weight, place * quarter, quarter, 1)
    fold = quarter // owned

    def folded(value):
        return jnp.concatenate(
            [value[..., j * owned : (j + 1) * owned, :] for j in range(fold)], axis=-1
        )

    def ff_columns(low, high, pair):
        return jnp.concatenate(
            [
                lax.dynamic_slice_in_dim(
                    gate_up_weight,
                    first + ((place * group + member) * 2 + pair) * owned_hidden + low,
                    high - low,
                    1,
                )
                for first in (0, hidden)
                for member in range(group)
            ],
            axis=1,
        )

    ff_sent = []
    for low, high in cuts:
        by_owner = [ff_columns(low, high, pair) for pair in range(2)]
        ff_sent.append((by_owner, folded(jnp.transpose(down_cols[low:high]))))
    (by_owner, second_down) = ff_sent[1]
    kept, given = pick(odd, *by_owner)
    second_sent = jnp.stack([*by_pair(kept, swap(given, "fsdp", 1)), second_down])

    segment_row = segment_ids[0]
    doc_starts = jnp.sum((segment_row[None, :] < segment_row[:, None]).astype(jnp.int32), axis=1)
    places = jnp.arange(seq_len, dtype=jnp.int32) - doc_starts
    inverse = THETA ** (-2.0 * jnp.arange(HD // 2, dtype=F32) / HD)
    angles = places.astype(F32)[:, None] * inverse[None, :]
    angles = jnp.concatenate([angles, angles], axis=-1)
    cosines = jnp.cos(angles)
    signs = jnp.where(jnp.arange(HD) < HD // 2, -1.0, 1.0).astype(F32)
    sines = jnp.sin(angles) * signs

    (
        tokens_all,
        qkv_mine,
        vectors,
        proj_mine,
        first_all,
        first_rows,
        second_sent,
        normed_in,
        queries,
        head_keys,
        head_values,
        merged,
        logsum,
        attended,
        cots,
    ) = opening(
        tokens[0],
        cotangent[0],
        jnp.concatenate([qkv_own, vector], axis=0),
        lax.dynamic_slice_in_dim(proj_weight, place * quarter, quarter, 1),
        (jnp.stack(ff_sent[0][0]), ff_sent[0][1], second_sent),
        (cosines, sines),
        (segment_row[:, None], segment_row[None]),
        (owned, vector_size, per_dev, group, line),
    )
    second_all = line_gather(second_sent)
    hidden_in, mids = middle(attended, tokens[0], vectors)

    spans = [high - low for low, high in cuts]
    first_term, out_first, mid_first = cut_call(
        False, (mids, cots, first_all, first_rows), (group, line, owned, spans[0])
    )
    second_term, out, grad_mid = cut_call(
        True, (mids, cots, second_all, out_first, mid_first), (group, line, owned, spans[1])
    )

    sums = [line_reduce(term) for term in (first_term, second_term)]

    tokens_grad, gain_terms, attn_term, *first_blocks = closing(
        (
            grad_mid,
            hidden_in,
            cotangent[0],
            tokens_all,
            normed_in,
            vectors,
            qkv_mine,
            proj_mine,
            queries,
            head_keys,
            head_values,
            merged,
            logsum,
            cosines,
            sines,
            segment_row[:, None],
            segment_row[None],
            sums[0],
        ),
        (owned, vector_rows, qkv_weight.shape[1], per_dev, group, line),
    )
    places_here = jnp.stack([place, lax.axis_index("fsdp") % 2]).astype(jnp.int32)
    attn_term = attn_term + nought(sums[1][0, 0, 0])
    attn_sum = line_reduce(attn_term)
    block_out, *second_blocks = spread(sums[1], out, hidden_in + nought(attn_term[0, 0, 0]))
    hidden_pieces = [first_blocks[0], second_blocks[0]]
    down_pieces = [first_blocks[1], second_blocks[1]]
    down_grad = down_call(places_here, down_pieces, fold)
    gate_up_grad = hidden_call(places_here, hidden_pieces, cuts, group)
    attn_sums = seq_blocks(attn_sum + nought(block_out[0, 0]))
    proj_grad = columns_call(
        places_here, [jnp.stack([part[:owned, cols:] for part in attn_sums])]
    )
    qkv_sums = in_order([part[:, :cols] for part in attn_sums])
    qkv_grad = jnp.concatenate(
        [part[:owned, :head_cols] for part in qkv_sums]
        + [part[:owned, head_cols:] for part in qkv_sums[0::2]]
        + [part[:owned, head_cols:] for part in qkv_sums[1::2]],
        axis=-1,
    ).astype(F32)
    vector_sum = sum(part[owned:].astype(F32) for part in qkv_sums).reshape(-1)
    return (
        block_out[None],
        tokens_grad[None],
        vector_sum[:owned],
        qkv_grad,
        vector_sum[2 * owned : vector_size],
        proj_grad,
        vector_sum[owned : 2 * owned],
        gate_up_grad,
        down_grad,
    )


def solution(mesh):
    in_specs = (
        P("fsdp", "seq", None),
        P("fsdp", None),
        P("fsdp"),
        P("fsdp", None),
        P("fsdp"),
        P("fsdp", None),
        P("fsdp"),
        P("fsdp", None),
        P("fsdp", None),
        P("fsdp", "seq", None),
    )
    out_specs = (
        P("fsdp", "seq", None),
        P("fsdp", "seq", None),
        P("fsdp"),
        P("fsdp", None),
        P("fsdp"),
        P("fsdp", None),
        P("fsdp"),
        P("fsdp", None),
        P("fsdp", None),
    )
    return jax.shard_map(local, mesh=mesh, in_specs=in_specs, out_specs=out_specs, check_vma=False)
```

```python
import functools

import jax
import jax.numpy as jnp
from jax import lax
from jax.experimental import pallas as pl
from jax.experimental.pallas import tpu as pltpu
from jax.sharding import PartitionSpec as P

H = 12
KV = 2
HD = 128
EPSILON = 1e-06
THETA = 1000000.0
FLOOR = -1e30
LOW = jnp.bfloat16
F32 = jnp.float32


def inverse_rms(value):
    return lax.rsqrt(jnp.mean(value * value, axis=-1, keepdims=True) + EPSILON)


def turned(value):
    halfway = value.shape[-1] // 2
    return jnp.concatenate([-value[..., halfway:], value[..., :halfway]], axis=-1)


def turned_back(value):
    halfway = value.shape[-1] // 2
    return jnp.concatenate([value[..., halfway:], -value[..., :halfway]], axis=-1)


def norm_back(value, factor, gain, upstream):
    weighted = upstream * gain
    gain_term = jnp.sum(upstream * value * factor, axis=0)
    through = factor * weighted - value * factor**3 * jnp.mean(
        weighted * value, axis=-1, keepdims=True
    )
    return (through, gain_term)


def dot(left, right):
    return jnp.dot(left, right, preferred_element_type=F32)


def column_product(left, right):
    return lax.dot_general(left, right, (((0,), (0,)), ((), ())), preferred_element_type=F32)


def times_transpose(left, right):
    return lax.dot_general(left, right, (((1,), (1,)), ((), ())), preferred_element_type=F32)


def swap(value, axis, distance):
    return lax.ppermute(value, axis, [(i, i ^ distance) for i in range(lax.axis_size(axis))])


def lines():
    size = lax.axis_size("fsdp")
    return [list(range(first, size, 2)) for first in range(2)]


def line_gather(value):
    return lax.all_gather(value, "fsdp", axis=0, axis_index_groups=lines(), tiled=False)


def line_reduce(value):
    return lax.psum_scatter(
        value, "fsdp", scatter_dimension=0, axis_index_groups=lines(), tiled=False
    )


def by_pair(own, other):
    second = lax.axis_index("fsdp") % 2 == 1
    return (jnp.where(second, other, own), jnp.where(second, own, other))


def pick(flag, first, second):
    return (jnp.where(flag, second, first), jnp.where(flag, first, second))


def nought(value):
    return jnp.minimum(jnp.abs(value), 0.0).astype(LOW)


def seq_blocks(value):
    across = swap(value, "seq", 2)
    return [value, swap(value, "seq", 1), across, swap(across, "seq", 1)]


def seq_reduce(parts):
    arrived = swap(jnp.stack([parts[1], parts[3]]), "seq", 1)
    across = (parts[2].astype(F32) + arrived[1].astype(F32)).astype(LOW)
    here = parts[0].astype(F32) + arrived[0].astype(F32)
    return here + swap(across, "seq", 2).astype(F32)


def in_order(blocks):
    me = lax.axis_index("seq")
    bits = 1
    while bits < len(blocks):
        flip = (me & bits) != 0
        blocks = [jnp.where(flip, blocks[k ^ bits], blocks[k]) for k in range(len(blocks))]
        bits *= 2
    return blocks


def relative(value):
    size = lax.axis_size("seq")
    me = lax.axis_index("seq")
    cut = value.reshape(size, value.shape[0] // size, *value.shape[1:])
    return [lax.dynamic_index_in_dim(cut, me ^ k, 0, keepdims=False) for k in range(size)]


def seq_exchange(pieces):
    taken = [part[0] for part in relative(pieces)]
    return in_order([taken[0]] + [swap(taken[k], "seq", k) for k in range(1, len(taken))])


MESH = pl.DeviceIdType.MESH


def neighbours():
    me, owner = lax.axis_index("seq"), lax.axis_index("fsdp")
    sibling = me + 1 - 2 * (me % 2)
    across = me + 2 - 4 * (me // 2 % 2)
    partner = owner + 1 - 2 * (owner % 2)
    return (me, sibling, across), ({"seq": sibling}, {"seq": across}, {"fsdp": partner})


def greet(devices):
    barrier = pltpu.get_barrier_semaphore()
    for device in devices:
        pl.semaphore_signal(barrier, inc=1, device_id=device, device_id_type=MESH)
    pl.semaphore_wait(barrier, len(devices))


class Sender:
    def __init__(self, send_sems, recv_sems):
        self.sems = (send_sems, recv_sems)
        self.count, self.open = 0, []

    def send(self, source, target, device):
        number = self.count
        copy = pltpu.make_async_remote_copy(
            src_ref=source,
            dst_ref=target,
            send_sem=self.sems[0].at[number],
            recv_sem=self.sems[1].at[number],
            device_id=device,
            device_id_type=MESH,
        )
        copy.start()
        self.count += 1
        self.open.append(copy)
        return copy

    def release(self, *copies):
        for copy in copies:
            copy.wait_send()
            self.open = [other for other in self.open if other is not copy]

    def finish(self):
        self.release(*self.open)


def plane_gather(link, blocks, ids):
    core, over_x, over_y = ids
    rows = blocks.shape[1]
    halves = (pl.ds(0, rows // 2), pl.ds(rows // 2, rows // 2))
    to_x = [link.send(blocks.at[0, half], blocks.at[2, half], over_x) for half in halves]
    last = [link.send(blocks.at[0], blocks.at[1], core)]
    yield
    to_y = [link.send(blocks.at[0, half], blocks.at[4, half], over_y) for half in halves[::-1]]
    yield
    to_x[0].wait_recv()
    diagonal = [link.send(blocks.at[2, halves[0]], blocks.at[6, halves[0]], over_y)]
    last.append(link.send(blocks.at[2, halves[0]], blocks.at[3, halves[0]], core))
    to_y[0].wait_recv()
    diagonal.append(link.send(blocks.at[4, halves[1]], blocks.at[6, halves[1]], over_x))
    last.append(link.send(blocks.at[4, halves[1]], blocks.at[5, halves[1]], core))
    to_x[1].wait_recv()
    last.append(link.send(blocks.at[2, halves[1]], blocks.at[3, halves[1]], core))
    to_y[1].wait_recv()
    last.append(link.send(blocks.at[4, halves[0]], blocks.at[5, halves[0]], core))
    for copy, half in zip(diagonal, halves):
        copy.wait_recv()
        last.append(link.send(blocks.at[6, half], blocks.at[7, half], core))
    for copy in last:
        copy.wait_recv()
    yield


def opening_kernel(
    shape,
    tokens,
    cotangent,
    qkv,
    proj,
    ff_own,
    ff_down,
    second_own,
    second_down,
    inverse,
    seg_col,
    seg_row,
    cosines,
    sines,
    tokens_out,
    weight,
    vectors,
    proj_mine,
    ff_all,
    ff_rows,
    second_out,
    normed_out,
    queries,
    keys,
    values,
    merged,
    logsum,
    part_out,
    cots_out,
    tokens_all,
    normed,
    part,
    cots,
    qkv_all,
    proj_all,
    ff_line,
    kv,
    send_sems,
    recv_sems,
    hand_send,
    hand_recv,
    local_sem,
):
    owned, vector_size, per_dev, group = shape
    (me, sibling, across), ids = neighbours()
    core, over_x, over_y = ids
    far = across + 1 - 2 * (across % 2)
    line = qkv_all.shape[0]
    size = 2 * line
    owner = lax.axis_index("fsdp")
    at, pair = owner // 2, owner % 2
    below, above = ({"fsdp": (owner + size - 2) % size}, {"fsdp": (owner + 2) % size})
    rows, width = tokens.shape
    seq_count = tokens_all.shape[0]
    seq_len = seq_count * rows
    halves = (pl.ds(0, rows // 2), pl.ds(rows // 2, rows // 2))
    others = (sibling, across, far)
    greet((*ids, {"seq": far}, below, above))
    link = Sender(send_sems, recv_sems)

    own_copy = pltpu.make_async_copy(ff_own.at[pair], ff_all.at[at, pair], local_sem.at[0])
    own_copy.start()
    leaving = [own_copy]

    def leave(source, target):
        copy = pltpu.make_async_copy(source, target, local_sem.at[len(leaving)])
        copy.start()
        leaving.append(copy)

    leave(second_own.at[pair], second_out.at[pair])
    leave(second_down, second_out.at[2])
    ff_line[at] = ff_down[...]
    tokens_all[me] = tokens[...]
    qkv_all[at, pair] = qkv[...]
    proj_all[at, pair] = proj[...]

    turned, handed = [], []

    def hand_on(k):
        z = (at + k) % line
        target, member = z // group, z % group
        copy = pltpu.make_async_remote_copy(
            src_ref=ff_line.at[z],
            dst_ref=ff_rows.at[me, member],
            send_sem=hand_send.at[k],
            recv_sem=hand_recv.at[me * group + member],
            device_id={"seq": target},
            device_id_type=MESH,
        )

        @pl.when(target != me)
        def _():
            copy.start()

        @pl.when(target == me)
        def _():
            ff_rows[me, member] = ff_line[z]

        handed.append((copy, target))

    def ring_steps():
        before = [None] * 3
        for k in range(line):
            z = (at + k) % line
            here = (ff_line.at[z], ff_all.at[z, pair], ff_all.at[z, 1 - pair])
            for place, target in enumerate(here):
                source = ff_own.at[pair] if k == 0 and place == 1 else target
                if k > 0:
                    before[place].wait_recv()
                elif place == 2:
                    turned[0].wait_recv()
                if k < line - 1:
                    before[place] = link.send(source, target, below)
                if place == 0:
                    hand_on(k)
                yield

    ring = ring_steps()

    def pump(count):
        for _ in range(count):
            next(ring, None)

    def along_line(array, k):
        here = array.at[(at + k) % line, pair]
        return link.send(here, here, below)

    def to_partner(array, k):
        here = array.at[(at + k) % line, pair]
        return link.send(here, here, over_y)

    onward = along_line(qkv_all, 0)
    last = [to_partner(qkv_all, 0)]
    to_x = [link.send(tokens_all.at[me, half], tokens_all.at[me, half], over_x) for half in halves]
    last.append(link.send(tokens_all.at[me], tokens_all.at[me], core))
    proj_onward = along_line(proj_all, 0)

    lanes = lax.broadcasted_iota(jnp.int32, (rows, HD), 1)
    for block in range(seq_count):
        here = pl.ds(block * rows, rows)
        before = jnp.sum((seg_row[...] < seg_col[here, :]).astype(F32), axis=1, keepdims=True)
        index = (block * rows + lax.broadcasted_iota(jnp.int32, (rows, 1), 0)).astype(F32)
        angles = (index - before) * inverse[...]
        cosines[here, :] = jnp.cos(angles)
        sines[here, :] = jnp.where(lanes < HD // 2, -jnp.sin(angles), jnp.sin(angles))
    for k in range(1, line):
        onward.wait_recv()
        if k < line - 1:
            onward = along_line(qkv_all, k)
        last.append(to_partner(qkv_all, k))
        proj_onward.wait_recv()
        if k < line - 1:
            proj_onward = along_line(proj_all, k)
        if k == line - 2:
            pump(2)
    turned.append(link.send(ff_own.at[1 - pair], ff_all.at[at, pair], over_y))
    for copy, half in zip(to_x, halves):
        copy.wait_recv()
        last.append(link.send(tokens_all.at[across, half], tokens_all.at[across, half], core))
    for copy in last:
        copy.wait_recv()
    proj_over = [to_partner(proj_all, k) for k in range(line)]
    second_over = link.send(second_own.at[1 - pair], second_out.at[pair], over_y)
    leave(tokens_all, tokens_out)
    cots[0] = cotangent[...]
    gather_cots = plane_gather(link, cots, ids)
    next(gather_cots)

    for z in range(line):
        for y in range(2):
            owner_row = 2 * z + y
            weight[pl.ds(owner_row * owned, owned), :] = qkv_all[z, y, :owned, :]
            done = 0
            cols = qkv_all.shape[3]
            for start, count, target in (
                (0, owned, 0),
                (owned, owned, 1),
                (2 * owned, vector_size - 2 * owned, 2),
            ):
                while count > 0:
                    row, col = start // cols, start % cols
                    span = min(count, cols - col)
                    length = (owned, owned, vector_size - 2 * owned)[target]
                    to = owner_row * length + (length - count)
                    vectors[target : target + 1, to : to + span] = qkv_all[
                        z, y, owned + row : owned + row + 1, col : col + span
                    ].astype(F32)
                    start, count = start + span, count - span

    head_cols = per_dev * HD
    holds_values = me % 2 == 1
    kv_first = (H + KV * (me % 2) + me // 2) * HD
    bias = jnp.concatenate(
        [
            vectors[2:3, pl.ds(pl.multiple_of(me * head_cols, HD), head_cols)],
            vectors[2:3, pl.ds(pl.multiple_of(kv_first, HD), HD)],
        ],
        axis=1,
    )
    for block in range(seq_count):
        here = pl.ds(block * rows, rows)
        value = tokens_all[block].astype(F32)
        normal = (value * inverse_rms(value) * vectors[0:1, :width]).astype(LOW)
        normed[block] = normal
        projected = dot(normal, weight[...]) + bias
        cosine, sine = cosines[here, :], sines[here, :]

        def rotate(head):
            return head * cosine + pltpu.roll(head, HD // 2, 1) * sine

        for head in range(per_dev):
            queries[head, here, :] = rotate(projected[:, head * HD : (head + 1) * HD]).astype(LOW)
        plain = projected[:, head_cols:]
        kv[0, here, :] = jnp.where(holds_values, plain, rotate(plain)).astype(LOW)
    swapped = link.send(kv.at[0], kv.at[1], core)
    leave(normed, normed_out)
    pump(3)
    swapped.wait_recv()
    keys[...] = jnp.where(holds_values, kv[1], kv[0])
    values[...] = jnp.where(holds_values, kv[0], kv[1])

    for copy in proj_over:
        copy.wait_recv()
    exchange = [
        link.send(proj_all.at[pl.ds(target * group, group)], proj_mine.at[me], {"seq": target})
        for target in others
    ]
    next(gather_cots)
    proj_mine[me] = proj_all[pl.ds(me * group, group)]

    for block in range(seq_count):
        here, last_key = pl.ds(block * rows, rows), (block + 1) * rows
        row_index = block * rows + lax.broadcasted_iota(jnp.int32, (rows, last_key), 0)
        key_index = lax.broadcasted_iota(jnp.int32, (rows, last_key), 1)
        allowed = (key_index <= row_index) & (seg_col[here, :] == seg_row[:, :last_key])
        for head in range(per_dev):
            scores = times_transpose(queries[head, here, :], keys[:last_key, :]) * HD ** (-0.5)
            scores = jnp.where(allowed, scores, FLOOR)
            highest = jnp.max(scores, axis=-1, keepdims=True)
            exponent = jnp.exp(scores - highest)
            total = jnp.sum(exponent, axis=-1, keepdims=True)
            mixture = dot((exponent / total).astype(LOW), values[:last_key, :])
            merged[here, head * HD : (head + 1) * HD] = mixture.astype(LOW)
            logsum[head, here, :] = highest + jnp.log(total)
    pump(2)
    for copy in exchange:
        copy.wait_recv()
    quarter = proj.shape[1]
    for block in range(seq_count):
        for k in range(seq_count):
            columns = proj_mine[k].reshape(-1, quarter)
            part[block, :, k * quarter : (k + 1) * quarter] = dot(
                merged[block * rows : (block + 1) * rows, :], columns
            ).astype(LOW)

    leave(part, part_out)
    pump(1)
    next(gather_cots)
    leave(cots, cots_out)
    pump(3 * line)
    for copy in leaving:
        copy.wait()
    second_over.wait_recv()
    for source in others:
        for member in range(group):
            pltpu.make_async_remote_copy(
                src_ref=ff_line.at[0],
                dst_ref=ff_rows.at[source, member],
                send_sem=hand_send.at[0],
                recv_sem=hand_recv.at[source * group + member],
                device_id=core,
                device_id_type=MESH,
            ).wait_recv()
    for copy, target in handed:

        @pl.when(target != me)
        def _():
            copy.wait_send()

    link.finish()


def opening(tokens, cotangent, qkv, proj, ff, inverse, segments, sizes):
    owned, vector_size, per_dev, group, line = sizes
    rows, width = tokens.shape
    block = (rows, width)
    seq_len = 4 * rows
    cols = qkv.shape[1]
    heads = (seq_len, HD)
    vmem, hbm = (pl.BlockSpec(memory_space=pltpu.VMEM), pl.BlockSpec(memory_space=pl.ANY))

    def like(*shape, dtype=LOW):
        return jax.ShapeDtypeStruct(shape, dtype)

    outs = [
        (like(*heads, dtype=F32), vmem),
        (like(*heads, dtype=F32), vmem),
        (like(4, *block), hbm),
        (like(width, cols), vmem),
        (like(3, max(width, 2048), dtype=F32), vmem),
        (like(4, group, 2, *proj.shape), vmem),
        (like(line, *ff[0].shape), hbm),
        (like(4, group, *ff[1].shape), vmem),
        (like(3, *ff[2].shape[1:]), hbm),
        (like(4, *block), hbm),
        (like(per_dev, *heads), vmem),
        (like(*heads), vmem),
        (like(*heads), vmem),
        (like(seq_len, per_dev * HD), vmem),
        (like(per_dev, seq_len, 1, dtype=F32), vmem),
        (like(4, *block), hbm),
        (like(8, *block), hbm),
    ]
    copies = 10 * line + 40
    return pl.pallas_call(
        functools.partial(opening_kernel, (owned, vector_size, per_dev, group)),
        out_shape=[shape for shape, _ in outs],
        in_specs=[vmem] * 6 + [hbm] * 2 + [vmem] * 3,
        out_specs=[place for _, place in outs],
        scratch_shapes=[
            pltpu.VMEM((4, *block), LOW),
            pltpu.VMEM((4, *block), LOW),
            pltpu.VMEM((4, *block), LOW),
            pltpu.VMEM((8, *block), LOW),
            pltpu.VMEM((line, 2, *qkv.shape), LOW),
            pltpu.VMEM((line, 2, *proj.shape), LOW),
            pltpu.VMEM((line, *ff[1].shape), LOW),
            pltpu.VMEM((2, *heads), LOW),
            pltpu.SemaphoreType.DMA((copies,)),
            pltpu.SemaphoreType.DMA((copies,)),
            pltpu.SemaphoreType.DMA((line,)),
            pltpu.SemaphoreType.DMA((4 * group,)),
            pltpu.SemaphoreType.DMA((8,)),
        ],
        cost_estimate=pl.CostEstimate(
            flops=100_000_000_000, bytes_accessed=40_000_000, transcendentals=4_000_000
        ),
        compiler_params=pltpu.CompilerParams(
            collective_id=0, has_side_effects=True, vmem_limit_bytes=58 << 20
        ),
    )(tokens, cotangent, qkv, proj, *ff, inverse, *segments)


def middle_kernel(
    part, tokens, vectors, hidden, mids, arrived, summed, across_in, send_sems, recv_sems
):
    (me, sibling, across), ids = neighbours()
    far = across + 1 - 2 * (across % 2)
    width = tokens.shape[1]
    greet(ids)
    link = Sender(send_sems, recv_sems)
    first = link.send(part.at[far], arrived.at[0], ids[0])
    second = link.send(part.at[sibling], arrived.at[1], ids[0])
    first.wait_recv()
    summed[...] = (part[across].astype(F32) + arrived[0].astype(F32)).astype(LOW)
    third = link.send(summed, across_in, ids[1])
    second.wait_recv()
    hidden[...] = tokens[...].astype(F32) + (part[me].astype(F32) + arrived[1].astype(F32))
    third.wait_recv()
    total = hidden[...] + across_in[...].astype(F32)
    hidden[...] = total
    mids[0] = (total * inverse_rms(total) * vectors[1:2, :width]).astype(LOW)
    for _ in plane_gather(link, mids, ids):
        pass
    link.finish()


def middle(part, tokens, vectors):
    block = tokens.shape
    vmem = pl.BlockSpec(memory_space=pltpu.VMEM)
    return pl.pallas_call(
        middle_kernel,
        out_shape=[jax.ShapeDtypeStruct(block, F32), jax.ShapeDtypeStruct((8, *block), LOW)],
        in_specs=[vmem] * 3,
        out_specs=[vmem] * 2,
        scratch_shapes=[
            pltpu.VMEM((2, *block), LOW),
            pltpu.VMEM(block, LOW),
            pltpu.VMEM(block, LOW),
            pltpu.SemaphoreType.DMA((16,)),
            pltpu.SemaphoreType.DMA((16,)),
        ],
        compiler_params=pltpu.CompilerParams(
            collective_id=1, has_side_effects=True, vmem_limit_bytes=58 << 20
        ),
    )(part, tokens, vectors)


def cut_kernel(shape, *refs):
    follows, group, units = shape
    if follows:
        mids_in, cots_in, whole_in, out_before, mid_before, *refs = refs
    else:
        mids_in, cots_in, weight_in, rows_in, *refs = refs
    term, out, mid, mids, cots, weight, rows, down, act, grad, stage, *refs = refs
    before, ahead, load_sems, weight_sems, stage_sems, before_sems, send_sems, recv_sems = refs
    (me, sibling, across), ids = neighbours()
    far = across + 1 - 2 * (across % 2)
    others = (sibling, across, far)
    line, _, owned, cols = weight.shape
    count, block, width = mids.shape
    quarter = width // 4
    fold = quarter // owned
    greet((ids[0], ids[1], {"seq": far}))
    link = Sender(send_sems, recv_sems)

    def load(source, target, sem):
        copy = pltpu.make_async_copy(source, target, sem)
        copy.start()
        return copy

    if follows:
        sent = [
            link.send(whole_in.at[pl.ds(k * group, group), 2], rows.at[me], {"seq": k})
            for k in others
        ]
        loads = [load(whole_in.at[pl.ds(me * group, group), 2], rows.at[me], weight_sems.at[line])]
        loads += [
            load(whole_in.at[z, pl.ds(0, 2)], weight.at[z], weight_sems.at[z]) for z in range(line)
        ]
    else:
        sent = []
        loads = [load(rows_in, rows, weight_sems.at[line]), load(weight_in, weight, weight_sems.at[0])]
    for t in range(count):
        load(mids_in.at[t], mids.at[t], load_sems.at[0, t])
        load(cots_in.at[t], cots.at[t], load_sems.at[1, t])
    for copy in loads:
        copy.wait()

    def forward(t, carry):
        pltpu.make_async_copy(mids_in.at[t], mids.at[t], load_sems.at[0, t]).wait()
        ahead[t] = dot(mids[t], weight[...].reshape(width, cols))
        return carry

    early = ahead.shape[0]
    if follows:
        lax.fori_loop(0, early, forward, 0)
    for copy in sent:
        copy.wait_recv()
    for k in range(4):
        for member in range(group):
            for j in range(fold):
                first = k * quarter + j * owned
                down[first : first + owned, member * units : (member + 1) * units] = rows[
                    k, member, :, j * units : (j + 1) * units
                ]

    def tokens(first, t, carry):
        if first == 0 and follows:
            gate_up = ahead[t]
        else:
            pltpu.make_async_copy(mids_in.at[t], mids.at[t], load_sems.at[0, t]).wait()
            gate_up = dot(mids[t], weight[...].reshape(width, cols))
        pltpu.make_async_copy(cots_in.at[t], cots.at[t], load_sems.at[1, t]).wait()
        grad_act = dot(cots[t], down[...])
        gate, upward = gate_up[:, : cols // 2], gate_up[:, cols // 2 :]
        sigmoid_gate = jax.nn.sigmoid(gate)
        silu = gate * sigmoid_gate
        act[t] = (silu * upward).astype(LOW)
        grad[t, :, : cols // 2] = (
            grad_act * upward * sigmoid_gate * (1.0 + gate * (1.0 - sigmoid_gate))
        ).astype(LOW)
        grad[t, :, cols // 2 :] = (grad_act * silu).astype(LOW)
        return carry

    if follows:
        lax.fori_loop(0, early, functools.partial(tokens, 0), 0)
        lax.fori_loop(early, count, functools.partial(tokens, early), 0)
    else:
        lax.fori_loop(0, count, functools.partial(tokens, 0), 0)

    all_act = act[...].reshape(count * block, cols // 2)
    for k in range(4):
        value = column_product(
            cots[:, :, k * quarter : (k + 1) * quarter].reshape(count * block, quarter), all_act
        ).astype(LOW)
        for member in range(group):
            for j in range(fold):
                rows[k, member, :, j * units : (j + 1) * units] = value[
                    j * owned : (j + 1) * owned, member * units : (member + 1) * units
                ]
    sent = [
        link.send(rows.at[k], term.at[pl.ds(me * group, group), 2], {"seq": k}) for k in others
    ]
    term[pl.ds(me * group, group), 2] = rows[me]
    all_grad = grad[...].reshape(count * block, cols)
    for z in range(line):
        value = column_product(
            mids[:, :, 2 * owned * z : 2 * owned * (z + 1)].reshape(count * block, 2 * owned),
            all_grad,
        ).astype(LOW)
        for y in range(2):
            term[z, y] = value[y * owned : (y + 1) * owned, :]

    def ask(t, slot):
        for place, source in enumerate((out_before, mid_before)):
            load(source.at[t], before.at[slot, place], before_sems.at[slot, place])

    if follows:
        ask(0, 0)

    def back(t, carry):
        slot = t % 2

        def hand_over(t, place, target):
            return pltpu.make_async_copy(
                stage.at[t % 2, place], target.at[t], stage_sems.at[t % 2, place]
            )

        @pl.when(t >= 2)
        def _():
            hand_over(t - 2, 0, out).wait()
            hand_over(t - 2, 1, mid).wait()

        values = [
            times_transpose(act[t], down[...]),
            times_transpose(grad[t], weight[...].reshape(width, cols)),
        ]
        if follows:

            @pl.when(t + 1 < count)
            def _():
                ask(t + 1, (t + 1) % 2)

            for place, source in enumerate((out_before, mid_before)):
                pltpu.make_async_copy(
                    source.at[t], before.at[slot, place], before_sems.at[slot, place]
                ).wait()
                values[place] = values[place] + before[slot, place].astype(F32)
        for place, target in enumerate((out, mid)):
            stage[slot, place] = values[place].astype(LOW)
            hand_over(t, place, target).start()
        return carry

    lax.fori_loop(0, count, back, 0)
    for t in (count - 2, count - 1):
        for place, target in enumerate((out, mid)):
            pltpu.make_async_copy(
                stage.at[t % 2, place], target.at[t], stage_sems.at[t % 2, place]
            ).wait()
    for copy in sent:
        copy.wait_recv()
    link.finish()


def cut_call(follows, args, sizes):
    group, line, owned, units = sizes
    mids = args[0]
    count, block, width = mids.shape
    cols = 2 * group * units
    hbm, vmem = (pl.BlockSpec(memory_space=pl.ANY), pl.BlockSpec(memory_space=pltpu.VMEM))
    rows = (4, group, owned, cols)
    low_scratch = [
        mids.shape,
        mids.shape,
        (line, 2, owned, cols),
        rows,
        (width, cols // 2),
        (count, block, cols // 2),
        (count, block, cols),
        (2, 2, block, width),
        (2, 2, block, width),
    ]
    return pl.pallas_call(
        functools.partial(cut_kernel, (follows, group, units)),
        out_shape=[
            jax.ShapeDtypeStruct((line, 3, owned, cols), LOW),
            jax.ShapeDtypeStruct(mids.shape, LOW),
            jax.ShapeDtypeStruct(mids.shape, LOW),
        ],
        in_specs=[hbm] * len(args),
        out_specs=[vmem, hbm, hbm],
        scratch_shapes=[pltpu.VMEM(shape, LOW) for shape in low_scratch]
        + [
            pltpu.VMEM((count // 2 if follows else 1, block, cols), F32),
            pltpu.SemaphoreType.DMA((2, count)),
            pltpu.SemaphoreType.DMA((line + 1,)),
            pltpu.SemaphoreType.DMA((2, 2)),
            pltpu.SemaphoreType.DMA((2, 2)),
            pltpu.SemaphoreType.DMA((6,)),
            pltpu.SemaphoreType.DMA((6,)),
        ],
        compiler_params=pltpu.CompilerParams(
            collective_id=4 if follows else 3, has_side_effects=True, vmem_limit_bytes=58 << 20
        ),
        cost_estimate=pl.CostEstimate(
            flops=50_000_000_000, bytes_accessed=40_000_000, transcendentals=2_000_000
        ),
    )(*args)


def spread_blocks(link, ids, pair, ff_sum, hidden_blocks, down_blocks, local_sems):
    core, over_x, over_y = ids
    kept, down = ff_sum.at[pair], ff_sum.at[2]
    local = [
        pltpu.make_async_copy(kept, hidden_blocks.at[0], local_sems.at[0]),
        pltpu.make_async_copy(down, down_blocks.at[0], local_sems.at[1]),
    ]
    for copy in local:
        copy.start()
    to_x = [
        link.send(kept, hidden_blocks.at[2], over_x),
        link.send(down, down_blocks.at[2], over_x),
    ]
    last = [
        link.send(kept, hidden_blocks.at[1], core),
        link.send(down, down_blocks.at[1], core),
    ]
    yield
    over = link.send(ff_sum.at[1 - pair], hidden_blocks.at[4], over_y)
    yield
    over.wait_recv()
    far = link.send(hidden_blocks.at[4], hidden_blocks.at[6], over_x)
    last.append(link.send(hidden_blocks.at[4], hidden_blocks.at[5], core))
    for copy, blocks in zip(to_x, (hidden_blocks, down_blocks)):
        copy.wait_recv()
        last.append(link.send(blocks.at[2], blocks.at[3], core))
    yield
    far.wait_recv()
    last.append(link.send(hidden_blocks.at[6], hidden_blocks.at[7], core))
    yield
    for copy in last:
        copy.wait_recv()
    for copy in local:
        copy.wait()
    yield


def output_kernel(
    terms_in,
    hidden,
    ff_sum,
    _,
    block_out,
    hidden_blocks,
    down_blocks,
    terms,
    arrived,
    held,
    from_x,
    from_y,
    corner,
    send_sems,
    recv_sems,
    load_sems,
    local_sems,
):
    _, ids = neighbours()
    core, over_x, over_y = ids
    pair = lax.axis_index("fsdp") % 2
    greet(ids)
    link = Sender(send_sems, recv_sems)
    order = (7, 6, 5, 4, 3, 2, 1, 0)
    loads = {k: pltpu.make_async_copy(terms_in.at[k], terms.at[k], load_sems.at[k]) for k in order}
    for k in order:
        loads[k].start()
    spread = spread_blocks(link, ids, pair, ff_sum, hidden_blocks, down_blocks, local_sems)
    halved = {}
    for k in (6, 4, 2, 0):
        loads[k + 1].wait()
        halved[k] = link.send(terms.at[k + 1], arrived.at[k // 2], core)
    next(spread)

    def chip_sum(k):
        loads[k].wait()
        halved[k].wait_recv()
        return terms[k].astype(F32) + arrived[k // 2].astype(F32)

    held[0] = chip_sum(6).astype(LOW)
    turn = link.send(held.at[0], corner, over_y)
    next(spread)
    held[1] = chip_sum(4).astype(LOW)
    direct = link.send(held.at[1], from_y, over_y)
    total = chip_sum(2)
    turn.wait_recv()
    held[2] = (total + corner[...].astype(F32)).astype(LOW)
    last = link.send(held.at[2], from_x, over_x)
    next(spread)
    total = hidden[...] + chip_sum(0)
    direct.wait_recv()
    last.wait_recv()
    total = total + from_x[...].astype(F32) + from_y[...].astype(F32)
    block_out[...] = total.astype(LOW)
    next(spread)
    next(spread)
    link.finish()


def spread(ff_sum, terms, hidden, earlier):
    hbm, vmem = (pl.BlockSpec(memory_space=pl.ANY), pl.BlockSpec(memory_space=pltpu.VMEM))
    shapes = [jax.ShapeDtypeStruct((count, *ff_sum.shape[1:]), LOW) for count in (8, 4)]
    sems = [pltpu.SemaphoreType.DMA((18,))] * 2
    block = hidden.shape
    return pl.pallas_call(
        output_kernel,
        out_shape=[jax.ShapeDtypeStruct(block, LOW), *shapes],
        in_specs=[hbm, vmem, vmem, hbm],
        out_specs=[vmem, hbm, hbm],
        scratch_shapes=[
            pltpu.VMEM(shape, LOW)
            for shape in (terms.shape, (4, *block), (3, *block), block, block, block)
        ]
        + [*sems, pltpu.SemaphoreType.DMA((8,)), pltpu.SemaphoreType.DMA((2,))],
        compiler_params=pltpu.CompilerParams(
            collective_id=5, has_side_effects=True, vmem_limit_bytes=58 << 20
        ),
        cost_estimate=pl.CostEstimate(
            flops=50_000_000_000, bytes_accessed=20_000_000, transcendentals=0
        ),
    )(terms, hidden, ff_sum, earlier)


def closing_kernel(
    shape,
    terms_in,
    hidden,
    upstream,
    tokens_in,
    normed_in,
    vectors,
    weight,
    proj_mine,
    queries,
    keys,
    values,
    merged,
    logsum,
    cosines,
    sines,
    seg_col,
    seg_row,
    ff_sum,
    tokens_grad,
    gain_terms,
    attn_sum,
    hidden_blocks,
    down_blocks,
    mid_terms,
    tokens_all,
    normed,
    arrived,
    held,
    from_x,
    from_y,
    corner,
    upper,
    grad_heads,
    grad_queries,
    grad_keys,
    grad_values,
    kv,
    projected,
    proj_part,
    proj_in,
    proj_half,
    bias_row,
    qkv_part,
    qkv_in,
    late,
    late_x,
    send_sems,
    recv_sems,
    local_sems,
    load_sems,
):
    owned, per_dev, group = shape
    (me, sibling, across), (core, over_x, over_y) = neighbours()
    far = across + 1 - 2 * (across % 2)
    others = (sibling, across, far)
    pair = lax.axis_index("fsdp") % 2
    rows, width = hidden.shape
    seq_count = tokens_all.shape[0]
    quarter = width // seq_count
    low, high = (pl.ds(0, rows // 2), pl.ds(rows // 2, rows // 2))
    gains = (vectors[0:1, :width], vectors[1:2, :width])
    greet((core, over_x, {"seq": far}, over_y))
    link = Sender(send_sems, recv_sems)

    loads = {}
    for k in (7, 3, 5, 1, 6, 2, 4, 0):
        loads[k] = pltpu.make_async_copy(terms_in.at[k], mid_terms.at[k], load_sems.at[k])
        loads[k].start()
    kept_loads = [
        pltpu.make_async_copy(source, target, load_sems.at[8 + number])
        for number, (source, target) in enumerate(((tokens_in, tokens_all), (normed_in, normed)))
    ]
    for copy in kept_loads:
        copy.start()
    halved = {}
    for k in (6, 2, 4, 0):
        loads[k + 1].wait()
        halved[k] = link.send(mid_terms.at[k + 1], arrived.at[k // 2], core)

    def chip_sum(k):
        loads[k].wait()
        halved[k].wait_recv()
        return mid_terms[k].astype(F32) + arrived[k // 2].astype(F32)

    held[2] = chip_sum(6).astype(LOW)
    turn_y = link.send(held.at[2, low], corner.at[0], over_x)
    turn_x = link.send(held.at[2, high], corner.at[1], over_y)
    held[0] = chip_sum(2).astype(LOW)
    direct_x = link.send(held.at[0, low], from_x.at[low], over_x)
    held[1] = chip_sum(4).astype(LOW)
    direct_y = link.send(held.at[1, high], from_y.at[high], over_y)
    tokens_grad[...] = chip_sum(0)
    turn_x.wait_recv()
    held[0, high] = (held[0, high].astype(F32) + corner[1].astype(F32)).astype(LOW)
    second_x = link.send(held.at[0, high], from_x.at[high], over_x)
    turn_y.wait_recv()
    held[1, low] = (held[1, low].astype(F32) + corner[0].astype(F32)).astype(LOW)
    second_y = link.send(held.at[1, low], from_y.at[low], over_y)
    for copy in (direct_x, direct_y, second_x, second_y):
        copy.wait_recv()

    grad_mid = tokens_grad[...] + from_x[...].astype(F32) + from_y[...].astype(F32)
    through, term = norm_back(hidden[...], inverse_rms(hidden[...]), gains[1], grad_mid)
    gain_terms[1:2, :] = term[None]
    total = upstream[...].astype(F32) + through
    tokens_grad[...] = total
    upper[me] = total.astype(LOW)
    last = [link.send(upper.at[me], upper.at[me], core)]
    to_x = [link.send(upper.at[me, half], upper.at[me, half], over_x) for half in (low, high)]
    for copy, half in zip(to_x, (low, high)):
        copy.wait_recv()
        last.append(link.send(upper.at[across, half], upper.at[across, half], core))
    for copy in last:
        copy.wait_recv()

    head_rows = per_dev * HD
    for block in range(seq_count):
        grad_heads[block * rows : (block + 1) * rows, :] = sum(
            times_transpose(
                upper[block, :, k * quarter : (k + 1) * quarter],
                proj_mine[k].reshape(head_rows, quarter),
            )
            for k in range(seq_count)
        ).astype(LOW)
    for k in range(seq_count):
        term = sum(
            column_product(
                merged[block * rows : (block + 1) * rows, :],
                upper[block, :, k * quarter : (k + 1) * quarter],
            )
            for block in range(seq_count)
        ).astype(LOW)
        for member in range(group):
            for y in range(2):
                first = (2 * member + y) * owned
                proj_part[y, k, member] = term[first : first + owned, :]
    proj_over = link.send(proj_part.at[1 - pair], proj_in, over_y)
    spread = spread_blocks(
        link, (core, over_x, over_y), pair, ff_sum, hidden_blocks, down_blocks, local_sems
    )
    next(spread)
    next(spread)

    grad_keys[...] = jnp.zeros_like(grad_keys)
    grad_values[...] = jnp.zeros_like(grad_values)
    scale = HD ** (-0.5)
    for block in range(seq_count):
        here, last_key = pl.ds(block * rows, rows), (block + 1) * rows
        row_index = block * rows + lax.broadcasted_iota(jnp.int32, (rows, last_key), 0)
        key_index = lax.broadcasted_iota(jnp.int32, (rows, last_key), 1)
        allowed = (key_index <= row_index) & (seg_col[here, :] == seg_row[:, :last_key])
        for head in range(per_dev):
            query = queries[head, here, :]
            upper_head = grad_heads[here, head * HD : (head + 1) * HD]
            scores = times_transpose(query, keys[:last_key, :]) * scale
            probs = jnp.where(allowed, jnp.exp(scores - logsum[head, here, :]), 0.0)
            grad_probs = times_transpose(upper_head, values[:last_key, :])
            inner = jnp.sum(probs * grad_probs, axis=-1, keepdims=True)
            grad_scores = (probs * (grad_probs - inner)).astype(LOW)
            grad_queries[head, here, :] = (dot(grad_scores, keys[:last_key, :]) * scale).astype(LOW)
            grad_keys[:last_key, :] += column_product(grad_scores, query)
            grad_values[:last_key, :] += column_product(probs.astype(LOW), upper_head)
    next(spread)
    for copy in kept_loads:
        copy.wait()
    holds_values = me % 2 == 1
    key_copy = (grad_keys[...] * scale).astype(LOW)
    value_copy = grad_values[...].astype(LOW)
    kv[0] = jnp.where(holds_values, key_copy, value_copy)
    swapped = link.send(kv.at[0], kv.at[1], core)
    grad_keys[...] = jnp.where(holds_values, value_copy, key_copy).astype(F32)
    proj_over.wait_recv()
    proj_half[...] = (proj_part[pair].astype(F32) + proj_in[...].astype(F32)).astype(LOW)
    cols = weight.shape[1]

    def proj_place(device):
        return (pl.ds(device * group, group), pl.ds(0, owned), pl.ds(cols, quarter))

    last = [
        link.send(proj_half.at[k], attn_sum.at[proj_place(me)], {"seq": k}) for k in others
    ]
    attn_sum[proj_place(me)] = proj_half[me]
    swapped.wait_recv()
    grad_kv = grad_keys[...] + kv[1].astype(F32)

    bias_row[...] = jnp.zeros_like(bias_row)
    bias_parts = 0.0
    gain_terms[0:1, :] = jnp.zeros((1, width), F32)
    for block in range(seq_count):
        here = pl.ds(block * rows, rows)
        cosine, sine = cosines[here, :], sines[here, :]

        def rotate_back(head):
            return head * cosine - pltpu.roll(head, HD // 2, 1) * sine

        for head in range(per_dev):
            projected[here, head * HD : (head + 1) * HD] = rotate_back(
                grad_queries[head, here, :].astype(F32)
            ).astype(LOW)
        plain = grad_kv[block * rows : (block + 1) * rows, :]
        projected[here, head_rows:] = jnp.where(holds_values, plain, rotate_back(plain)).astype(LOW)
        grad_block = projected[here, :]
        bias_parts += jnp.sum(grad_block.astype(F32), axis=0, keepdims=True)
        grad_in = times_transpose(grad_block, weight[...])
        value = tokens_all[block].astype(F32)
        gain_terms[0:1, :] += jnp.sum(
            grad_in * value * inverse_rms(value), axis=0, keepdims=True
        )
        arrived[block] = grad_in.astype(LOW)
    first = link.send(arrived.at[far], late.at[0], core)
    second = link.send(arrived.at[sibling], late.at[1], core)
    first.wait_recv()
    link.release(direct_x, second_x)
    held[0] = (arrived[across].astype(F32) + late[0].astype(F32)).astype(LOW)
    third = link.send(held.at[0], late_x, over_x)
    kv_first = (H + KV * (me % 2) + me // 2) * HD
    bias_row[0:1, pl.ds(pl.multiple_of(me * head_rows, HD), head_rows)] = bias_parts[:, :head_rows]
    bias_row[0:1, pl.ds(pl.multiple_of(kv_first, HD), HD)] = bias_parts[:, head_rows:]
    line = qkv_in.shape[0]
    owned_bias = bias_row.shape[1] // (2 * line)
    qkv_part[:, :, owned:, :] = jnp.zeros_like(qkv_part[:, :, owned:, :])
    for z in range(line):
        for y in range(2):
            owner, at = 2 * z + y, 0
            for source, row, length in (
                (gain_terms, 0, owned),
                (gain_terms, 1, owned),
                (bias_row, 0, owned_bias),
            ):
                done = 0
                while done < length:
                    span = min(length - done, cols - at % cols)
                    first_col = owner * length + done
                    qkv_part[
                        y, z, owned + at // cols : owned + at // cols + 1, at % cols : at % cols + span
                    ] = source[row : row + 1, first_col : first_col + span].astype(LOW)
                    done, at = done + span, at + span
    for z in range(line):
        term = sum(
            column_product(
                normed[block, :, 2 * owned * z : 2 * owned * (z + 1)],
                projected[block * rows : (block + 1) * rows, :],
            )
            for block in range(seq_count)
        ).astype(LOW)
        for y in range(2):
            qkv_part[y, z, :owned, :] = term[y * owned : (y + 1) * owned, :]
    qkv_over = link.send(qkv_part.at[1 - pair], qkv_in, over_y)
    next(spread)
    second.wait_recv()
    third.wait_recv()
    grad_in = arrived[me].astype(F32) + late[1].astype(F32) + late_x[...].astype(F32)
    value = tokens_all[me].astype(F32)
    through, _ = norm_back(value, inverse_rms(value), gains[0], grad_in)
    tokens_grad[...] += through
    qkv_over.wait_recv()
    attn_sum[:, :, :cols] = (qkv_part[pair].astype(F32) + qkv_in[...].astype(F32)).astype(LOW)
    attn_sum[:, owned:, cols:] = jnp.zeros_like(attn_sum[:, owned:, cols:])
    for copy in last:
        copy.wait_recv()
    next(spread)
    link.finish()


def closing(args, sizes):
    owned, vector_rows, bias_cols, per_dev, group, line = sizes
    hidden, weight, proj_mine = args[1], args[6], args[7]
    rows, width = hidden.shape
    block = (rows, width)
    cols = weight.shape[1]
    quarter = proj_mine.shape[-1]
    heads = (4 * rows, HD)
    rows_in = (4, group, owned, quarter)
    outs = [
        jax.ShapeDtypeStruct(block, F32),
        jax.ShapeDtypeStruct((2, width), F32),
        jax.ShapeDtypeStruct((line, owned + vector_rows, cols + quarter), LOW),
        jax.ShapeDtypeStruct((8, *args[-1].shape[1:]), LOW),
        jax.ShapeDtypeStruct((4, *args[-1].shape[1:]), LOW),
    ]
    low_scratch = [
        (8, *block),
        (4, *block),
        (4, *block),
        (4, *block),
        (3, *block),
        block,
        block,
        (2, rows // 2, width),
        (4, *block),
        (4 * rows, per_dev * HD),
        (per_dev, *heads),
    ]
    return pl.pallas_call(
        functools.partial(closing_kernel, (owned, per_dev, group)),
        out_shape=outs,
        in_specs=[
            pl.BlockSpec(memory_space=pl.ANY if k in (0, 3, 4) else pltpu.VMEM)
            for k in range(len(args))
        ],
        out_specs=[pl.BlockSpec(memory_space=pltpu.VMEM)] * (len(outs) - 2)
        + [pl.BlockSpec(memory_space=pl.ANY)] * 2,
        scratch_shapes=[pltpu.VMEM(shape, LOW) for shape in low_scratch]
        + [pltpu.VMEM(heads, F32)] * 2
        + [
            pltpu.VMEM(shape, LOW)
            for shape in (
                (2, *heads),
                (4 * rows, cols),
                (2, *rows_in),
                rows_in,
                rows_in,
            )
        ]
        + [pltpu.VMEM((1, bias_cols), F32)]
        + [
            pltpu.VMEM(shape, LOW)
            for shape in (
                (2, line, owned + vector_rows, cols),
                (line, owned + vector_rows, cols),
                (2, *block),
                block,
            )
        ]
        + [pltpu.SemaphoreType.DMA((48,))] * 2
        + [pltpu.SemaphoreType.DMA((2,)), pltpu.SemaphoreType.DMA((10,))],
        compiler_params=pltpu.CompilerParams(
            collective_id=2, has_side_effects=True, vmem_limit_bytes=58 << 20
        ),
        cost_estimate=pl.CostEstimate(
            flops=100_000_000_000, bytes_accessed=40_000_000, transcendentals=4_000_000
        ),
    )(*args)


def columns_kernel(place, *refs):
    *pieces, out = refs
    row = 0
    for piece in pieces:
        count, rows, quarter = piece.shape
        for k in range(count):
            here = place[0] + k - 2 * ((place[0] % 2) * (k % 2)) - 4 * (
                (place[0] // 2 % 2) * (k // 2 % 2)
            )
            out[pl.ds(row, rows), pl.ds(k * quarter, quarter)] = piece[here].astype(F32)
        row += rows


def columns_call(place, pieces):
    rows = sum(piece.shape[1] for piece in pieces)
    width = pieces[0].shape[0] * pieces[0].shape[2]
    return pl.pallas_call(
        columns_kernel,
        out_shape=jax.ShapeDtypeStruct((rows, width), F32),
        in_specs=[pl.BlockSpec(memory_space=pltpu.SMEM)]
        + [pl.BlockSpec(memory_space=pltpu.VMEM)] * len(pieces),
        out_specs=pl.BlockSpec(memory_space=pltpu.VMEM),
        compiler_params=pltpu.CompilerParams(vmem_limit_bytes=40 << 20),
    )(place, *pieces)


def down_kernel(fold, place, *refs):
    *pieces, out = refs
    row = 0
    for piece in pieces:
        count, owned, width = piece.shape
        span = width // fold
        for k in range(count):
            here = place[0] + k - 2 * ((place[0] % 2) * (k % 2)) - 4 * (
                (place[0] // 2 % 2) * (k // 2 % 2)
            )
            whole = piece[here].astype(F32)
            for j in range(fold):
                whole_part = whole[:, j * span : (j + 1) * span]
                out[pl.ds(row, span), pl.ds((k * fold + j) * owned, owned)] = whole_part.T
        row += span


def down_call(place, pieces, fold):
    rows = sum(piece.shape[2] // fold for piece in pieces)
    width = pieces[0].shape[0] * pieces[0].shape[1] * fold
    return pl.pallas_call(
        functools.partial(down_kernel, fold),
        out_shape=jax.ShapeDtypeStruct((rows, width), F32),
        in_specs=[pl.BlockSpec(memory_space=pltpu.SMEM)]
        + [pl.BlockSpec(memory_space=pltpu.VMEM)] * len(pieces),
        out_specs=pl.BlockSpec(memory_space=pltpu.VMEM),
        compiler_params=pltpu.CompilerParams(vmem_limit_bytes=40 << 20),
    )(place, *pieces)


def hidden_kernel(cuts, group, place, *refs):
    *pieces, out = refs
    units = cuts[-1][1]
    count = pieces[0].shape[0] // 2
    for k in range(count):
        here = place[0] + k - 2 * ((place[0] % 2) * (k % 2)) - 4 * (
            (place[0] // 2 % 2) * (k // 2 % 2)
        )
        for pair in range(2):
            entry = (pair + place[1] - 2 * pair * place[1]) * count + here
            for part in range(2):
                for member in range(group):
                    first = (((part * count + k) * group + member) * 2 + pair) * units
                    for piece, (low, high) in zip(pieces, cuts):
                        span = high - low
                        at = (part * group + member) * span
                        out[:, first + low : first + high] = piece[entry][
                            :, at : at + span
                        ].astype(F32)


def hidden_call(place, pieces, cuts, group):
    rows = pieces[0].shape[1]
    units = cuts[-1][1]
    width = 2 * 8 * group * units
    step = 16
    return pl.pallas_call(
        functools.partial(hidden_kernel, cuts, group),
        grid=(rows // step,),
        out_shape=jax.ShapeDtypeStruct((rows, width), F32),
        in_specs=[pl.BlockSpec(memory_space=pltpu.SMEM)]
        + [pl.BlockSpec((8, step, piece.shape[2]), lambda i: (0, i, 0)) for piece in pieces],
        out_specs=pl.BlockSpec((step, width), lambda i: (i, 0)),
        compiler_params=pltpu.CompilerParams(vmem_limit_bytes=40 << 20),
    )(place, *pieces)


def local(
    tokens,
    segment_ids,
    attn_gain,
    qkv_weight,
    qkv_bias,
    proj_weight,
    mlp_gain,
    gate_up_weight,
    down_weight,
    cotangent,
):
    seq_count = lax.axis_size("seq")
    fsdp_count = lax.axis_size("fsdp")
    line = fsdp_count // 2
    place = lax.axis_index("seq")
    odd = lax.axis_index("fsdp") % 2 == 1
    tok_rows, width = tokens.shape[1:]
    seq_len = tok_rows * seq_count
    owned = qkv_weight.shape[0]
    owned_hidden = down_weight.shape[0]
    hidden = owned_hidden * fsdp_count
    quarter = width // seq_count
    per_dev = H // seq_count
    head_cols = per_dev * HD
    score_scale = HD ** (-0.5)
    group = line // seq_count
    cut_at = owned_hidden // 2 // 128 * 128
    cuts = [(0, cut_at), (cut_at, owned_hidden)]

    holds_values = place % 2 == 1
    kv_first = (H + KV * (place % 2) + place // 2) * HD
    qkv_own = jnp.concatenate(
        [
            lax.dynamic_slice_in_dim(qkv_weight, place * head_cols, head_cols, 1),
            lax.dynamic_slice_in_dim(qkv_weight, kv_first, HD, 1),
        ],
        axis=1,
    )
    cols = head_cols + HD
    vector = jnp.concatenate([attn_gain, mlp_gain, qkv_bias])
    vector_size = vector.shape[0]
    vector_rows = -(-vector_size // (16 * cols)) * 16
    vector = jnp.pad(vector, (0, vector_rows * cols - vector_size)).reshape(vector_rows, cols)
    proj_cols = lax.dynamic_slice_in_dim(proj_weight, place * quarter, quarter, 1)
    down_cols = lax.dynamic_slice_in_dim(down_weight, place * quarter, quarter, 1)
    fold = quarter // owned

    def folded(value):
        return jnp.concatenate(
            [value[..., j * owned : (j + 1) * owned, :] for j in range(fold)], axis=-1
        )

    def ff_columns(low, high, pair):
        return jnp.concatenate(
            [
                lax.dynamic_slice_in_dim(
                    gate_up_weight,
                    first + ((place * group + member) * 2 + pair) * owned_hidden + low,
                    high - low,
                    1,
                )
                for first in (0, hidden)
                for member in range(group)
            ],
            axis=1,
        )

    ff_sent = []
    for low, high in cuts:
        by_owner = [ff_columns(low, high, pair) for pair in range(2)]
        ff_sent.append((by_owner, folded(jnp.transpose(down_cols[low:high]))))
    segment_row = segment_ids[0]
    inverse = THETA ** (-2.0 * jnp.arange(HD // 2, dtype=F32) / HD)
    inverse = jnp.concatenate([inverse, inverse])[None]

    (
        cosines,
        sines,
        tokens_all,
        qkv_mine,
        vectors,
        proj_mine,
        first_all,
        first_rows,
        second_sent,
        normed_in,
        queries,
        head_keys,
        head_values,
        merged,
        logsum,
        attended,
        cots,
    ) = opening(
        tokens[0],
        cotangent[0],
        jnp.concatenate([qkv_own, vector], axis=0),
        lax.dynamic_slice_in_dim(proj_weight, place * quarter, quarter, 1),
        [part for by_owner, rows in ff_sent for part in (jnp.stack(by_owner), rows)],
        inverse,
        (segment_row[:, None], segment_row[None]),
        (owned, vector_size, per_dev, group, line),
    )
    second_all = line_gather(second_sent)
    hidden_in, mids = middle(attended, tokens[0], vectors)

    spans = [high - low for low, high in cuts]
    first_term, out_first, mid_first = cut_call(
        False, (mids, cots, first_all, first_rows), (group, line, owned, spans[0])
    )
    second_term, out, grad_mid = cut_call(
        True, (mids, cots, second_all, out_first, mid_first), (group, line, owned, spans[1])
    )

    sums = [line_reduce(term) for term in (first_term, second_term)]

    tokens_grad, gain_terms, attn_term, *first_blocks = closing(
        (
            grad_mid,
            hidden_in,
            cotangent[0],
            tokens_all,
            normed_in,
            vectors,
            qkv_mine,
            proj_mine,
            queries,
            head_keys,
            head_values,
            merged,
            logsum,
            cosines,
            sines,
            segment_row[:, None],
            segment_row[None],
            sums[0],
        ),
        (owned, vector_rows, qkv_weight.shape[1], per_dev, group, line),
    )
    places_here = jnp.stack([place, lax.axis_index("fsdp") % 2]).astype(jnp.int32)
    attn_term = attn_term + nought(sums[1][0, 0, 0])
    attn_sum = line_reduce(attn_term)
    block_out, *second_blocks = spread(sums[1], out, hidden_in, attn_term)
    hidden_pieces = [first_blocks[0], second_blocks[0]]
    down_pieces = [first_blocks[1], second_blocks[1]]
    down_grad = down_call(places_here, down_pieces, fold)
    gate_up_grad = hidden_call(places_here, hidden_pieces, cuts, group)
    attn_sums = seq_blocks(attn_sum + nought(block_out[0, 0]))
    proj_grad = columns_call(
        places_here, [jnp.stack([part[:owned, cols:] for part in attn_sums])]
    )
    qkv_sums = in_order([part[:, :cols] for part in attn_sums])
    qkv_grad = jnp.concatenate(
        [part[:owned, :head_cols] for part in qkv_sums]
        + [part[:owned, head_cols:] for part in qkv_sums[0::2]]
        + [part[:owned, head_cols:] for part in qkv_sums[1::2]],
        axis=-1,
    ).astype(F32)
    vector_sum = sum(part[owned:].astype(F32) for part in qkv_sums).reshape(-1)
    return (
        block_out[None],
        tokens_grad[None],
        vector_sum[:owned],
        qkv_grad,
        vector_sum[2 * owned : vector_size],
        proj_grad,
        vector_sum[owned : 2 * owned],
        gate_up_grad,
        down_grad,
    )


def solution(mesh):
    in_specs = (
        P("fsdp", "seq", None),
        P("fsdp", None),
        P("fsdp"),
        P("fsdp", None),
        P("fsdp"),
        P("fsdp", None),
        P("fsdp"),
        P("fsdp", None),
        P("fsdp", None),
        P("fsdp", "seq", None),
    )
    out_specs = (
        P("fsdp", "seq", None),
        P("fsdp", "seq", None),
        P("fsdp"),
        P("fsdp", None),
        P("fsdp"),
        P("fsdp", None),
        P("fsdp"),
        P("fsdp", None),
        P("fsdp", None),
    )
    return jax.shard_map(local, mesh=mesh, in_specs=in_specs, out_specs=out_specs, check_vma=False)
```

```python
import functools

import jax
import jax.numpy as jnp
from jax import lax
from jax.experimental import pallas as pl
from jax.experimental.pallas import tpu as pltpu
from jax.sharding import PartitionSpec as P

H = 12
KV = 2
HD = 128
EPSILON = 1e-06
THETA = 1000000.0
FLOOR = -1e30
LOW = jnp.bfloat16
F32 = jnp.float32


def inverse_rms(value):
    return lax.rsqrt(jnp.mean(value * value, axis=-1, keepdims=True) + EPSILON)


def turned(value):
    halfway = value.shape[-1] // 2
    return jnp.concatenate([-value[..., halfway:], value[..., :halfway]], axis=-1)


def turned_back(value):
    halfway = value.shape[-1] // 2
    return jnp.concatenate([value[..., halfway:], -value[..., :halfway]], axis=-1)


def norm_back(value, factor, gain, upstream):
    weighted = upstream * gain
    gain_term = jnp.sum(upstream * value * factor, axis=0)
    through = factor * weighted - value * factor**3 * jnp.mean(
        weighted * value, axis=-1, keepdims=True
    )
    return (through, gain_term)


def dot(left, right):
    return jnp.dot(left, right, preferred_element_type=F32)


def column_product(left, right):
    return lax.dot_general(left, right, (((0,), (0,)), ((), ())), preferred_element_type=F32)


def times_transpose(left, right):
    return lax.dot_general(left, right, (((1,), (1,)), ((), ())), preferred_element_type=F32)


def swap(value, axis, distance):
    return lax.ppermute(value, axis, [(i, i ^ distance) for i in range(lax.axis_size(axis))])


def lines():
    size = lax.axis_size("fsdp")
    return [list(range(first, size, 2)) for first in range(2)]


def line_gather(value):
    return lax.all_gather(value, "fsdp", axis=0, axis_index_groups=lines(), tiled=False)


def line_reduce(value):
    return lax.psum_scatter(
        value, "fsdp", scatter_dimension=0, axis_index_groups=lines(), tiled=False
    )


def by_pair(own, other):
    second = lax.axis_index("fsdp") % 2 == 1
    return (jnp.where(second, other, own), jnp.where(second, own, other))


def pick(flag, first, second):
    return (jnp.where(flag, second, first), jnp.where(flag, first, second))


def nought(value):
    return jnp.minimum(jnp.abs(value), 0.0).astype(LOW)


def seq_blocks(value):
    across = swap(value, "seq", 2)
    return [value, swap(value, "seq", 1), across, swap(across, "seq", 1)]


def seq_reduce(parts):
    arrived = swap(jnp.stack([parts[1], parts[3]]), "seq", 1)
    across = (parts[2].astype(F32) + arrived[1].astype(F32)).astype(LOW)
    here = parts[0].astype(F32) + arrived[0].astype(F32)
    return here + swap(across, "seq", 2).astype(F32)


def in_order(blocks):
    me = lax.axis_index("seq")
    bits = 1
    while bits < len(blocks):
        flip = (me & bits) != 0
        blocks = [jnp.where(flip, blocks[k ^ bits], blocks[k]) for k in range(len(blocks))]
        bits *= 2
    return blocks


def relative(value):
    size = lax.axis_size("seq")
    me = lax.axis_index("seq")
    cut = value.reshape(size, value.shape[0] // size, *value.shape[1:])
    return [lax.dynamic_index_in_dim(cut, me ^ k, 0, keepdims=False) for k in range(size)]


def seq_exchange(pieces):
    taken = [part[0] for part in relative(pieces)]
    return in_order([taken[0]] + [swap(taken[k], "seq", k) for k in range(1, len(taken))])


MESH = pl.DeviceIdType.MESH


def neighbours():
    me, owner = lax.axis_index("seq"), lax.axis_index("fsdp")
    sibling = me + 1 - 2 * (me % 2)
    across = me + 2 - 4 * (me // 2 % 2)
    partner = owner + 1 - 2 * (owner % 2)
    return (me, sibling, across), ({"seq": sibling}, {"seq": across}, {"fsdp": partner})


def greet(devices):
    barrier = pltpu.get_barrier_semaphore()
    for device in devices:
        pl.semaphore_signal(barrier, inc=1, device_id=device, device_id_type=MESH)
    pl.semaphore_wait(barrier, len(devices))


class Sender:
    def __init__(self, send_sems, recv_sems):
        self.sems = (send_sems, recv_sems)
        self.count, self.open = 0, []

    def send(self, source, target, device):
        number = self.count
        copy = pltpu.make_async_remote_copy(
            src_ref=source,
            dst_ref=target,
            send_sem=self.sems[0].at[number],
            recv_sem=self.sems[1].at[number],
            device_id=device,
            device_id_type=MESH,
        )
        copy.start()
        self.count += 1
        self.open.append(copy)
        return copy

    def release(self, *copies):
        for copy in copies:
            copy.wait_send()
            self.open = [other for other in self.open if other is not copy]

    def finish(self):
        self.release(*self.open)


def plane_gather(link, blocks, ids):
    core, over_x, over_y = ids
    rows = blocks.shape[1]
    halves = (pl.ds(0, rows // 2), pl.ds(rows // 2, rows // 2))
    to_x = [link.send(blocks.at[0, half], blocks.at[2, half], over_x) for half in halves]
    last = [link.send(blocks.at[0], blocks.at[1], core)]
    yield
    to_y = [link.send(blocks.at[0, half], blocks.at[4, half], over_y) for half in halves[::-1]]
    yield
    to_x[0].wait_recv()
    diagonal = [link.send(blocks.at[2, halves[0]], blocks.at[6, halves[0]], over_y)]
    last.append(link.send(blocks.at[2, halves[0]], blocks.at[3, halves[0]], core))
    to_y[0].wait_recv()
    diagonal.append(link.send(blocks.at[4, halves[1]], blocks.at[6, halves[1]], over_x))
    last.append(link.send(blocks.at[4, halves[1]], blocks.at[5, halves[1]], core))
    to_x[1].wait_recv()
    last.append(link.send(blocks.at[2, halves[1]], blocks.at[3, halves[1]], core))
    to_y[1].wait_recv()
    last.append(link.send(blocks.at[4, halves[0]], blocks.at[5, halves[0]], core))
    for copy, half in zip(diagonal, halves):
        copy.wait_recv()
        last.append(link.send(blocks.at[6, half], blocks.at[7, half], core))
    for copy in last:
        copy.wait_recv()
    yield


def opening_kernel(
    shape,
    tokens,
    cotangent,
    qkv,
    proj,
    ff_own,
    ff_down,
    second_own,
    second_down,
    inverse,
    seg_col,
    seg_row,
    cosines,
    sines,
    tokens_out,
    weight,
    vectors,
    proj_mine,
    ff_all,
    ff_rows,
    second_out,
    normed_out,
    queries,
    keys,
    values,
    merged,
    logsum,
    part_out,
    cots_out,
    tokens_all,
    normed,
    part,
    cots,
    qkv_all,
    proj_all,
    ff_line,
    kv,
    send_sems,
    recv_sems,
    hand_send,
    hand_recv,
    local_sem,
):
    owned, vector_size, per_dev, group = shape
    (me, sibling, across), ids = neighbours()
    core, over_x, over_y = ids
    far = across + 1 - 2 * (across % 2)
    line = qkv_all.shape[0]
    size = 2 * line
    owner = lax.axis_index("fsdp")
    at, pair = owner // 2, owner % 2
    below, above = ({"fsdp": (owner + size - 2) % size}, {"fsdp": (owner + 2) % size})
    rows, width = tokens.shape
    seq_count = tokens_all.shape[0]
    seq_len = seq_count * rows
    halves = (pl.ds(0, rows // 2), pl.ds(rows // 2, rows // 2))
    others = (sibling, across, far)
    greet((*ids, {"seq": far}, below, above))
    link = Sender(send_sems, recv_sems)

    own_copy = pltpu.make_async_copy(ff_own.at[pair], ff_all.at[at, pair], local_sem.at[0])
    own_copy.start()
    leaving = [own_copy]

    def leave(source, target):
        copy = pltpu.make_async_copy(source, target, local_sem.at[len(leaving)])
        copy.start()
        leaving.append(copy)

    leave(second_own.at[pair], second_out.at[pair])
    leave(second_down, second_out.at[2])
    ff_line[at] = ff_down[...]
    tokens_all[me] = tokens[...]
    qkv_all[at, pair] = qkv[...]
    proj_all[at, pair] = proj[...]

    turned, handed = [], []

    def hand_on(k):
        z = (at + k) % line
        target, member = z // group, z % group
        copy = pltpu.make_async_remote_copy(
            src_ref=ff_line.at[z],
            dst_ref=ff_rows.at[me, member],
            send_sem=hand_send.at[k],
            recv_sem=hand_recv.at[me * group + member],
            device_id={"seq": target},
            device_id_type=MESH,
        )

        @pl.when(target != me)
        def _():
            copy.start()

        @pl.when(target == me)
        def _():
            ff_rows[me, member] = ff_line[z]

        handed.append((copy, target))

    def ring_steps():
        before = [None] * 3
        for k in range(line):
            z = (at + k) % line
            here = (ff_line.at[z], ff_all.at[z, pair], ff_all.at[z, 1 - pair])
            for place, target in enumerate(here):
                source = ff_own.at[pair] if k == 0 and place == 1 else target
                if k > 0:
                    before[place].wait_recv()
                elif place == 2:
                    turned[0].wait_recv()
                if k < line - 1:
                    before[place] = link.send(source, target, below)
                if place == 0:
                    hand_on(k)
                yield

    ring = ring_steps()

    def pump(count):
        for _ in range(count):
            next(ring, None)

    def along_line(array, k):
        here = array.at[(at + k) % line, pair]
        return link.send(here, here, below)

    def to_partner(array, k):
        here = array.at[(at + k) % line, pair]
        return link.send(here, here, over_y)

    onward = along_line(qkv_all, 0)
    last = [to_partner(qkv_all, 0)]
    to_x = [link.send(tokens_all.at[me, half], tokens_all.at[me, half], over_x) for half in halves]
    last.append(link.send(tokens_all.at[me], tokens_all.at[me], core))
    proj_onward = along_line(proj_all, 0)

    lanes = lax.broadcasted_iota(jnp.int32, (rows, HD), 1)
    for block in range(seq_count):
        here = pl.ds(block * rows, rows)
        before = jnp.sum((seg_row[...] < seg_col[here, :]).astype(F32), axis=1, keepdims=True)
        index = (block * rows + lax.broadcasted_iota(jnp.int32, (rows, 1), 0)).astype(F32)
        angles = (index - before) * inverse[...]
        cosines[here, :] = jnp.cos(angles)
        sines[here, :] = jnp.where(lanes < HD // 2, -jnp.sin(angles), jnp.sin(angles))
    for k in range(1, line):
        onward.wait_recv()
        if k < line - 1:
            onward = along_line(qkv_all, k)
        last.append(to_partner(qkv_all, k))
        proj_onward.wait_recv()
        if k < line - 1:
            proj_onward = along_line(proj_all, k)
        if k == line - 2:
            pump(2)
    turned.append(link.send(ff_own.at[1 - pair], ff_all.at[at, pair], over_y))
    for copy, half in zip(to_x, halves):
        copy.wait_recv()
        last.append(link.send(tokens_all.at[across, half], tokens_all.at[across, half], core))
    for copy in last:
        copy.wait_recv()
    proj_over = [to_partner(proj_all, k) for k in range(line)]
    second_over = link.send(second_own.at[1 - pair], second_out.at[pair], over_y)
    leave(tokens_all, tokens_out)
    cots[0] = cotangent[...]
    gather_cots = plane_gather(link, cots, ids)
    next(gather_cots)

    for z in range(line):
        for y in range(2):
            owner_row = 2 * z + y
            weight[pl.ds(owner_row * owned, owned), :] = qkv_all[z, y, :owned, :]
            done = 0
            cols = qkv_all.shape[3]
            for start, count, target in (
                (0, owned, 0),
                (owned, owned, 1),
                (2 * owned, vector_size - 2 * owned, 2),
            ):
                while count > 0:
                    row, col = start // cols, start % cols
                    span = min(count, cols - col)
                    length = (owned, owned, vector_size - 2 * owned)[target]
                    to = owner_row * length + (length - count)
                    vectors[target : target + 1, to : to + span] = qkv_all[
                        z, y, owned + row : owned + row + 1, col : col + span
                    ].astype(F32)
                    start, count = start + span, count - span

    head_cols = per_dev * HD
    holds_values = me % 2 == 1
    kv_first = (H + KV * (me % 2) + me // 2) * HD
    bias = jnp.concatenate(
        [
            vectors[2:3, pl.ds(pl.multiple_of(me * head_cols, HD), head_cols)],
            vectors[2:3, pl.ds(pl.multiple_of(kv_first, HD), HD)],
        ],
        axis=1,
    )
    for block in range(seq_count):
        here = pl.ds(block * rows, rows)
        value = tokens_all[block].astype(F32)
        normal = (value * inverse_rms(value) * vectors[0:1, :width]).astype(LOW)
        normed[block] = normal
        projected = dot(normal, weight[...]) + bias
        cosine, sine = cosines[here, :], sines[here, :]

        def rotate(head):
            return head * cosine + pltpu.roll(head, HD // 2, 1) * sine

        for head in range(per_dev):
            queries[head, here, :] = rotate(projected[:, head * HD : (head + 1) * HD]).astype(LOW)
        plain = projected[:, head_cols:]
        kv[0, here, :] = jnp.where(holds_values, plain, rotate(plain)).astype(LOW)
    swapped = link.send(kv.at[0], kv.at[1], core)
    leave(normed, normed_out)
    pump(3)
    swapped.wait_recv()
    keys[...] = jnp.where(holds_values, kv[1], kv[0])
    values[...] = jnp.where(holds_values, kv[0], kv[1])

    for copy in proj_over:
        copy.wait_recv()
    exchange = [
        link.send(proj_all.at[pl.ds(target * group, group)], proj_mine.at[me], {"seq": target})
        for target in others
    ]
    next(gather_cots)
    proj_mine[me] = proj_all[pl.ds(me * group, group)]

    for block in range(seq_count):
        here, last_key = pl.ds(block * rows, rows), (block + 1) * rows
        row_index = block * rows + lax.broadcasted_iota(jnp.int32, (rows, last_key), 0)
        key_index = lax.broadcasted_iota(jnp.int32, (rows, last_key), 1)
        allowed = (key_index <= row_index) & (seg_col[here, :] == seg_row[:, :last_key])
        for head in range(per_dev):
            scores = times_transpose(queries[head, here, :], keys[:last_key, :]) * HD ** (-0.5)
            scores = jnp.where(allowed, scores, FLOOR)
            highest = jnp.max(scores, axis=-1, keepdims=True)
            exponent = jnp.exp(scores - highest)
            total = jnp.sum(exponent, axis=-1, keepdims=True)
            mixture = dot((exponent / total).astype(LOW), values[:last_key, :])
            merged[here, head * HD : (head + 1) * HD] = mixture.astype(LOW)
            logsum[head, here, :] = highest + jnp.log(total)
    pump(2)
    for copy in exchange:
        copy.wait_recv()
    quarter = proj.shape[1]
    for block in range(seq_count):
        for k in range(seq_count):
            columns = proj_mine[k].reshape(-1, quarter)
            part[block, :, k * quarter : (k + 1) * quarter] = dot(
                merged[block * rows : (block + 1) * rows, :], columns
            ).astype(LOW)

    leave(part, part_out)
    pump(1)
    next(gather_cots)
    leave(cots, cots_out)
    pump(3 * line)
    for copy in leaving:
        copy.wait()
    second_over.wait_recv()
    for source in others:
        for member in range(group):
            pltpu.make_async_remote_copy(
                src_ref=ff_line.at[0],
                dst_ref=ff_rows.at[source, member],
                send_sem=hand_send.at[0],
                recv_sem=hand_recv.at[source * group + member],
                device_id=core,
                device_id_type=MESH,
            ).wait_recv()
    for copy, target in handed:

        @pl.when(target != me)
        def _():
            copy.wait_send()

    link.finish()


def opening(tokens, cotangent, qkv, proj, ff, inverse, segments, sizes):
    owned, vector_size, per_dev, group, line = sizes
    rows, width = tokens.shape
    block = (rows, width)
    seq_len = 4 * rows
    cols = qkv.shape[1]
    heads = (seq_len, HD)
    vmem, hbm = (pl.BlockSpec(memory_space=pltpu.VMEM), pl.BlockSpec(memory_space=pl.ANY))

    def like(*shape, dtype=LOW):
        return jax.ShapeDtypeStruct(shape, dtype)

    outs = [
        (like(*heads, dtype=F32), vmem),
        (like(*heads, dtype=F32), vmem),
        (like(4, *block), hbm),
        (like(width, cols), vmem),
        (like(3, max(width, 2048), dtype=F32), vmem),
        (like(4, group, 2, *proj.shape), vmem),
        (like(line, *ff[0].shape), hbm),
        (like(4, group, *ff[1].shape), vmem),
        (like(3, *ff[2].shape[1:]), hbm),
        (like(4, *block), hbm),
        (like(per_dev, *heads), vmem),
        (like(*heads), vmem),
        (like(*heads), vmem),
        (like(seq_len, per_dev * HD), vmem),
        (like(per_dev, seq_len, 1, dtype=F32), vmem),
        (like(4, *block), hbm),
        (like(8, *block), hbm),
    ]
    copies = 10 * line + 40
    return pl.pallas_call(
        functools.partial(opening_kernel, (owned, vector_size, per_dev, group)),
        out_shape=[shape for shape, _ in outs],
        in_specs=[vmem] * 6 + [hbm] * 2 + [vmem] * 3,
        out_specs=[place for _, place in outs],
        scratch_shapes=[
            pltpu.VMEM((4, *block), LOW),
            pltpu.VMEM((4, *block), LOW),
            pltpu.VMEM((4, *block), LOW),
            pltpu.VMEM((8, *block), LOW),
            pltpu.VMEM((line, 2, *qkv.shape), LOW),
            pltpu.VMEM((line, 2, *proj.shape), LOW),
            pltpu.VMEM((line, *ff[1].shape), LOW),
            pltpu.VMEM((2, *heads), LOW),
            pltpu.SemaphoreType.DMA((copies,)),
            pltpu.SemaphoreType.DMA((copies,)),
            pltpu.SemaphoreType.DMA((line,)),
            pltpu.SemaphoreType.DMA((4 * group,)),
            pltpu.SemaphoreType.DMA((8,)),
        ],
        cost_estimate=pl.CostEstimate(
            flops=100_000_000_000, bytes_accessed=40_000_000, transcendentals=4_000_000
        ),
        compiler_params=pltpu.CompilerParams(
            collective_id=0, has_side_effects=True, vmem_limit_bytes=58 << 20
        ),
    )(tokens, cotangent, qkv, proj, *ff, inverse, *segments)


def middle_kernel(
    part, tokens, vectors, hidden, mids, arrived, summed, across_in, send_sems, recv_sems
):
    (me, sibling, across), ids = neighbours()
    far = across + 1 - 2 * (across % 2)
    width = tokens.shape[1]
    greet(ids)
    link = Sender(send_sems, recv_sems)
    first = link.send(part.at[far], arrived.at[0], ids[0])
    second = link.send(part.at[sibling], arrived.at[1], ids[0])
    first.wait_recv()
    summed[...] = (part[across].astype(F32) + arrived[0].astype(F32)).astype(LOW)
    third = link.send(summed, across_in, ids[1])
    second.wait_recv()
    hidden[...] = tokens[...].astype(F32) + (part[me].astype(F32) + arrived[1].astype(F32))
    third.wait_recv()
    total = hidden[...] + across_in[...].astype(F32)
    hidden[...] = total
    mids[0] = (total * inverse_rms(total) * vectors[1:2, :width]).astype(LOW)
    for _ in plane_gather(link, mids, ids):
        pass
    link.finish()


def middle(part, tokens, vectors):
    block = tokens.shape
    vmem = pl.BlockSpec(memory_space=pltpu.VMEM)
    return pl.pallas_call(
        middle_kernel,
        out_shape=[jax.ShapeDtypeStruct(block, F32), jax.ShapeDtypeStruct((8, *block), LOW)],
        in_specs=[vmem] * 3,
        out_specs=[vmem] * 2,
        scratch_shapes=[
            pltpu.VMEM((2, *block), LOW),
            pltpu.VMEM(block, LOW),
            pltpu.VMEM(block, LOW),
            pltpu.SemaphoreType.DMA((16,)),
            pltpu.SemaphoreType.DMA((16,)),
        ],
        compiler_params=pltpu.CompilerParams(
            collective_id=1, has_side_effects=True, vmem_limit_bytes=58 << 20
        ),
    )(part, tokens, vectors)


def cut_kernel(shape, *refs):
    follows, group, units = shape
    if follows:
        mids_in, cots_in, whole_in, out_before, mid_before, hidden_in, *refs = refs
    else:
        mids_in, cots_in, weight_in, rows_in, *refs = refs
    term, out, mid, *refs = refs
    if follows:
        ahead, *refs = refs
    mids, cots, weight, rows, down, act, grad, stage, before, *refs = refs
    if follows:
        odd, arrived, held, from_y, corner, total, slots, ahead_sems, *refs = refs
    load_sems, weight_sems, stage_sems, before_sems, send_sems, recv_sems = refs
    (me, sibling, across), ids = neighbours()
    far = across + 1 - 2 * (across % 2)
    others = (sibling, across, far)
    line, _, owned, cols = weight.shape
    count, block, width = mids.shape
    quarter = width // 4
    fold = quarter // owned
    core, over_x, over_y = ids
    greet((core, over_x, {"seq": far}, over_y))
    link = Sender(send_sems, recv_sems)

    def load(source, target, sem):
        copy = pltpu.make_async_copy(source, target, sem)
        copy.start()
        return copy

    if follows:
        sent = [
            link.send(whole_in.at[pl.ds(k * group, group), 2], rows.at[me], {"seq": k})
            for k in others
        ]
        loads = [load(whole_in.at[pl.ds(me * group, group), 2], rows.at[me], weight_sems.at[line])]
        loads += [
            load(whole_in.at[z, pl.ds(0, 2)], weight.at[z], weight_sems.at[z]) for z in range(line)
        ]
    else:
        sent = []
        loads = [load(rows_in, rows, weight_sems.at[line]), load(weight_in, weight, weight_sems.at[0])]
    for t in range(count):
        load(mids_in.at[t], mids.at[t], load_sems.at[0, t])
        load(cots_in.at[t], cots.at[t], load_sems.at[1, t])
    if follows:
        loads.append(load(hidden_in, total, ahead_sems.at[2]))
    for copy in loads:
        copy.wait()

    def put(t):
        return pltpu.make_async_copy(slots.at[t % 2], ahead.at[t], ahead_sems.at[t % 2])

    def take(t):
        return pltpu.make_async_copy(ahead.at[t], slots.at[t % 2], ahead_sems.at[t % 2])

    def forward(t, carry):
        pltpu.make_async_copy(mids_in.at[t], mids.at[t], load_sems.at[0, t]).wait()

        @pl.when(t >= 2)
        def _():
            put(t - 2).wait()

        slots[t % 2] = dot(mids[t], weight[...].reshape(width, cols))
        put(t).start()
        return carry

    if follows:
        lax.fori_loop(0, count, forward, 0)
        for t in (count - 2, count - 1):
            put(t).wait()
        take(0).start()
    for copy in sent:
        copy.wait_recv()
    for k in range(4):
        for member in range(group):
            for j in range(fold):
                first = k * quarter + j * owned
                down[first : first + owned, member * units : (member + 1) * units] = rows[
                    k, member, :, j * units : (j + 1) * units
                ]

    def tokens(t, carry):
        if follows:

            @pl.when(t + 1 < count)
            def _():
                take(t + 1).start()

            take(t).wait()
            gate_up = slots[t % 2]
        else:
            pltpu.make_async_copy(mids_in.at[t], mids.at[t], load_sems.at[0, t]).wait()
            gate_up = dot(mids[t], weight[...].reshape(width, cols))
        pltpu.make_async_copy(cots_in.at[t], cots.at[t], load_sems.at[1, t]).wait()
        grad_act = dot(cots[t], down[...])
        gate, upward = gate_up[:, : cols // 2], gate_up[:, cols // 2 :]
        sigmoid_gate = jax.nn.sigmoid(gate)
        silu = gate * sigmoid_gate
        act[t] = (silu * upward).astype(LOW)
        grad[t, :, : cols // 2] = (
            grad_act * upward * sigmoid_gate * (1.0 + gate * (1.0 - sigmoid_gate))
        ).astype(LOW)
        grad[t, :, cols // 2 :] = (grad_act * silu).astype(LOW)
        return carry

    lax.fori_loop(0, count, tokens, 0)

    def ask(source, t, slot):
        return load(source.at[t], before.at[slot], before_sems.at[slot])

    all_act = act[...].reshape(count * block, cols // 2)
    for k in range(4):
        value = column_product(
            cots[:, :, k * quarter : (k + 1) * quarter].reshape(count * block, quarter), all_act
        ).astype(LOW)
        for member in range(group):
            for j in range(fold):
                rows[k, member, :, j * units : (j + 1) * units] = value[
                    j * owned : (j + 1) * owned, member * units : (member + 1) * units
                ]
    sent = [
        link.send(rows.at[k], term.at[pl.ds(me * group, group), 2], {"seq": k}) for k in others
    ]
    term[pl.ds(me * group, group), 2] = rows[me]
    if follows:
        order = (7, 5, 6, 3, 4, 1, 2, 0)
        asked = ask(out_before, order[0], 0)
        halved = {}
        for number, t in enumerate(order):
            ready = asked
            if number + 1 < count:
                asked = ask(out_before, order[number + 1], (number + 1) % 2)
            value = times_transpose(act[t], down[...])
            ready.wait()
            value = value + before[number % 2].astype(F32)
            if t % 2 == 1:
                slot = t // 2 % 2
                if t < 4:
                    link.release(halved[t + 3])
                odd[slot] = value.astype(LOW)
                halved[t - 1] = link.send(odd.at[slot], arrived.at[t // 2], core)
                continue
            halved[t].wait_recv()
            value = value + arrived[t // 2].astype(F32)
            if t == 0:
                total[...] += value
            else:
                held[t // 2 - 1] = value.astype(LOW)
            if t == 6:
                turn = link.send(held.at[2], corner, over_y)
            if t == 4:
                direct = link.send(held.at[1], from_y, over_y)

    all_grad = grad[...].reshape(count * block, cols)
    for z in range(line):
        value = column_product(
            mids[:, :, 2 * owned * z : 2 * owned * (z + 1)].reshape(count * block, 2 * owned),
            all_grad,
        ).astype(LOW)
        for y in range(2):
            term[z, y] = value[y * owned : (y + 1) * owned, :]
        if follows and z == line - 2:
            turn.wait_recv()
            held[0] = (held[0].astype(F32) + corner[...].astype(F32)).astype(LOW)
            last = link.send(held.at[0], out, over_x)

    targets = {0: mid} if follows else {0: mid, 1: out}
    if follows:
        ask(mid_before, 0, 0)

    def hand_over(t, place):
        return pltpu.make_async_copy(
            stage.at[t % 2, place], targets[place].at[t], stage_sems.at[t % 2, place]
        )

    def back(t, carry):
        @pl.when(t >= 2)
        def _():
            for place in targets:
                hand_over(t - 2, place).wait()

        values = {0: times_transpose(grad[t], weight[...].reshape(width, cols))}
        if follows:

            @pl.when(t + 1 < count)
            def _():
                ask(mid_before, t + 1, (t + 1) % 2)

            pltpu.make_async_copy(
                mid_before.at[t], before.at[t % 2], before_sems.at[t % 2]
            ).wait()
            values[0] = values[0] + before[t % 2].astype(F32)
        else:
            values[1] = times_transpose(act[t], down[...])
        for place in targets:
            stage[t % 2, place] = values[place].astype(LOW)
            hand_over(t, place).start()
        return carry

    lax.fori_loop(0, count, back, 0)
    for t in (count - 2, count - 1):
        for place in targets:
            hand_over(t, place).wait()
    for copy in sent:
        copy.wait_recv()
    if follows:
        direct.wait_recv()
        last.wait_recv()
        out[...] = (total[...] + out[...].astype(F32) + from_y[...].astype(F32)).astype(LOW)
    link.finish()


def cut_call(follows, args, sizes):
    group, line, owned, units = sizes
    mids = args[0]
    count, block, width = mids.shape
    cols = 2 * group * units
    hbm, vmem = (pl.BlockSpec(memory_space=pl.ANY), pl.BlockSpec(memory_space=pltpu.VMEM))
    rows = (4, group, owned, cols)
    like_mids = jax.ShapeDtypeStruct(mids.shape, LOW)
    low_scratch = [
        mids.shape,
        mids.shape,
        (line, 2, owned, cols),
        rows,
        (width, cols // 2),
        (count, block, cols // 2),
        (count, block, cols),
        (2, 1 if follows else 2, block, width),
        (2, block, width),
    ]
    ahead, late_scratch = [], []
    if follows:
        for size in (2, 4, 3):
            low_scratch.append((size, block, width))
        low_scratch += [(block, width)] * 2
        ahead = [jax.ShapeDtypeStruct((count, block, cols), F32)]
        late_scratch = [
            pltpu.VMEM((block, width), F32),
            pltpu.VMEM((2, block, cols), F32),
            pltpu.SemaphoreType.DMA((3,)),
        ]
    return pl.pallas_call(
        functools.partial(cut_kernel, (follows, group, units)),
        out_shape=[
            jax.ShapeDtypeStruct((line, 3, owned, cols), LOW),
            jax.ShapeDtypeStruct((block, width), LOW) if follows else like_mids,
            like_mids,
            *ahead,
        ],
        in_specs=[hbm] * len(args),
        out_specs=[vmem, vmem if follows else hbm, hbm] + [hbm] * len(ahead),
        scratch_shapes=[pltpu.VMEM(shape, LOW) for shape in low_scratch]
        + late_scratch
        + [
            pltpu.SemaphoreType.DMA((2, count)),
            pltpu.SemaphoreType.DMA((line + 1,)),
            pltpu.SemaphoreType.DMA((2, 2)),
            pltpu.SemaphoreType.DMA((2,)),
            pltpu.SemaphoreType.DMA((16,)),
            pltpu.SemaphoreType.DMA((16,)),
        ],
        compiler_params=pltpu.CompilerParams(
            collective_id=4 if follows else 3, has_side_effects=True, vmem_limit_bytes=61 << 20
        ),
        cost_estimate=pl.CostEstimate(
            flops=50_000_000_000, bytes_accessed=40_000_000, transcendentals=2_000_000
        ),
    )(*args)


def spread_blocks(link, ids, pair, ff_sum, hidden_blocks, down_blocks, local_sems):
    core, over_x, over_y = ids
    kept, down = ff_sum.at[pair], ff_sum.at[2]
    local = [
        pltpu.make_async_copy(kept, hidden_blocks.at[0], local_sems.at[0]),
        pltpu.make_async_copy(down, down_blocks.at[0], local_sems.at[1]),
    ]
    for copy in local:
        copy.start()
    to_x = [
        link.send(kept, hidden_blocks.at[2], over_x),
        link.send(down, down_blocks.at[2], over_x),
    ]
    last = [
        link.send(kept, hidden_blocks.at[1], core),
        link.send(down, down_blocks.at[1], core),
    ]
    yield
    over = link.send(ff_sum.at[1 - pair], hidden_blocks.at[4], over_y)
    yield
    over.wait_recv()
    far = link.send(hidden_blocks.at[4], hidden_blocks.at[6], over_x)
    last.append(link.send(hidden_blocks.at[4], hidden_blocks.at[5], core))
    for copy, blocks in zip(to_x, (hidden_blocks, down_blocks)):
        copy.wait_recv()
        last.append(link.send(blocks.at[2], blocks.at[3], core))
    yield
    far.wait_recv()
    last.append(link.send(hidden_blocks.at[6], hidden_blocks.at[7], core))
    yield
    for copy in last:
        copy.wait_recv()
    for copy in local:
        copy.wait()
    yield


def spread_kernel(ff_sum, _, hidden_blocks, down_blocks, send_sems, recv_sems, local_sems):
    _, ids = neighbours()
    greet(ids)
    link = Sender(send_sems, recv_sems)
    pair = lax.axis_index("fsdp") % 2
    for _ in spread_blocks(link, ids, pair, ff_sum, hidden_blocks, down_blocks, local_sems):
        pass
    link.finish()


def spread(ff_sum, earlier):
    hbm, vmem = (pl.BlockSpec(memory_space=pl.ANY), pl.BlockSpec(memory_space=pltpu.VMEM))
    return pl.pallas_call(
        spread_kernel,
        out_shape=[
            jax.ShapeDtypeStruct((count, *ff_sum.shape[1:]), LOW) for count in (8, 4)
        ],
        in_specs=[vmem, hbm],
        out_specs=[hbm] * 2,
        scratch_shapes=[pltpu.SemaphoreType.DMA((12,))] * 2 + [pltpu.SemaphoreType.DMA((2,))],
        compiler_params=pltpu.CompilerParams(
            collective_id=5, has_side_effects=True, vmem_limit_bytes=58 << 20
        ),
        cost_estimate=pl.CostEstimate(
            flops=50_000_000_000, bytes_accessed=20_000_000, transcendentals=0
        ),
    )(ff_sum, earlier)


def closing_kernel(
    shape,
    terms_in,
    hidden,
    upstream,
    tokens_in,
    normed_in,
    vectors,
    weight,
    proj_mine,
    queries,
    keys,
    values,
    merged,
    logsum,
    cosines,
    sines,
    seg_col,
    seg_row,
    ff_sum,
    tokens_grad,
    gain_terms,
    attn_sum,
    hidden_blocks,
    down_blocks,
    mid_terms,
    tokens_all,
    normed,
    arrived,
    held,
    from_x,
    from_y,
    corner,
    upper,
    grad_heads,
    grad_queries,
    grad_keys,
    grad_values,
    kv,
    projected,
    proj_part,
    proj_in,
    proj_half,
    bias_row,
    qkv_part,
    qkv_in,
    late,
    late_x,
    send_sems,
    recv_sems,
    local_sems,
    load_sems,
):
    owned, per_dev, group = shape
    (me, sibling, across), (core, over_x, over_y) = neighbours()
    far = across + 1 - 2 * (across % 2)
    others = (sibling, across, far)
    pair = lax.axis_index("fsdp") % 2
    rows, width = hidden.shape
    seq_count = tokens_all.shape[0]
    quarter = width // seq_count
    low, high = (pl.ds(0, rows // 2), pl.ds(rows // 2, rows // 2))
    gains = (vectors[0:1, :width], vectors[1:2, :width])
    greet((core, over_x, {"seq": far}, over_y))
    link = Sender(send_sems, recv_sems)

    loads = {}
    for k in (7, 3, 5, 1, 6, 2, 4, 0):
        loads[k] = pltpu.make_async_copy(terms_in.at[k], mid_terms.at[k], load_sems.at[k])
        loads[k].start()
    kept_loads = [
        pltpu.make_async_copy(source, target, load_sems.at[8 + number])
        for number, (source, target) in enumerate(((tokens_in, tokens_all), (normed_in, normed)))
    ]
    for copy in kept_loads:
        copy.start()
    halved = {}
    for k in (6, 2, 4, 0):
        loads[k + 1].wait()
        halved[k] = link.send(mid_terms.at[k + 1], arrived.at[k // 2], core)

    def chip_sum(k):
        loads[k].wait()
        halved[k].wait_recv()
        return mid_terms[k].astype(F32) + arrived[k // 2].astype(F32)

    held[2] = chip_sum(6).astype(LOW)
    turn_y = link.send(held.at[2, low], corner.at[0], over_x)
    turn_x = link.send(held.at[2, high], corner.at[1], over_y)
    held[0] = chip_sum(2).astype(LOW)
    direct_x = link.send(held.at[0, low], from_x.at[low], over_x)
    held[1] = chip_sum(4).astype(LOW)
    direct_y = link.send(held.at[1, high], from_y.at[high], over_y)
    tokens_grad[...] = chip_sum(0)
    turn_x.wait_recv()
    held[0, high] = (held[0, high].astype(F32) + corner[1].astype(F32)).astype(LOW)
    second_x = link.send(held.at[0, high], from_x.at[high], over_x)
    turn_y.wait_recv()
    held[1, low] = (held[1, low].astype(F32) + corner[0].astype(F32)).astype(LOW)
    second_y = link.send(held.at[1, low], from_y.at[low], over_y)
    for copy in (direct_x, direct_y, second_x, second_y):
        copy.wait_recv()

    grad_mid = tokens_grad[...] + from_x[...].astype(F32) + from_y[...].astype(F32)
    through, term = norm_back(hidden[...], inverse_rms(hidden[...]), gains[1], grad_mid)
    gain_terms[1:2, :] = term[None]
    total = upstream[...].astype(F32) + through
    tokens_grad[...] = total
    upper[me] = total.astype(LOW)
    last = [link.send(upper.at[me], upper.at[me], core)]
    to_x = [link.send(upper.at[me, half], upper.at[me, half], over_x) for half in (low, high)]
    for copy, half in zip(to_x, (low, high)):
        copy.wait_recv()
        last.append(link.send(upper.at[across, half], upper.at[across, half], core))
    for copy in last:
        copy.wait_recv()

    head_rows = per_dev * HD
    for block in range(seq_count):
        grad_heads[block * rows : (block + 1) * rows, :] = sum(
            times_transpose(
                upper[block, :, k * quarter : (k + 1) * quarter],
                proj_mine[k].reshape(head_rows, quarter),
            )
            for k in range(seq_count)
        ).astype(LOW)
    for k in range(seq_count):
        term = sum(
            column_product(
                merged[block * rows : (block + 1) * rows, :],
                upper[block, :, k * quarter : (k + 1) * quarter],
            )
            for block in range(seq_count)
        ).astype(LOW)
        for member in range(group):
            for y in range(2):
                first = (2 * member + y) * owned
                proj_part[y, k, member] = term[first : first + owned, :]
    proj_over = link.send(proj_part.at[1 - pair], proj_in, over_y)
    spread = spread_blocks(
        link, (core, over_x, over_y), pair, ff_sum, hidden_blocks, down_blocks, local_sems
    )
    next(spread)
    next(spread)

    grad_keys[...] = jnp.zeros_like(grad_keys)
    grad_values[...] = jnp.zeros_like(grad_values)
    scale = HD ** (-0.5)
    for block in range(seq_count):
        here, last_key = pl.ds(block * rows, rows), (block + 1) * rows
        row_index = block * rows + lax.broadcasted_iota(jnp.int32, (rows, last_key), 0)
        key_index = lax.broadcasted_iota(jnp.int32, (rows, last_key), 1)
        allowed = (key_index <= row_index) & (seg_col[here, :] == seg_row[:, :last_key])
        for head in range(per_dev):
            query = queries[head, here, :]
            upper_head = grad_heads[here, head * HD : (head + 1) * HD]
            scores = times_transpose(query, keys[:last_key, :]) * scale
            probs = jnp.where(allowed, jnp.exp(scores - logsum[head, here, :]), 0.0)
            grad_probs = times_transpose(upper_head, values[:last_key, :])
            inner = jnp.sum(probs * grad_probs, axis=-1, keepdims=True)
            grad_scores = (probs * (grad_probs - inner)).astype(LOW)
            grad_queries[head, here, :] = (dot(grad_scores, keys[:last_key, :]) * scale).astype(LOW)
            grad_keys[:last_key, :] += column_product(grad_scores, query)
            grad_values[:last_key, :] += column_product(probs.astype(LOW), upper_head)
    next(spread)
    for copy in kept_loads:
        copy.wait()
    holds_values = me % 2 == 1
    key_copy = (grad_keys[...] * scale).astype(LOW)
    value_copy = grad_values[...].astype(LOW)
    kv[0] = jnp.where(holds_values, key_copy, value_copy)
    swapped = link.send(kv.at[0], kv.at[1], core)
    grad_keys[...] = jnp.where(holds_values, value_copy, key_copy).astype(F32)
    proj_over.wait_recv()
    proj_half[...] = (proj_part[pair].astype(F32) + proj_in[...].astype(F32)).astype(LOW)
    cols = weight.shape[1]

    def proj_place(device):
        return (pl.ds(device * group, group), pl.ds(0, owned), pl.ds(cols, quarter))

    last = [
        link.send(proj_half.at[k], attn_sum.at[proj_place(me)], {"seq": k}) for k in others
    ]
    attn_sum[proj_place(me)] = proj_half[me]
    swapped.wait_recv()
    grad_kv = grad_keys[...] + kv[1].astype(F32)

    bias_row[...] = jnp.zeros_like(bias_row)
    bias_parts = 0.0
    gain_terms[0:1, :] = jnp.zeros((1, width), F32)
    for block in range(seq_count):
        here = pl.ds(block * rows, rows)
        cosine, sine = cosines[here, :], sines[here, :]

        def rotate_back(head):
            return head * cosine - pltpu.roll(head, HD // 2, 1) * sine

        for head in range(per_dev):
            projected[here, head * HD : (head + 1) * HD] = rotate_back(
                grad_queries[head, here, :].astype(F32)
            ).astype(LOW)
        plain = grad_kv[block * rows : (block + 1) * rows, :]
        projected[here, head_rows:] = jnp.where(holds_values, plain, rotate_back(plain)).astype(LOW)
        grad_block = projected[here, :]
        bias_parts += jnp.sum(grad_block.astype(F32), axis=0, keepdims=True)
        grad_in = times_transpose(grad_block, weight[...])
        value = tokens_all[block].astype(F32)
        gain_terms[0:1, :] += jnp.sum(
            grad_in * value * inverse_rms(value), axis=0, keepdims=True
        )
        arrived[block] = grad_in.astype(LOW)
    first = link.send(arrived.at[far], late.at[0], core)
    second = link.send(arrived.at[sibling], late.at[1], core)
    first.wait_recv()
    link.release(direct_x, second_x)
    held[0] = (arrived[across].astype(F32) + late[0].astype(F32)).astype(LOW)
    third = link.send(held.at[0], late_x, over_x)
    kv_first = (H + KV * (me % 2) + me // 2) * HD
    bias_row[0:1, pl.ds(pl.multiple_of(me * head_rows, HD), head_rows)] = bias_parts[:, :head_rows]
    bias_row[0:1, pl.ds(pl.multiple_of(kv_first, HD), HD)] = bias_parts[:, head_rows:]
    line = qkv_in.shape[0]
    owned_bias = bias_row.shape[1] // (2 * line)
    qkv_part[:, :, owned:, :] = jnp.zeros_like(qkv_part[:, :, owned:, :])
    for z in range(line):
        for y in range(2):
            owner, at = 2 * z + y, 0
            for source, row, length in (
                (gain_terms, 0, owned),
                (gain_terms, 1, owned),
                (bias_row, 0, owned_bias),
            ):
                done = 0
                while done < length:
                    span = min(length - done, cols - at % cols)
                    first_col = owner * length + done
                    qkv_part[
                        y, z, owned + at // cols : owned + at // cols + 1, at % cols : at % cols + span
                    ] = source[row : row + 1, first_col : first_col + span].astype(LOW)
                    done, at = done + span, at + span
    for z in range(line):
        term = sum(
            column_product(
                normed[block, :, 2 * owned * z : 2 * owned * (z + 1)],
                projected[block * rows : (block + 1) * rows, :],
            )
            for block in range(seq_count)
        ).astype(LOW)
        for y in range(2):
            qkv_part[y, z, :owned, :] = term[y * owned : (y + 1) * owned, :]
    qkv_over = link.send(qkv_part.at[1 - pair], qkv_in, over_y)
    next(spread)
    second.wait_recv()
    third.wait_recv()
    grad_in = arrived[me].astype(F32) + late[1].astype(F32) + late_x[...].astype(F32)
    value = tokens_all[me].astype(F32)
    through, _ = norm_back(value, inverse_rms(value), gains[0], grad_in)
    tokens_grad[...] += through
    qkv_over.wait_recv()
    attn_sum[:, :, :cols] = (qkv_part[pair].astype(F32) + qkv_in[...].astype(F32)).astype(LOW)
    attn_sum[:, owned:, cols:] = jnp.zeros_like(attn_sum[:, owned:, cols:])
    for copy in last:
        copy.wait_recv()
    next(spread)
    link.finish()


def closing(args, sizes):
    owned, vector_rows, bias_cols, per_dev, group, line = sizes
    hidden, weight, proj_mine = args[1], args[6], args[7]
    rows, width = hidden.shape
    block = (rows, width)
    cols = weight.shape[1]
    quarter = proj_mine.shape[-1]
    heads = (4 * rows, HD)
    rows_in = (4, group, owned, quarter)
    outs = [
        jax.ShapeDtypeStruct(block, F32),
        jax.ShapeDtypeStruct((2, width), F32),
        jax.ShapeDtypeStruct((line, owned + vector_rows, cols + quarter), LOW),
        jax.ShapeDtypeStruct((8, *args[-1].shape[1:]), LOW),
        jax.ShapeDtypeStruct((4, *args[-1].shape[1:]), LOW),
    ]
    low_scratch = [
        (8, *block),
        (4, *block),
        (4, *block),
        (4, *block),
        (3, *block),
        block,
        block,
        (2, rows // 2, width),
        (4, *block),
        (4 * rows, per_dev * HD),
        (per_dev, *heads),
    ]
    return pl.pallas_call(
        functools.partial(closing_kernel, (owned, per_dev, group)),
        out_shape=outs,
        in_specs=[
            pl.BlockSpec(memory_space=pl.ANY if k in (0, 3, 4) else pltpu.VMEM)
            for k in range(len(args))
        ],
        out_specs=[pl.BlockSpec(memory_space=pltpu.VMEM)] * (len(outs) - 2)
        + [pl.BlockSpec(memory_space=pl.ANY)] * 2,
        scratch_shapes=[pltpu.VMEM(shape, LOW) for shape in low_scratch]
        + [pltpu.VMEM(heads, F32)] * 2
        + [
            pltpu.VMEM(shape, LOW)
            for shape in (
                (2, *heads),
                (4 * rows, cols),
                (2, *rows_in),
                rows_in,
                rows_in,
            )
        ]
        + [pltpu.VMEM((1, bias_cols), F32)]
        + [
            pltpu.VMEM(shape, LOW)
            for shape in (
                (2, line, owned + vector_rows, cols),
                (line, owned + vector_rows, cols),
                (2, *block),
                block,
            )
        ]
        + [pltpu.SemaphoreType.DMA((48,))] * 2
        + [pltpu.SemaphoreType.DMA((2,)), pltpu.SemaphoreType.DMA((10,))],
        compiler_params=pltpu.CompilerParams(
            collective_id=2, has_side_effects=True, vmem_limit_bytes=58 << 20
        ),
        cost_estimate=pl.CostEstimate(
            flops=100_000_000_000, bytes_accessed=40_000_000, transcendentals=4_000_000
        ),
    )(*args)


def columns_kernel(place, *refs):
    *pieces, out = refs
    row = 0
    for piece in pieces:
        count, rows, quarter = piece.shape
        for k in range(count):
            here = place[0] + k - 2 * ((place[0] % 2) * (k % 2)) - 4 * (
                (place[0] // 2 % 2) * (k // 2 % 2)
            )
            out[pl.ds(row, rows), pl.ds(k * quarter, quarter)] = piece[here].astype(F32)
        row += rows


def columns_call(place, pieces):
    rows = sum(piece.shape[1] for piece in pieces)
    width = pieces[0].shape[0] * pieces[0].shape[2]
    return pl.pallas_call(
        columns_kernel,
        out_shape=jax.ShapeDtypeStruct((rows, width), F32),
        in_specs=[pl.BlockSpec(memory_space=pltpu.SMEM)]
        + [pl.BlockSpec(memory_space=pltpu.VMEM)] * len(pieces),
        out_specs=pl.BlockSpec(memory_space=pltpu.VMEM),
        compiler_params=pltpu.CompilerParams(vmem_limit_bytes=40 << 20),
    )(place, *pieces)


def down_kernel(fold, place, *refs):
    *pieces, out = refs
    row = 0
    for piece in pieces:
        count, owned, width = piece.shape
        span = width // fold
        for k in range(count):
            here = place[0] + k - 2 * ((place[0] % 2) * (k % 2)) - 4 * (
                (place[0] // 2 % 2) * (k // 2 % 2)
            )
            whole = piece[here].astype(F32)
            for j in range(fold):
                whole_part = whole[:, j * span : (j + 1) * span]
                out[pl.ds(row, span), pl.ds((k * fold + j) * owned, owned)] = whole_part.T
        row += span


def down_call(place, pieces, fold):
    rows = sum(piece.shape[2] // fold for piece in pieces)
    width = pieces[0].shape[0] * pieces[0].shape[1] * fold
    return pl.pallas_call(
        functools.partial(down_kernel, fold),
        out_shape=jax.ShapeDtypeStruct((rows, width), F32),
        in_specs=[pl.BlockSpec(memory_space=pltpu.SMEM)]
        + [pl.BlockSpec(memory_space=pltpu.VMEM)] * len(pieces),
        out_specs=pl.BlockSpec(memory_space=pltpu.VMEM),
        compiler_params=pltpu.CompilerParams(vmem_limit_bytes=40 << 20),
    )(place, *pieces)


def hidden_kernel(cuts, group, place, *refs):
    *pieces, out = refs
    units = cuts[-1][1]
    count = pieces[0].shape[0] // 2
    for k in range(count):
        here = place[0] + k - 2 * ((place[0] % 2) * (k % 2)) - 4 * (
            (place[0] // 2 % 2) * (k // 2 % 2)
        )
        for pair in range(2):
            entry = (pair + place[1] - 2 * pair * place[1]) * count + here
            for part in range(2):
                for member in range(group):
                    first = (((part * count + k) * group + member) * 2 + pair) * units
                    for piece, (low, high) in zip(pieces, cuts):
                        span = high - low
                        at = (part * group + member) * span
                        out[:, first + low : first + high] = piece[entry][
                            :, at : at + span
                        ].astype(F32)


def hidden_call(place, pieces, cuts, group):
    rows = pieces[0].shape[1]
    units = cuts[-1][1]
    width = 2 * 8 * group * units
    step = 16
    return pl.pallas_call(
        functools.partial(hidden_kernel, cuts, group),
        grid=(rows // step,),
        out_shape=jax.ShapeDtypeStruct((rows, width), F32),
        in_specs=[pl.BlockSpec(memory_space=pltpu.SMEM)]
        + [pl.BlockSpec((8, step, piece.shape[2]), lambda i: (0, i, 0)) for piece in pieces],
        out_specs=pl.BlockSpec((step, width), lambda i: (i, 0)),
        compiler_params=pltpu.CompilerParams(vmem_limit_bytes=40 << 20),
    )(place, *pieces)


def local(
    tokens,
    segment_ids,
    attn_gain,
    qkv_weight,
    qkv_bias,
    proj_weight,
    mlp_gain,
    gate_up_weight,
    down_weight,
    cotangent,
):
    seq_count = lax.axis_size("seq")
    fsdp_count = lax.axis_size("fsdp")
    line = fsdp_count // 2
    place = lax.axis_index("seq")
    odd = lax.axis_index("fsdp") % 2 == 1
    tok_rows, width = tokens.shape[1:]
    seq_len = tok_rows * seq_count
    owned = qkv_weight.shape[0]
    owned_hidden = down_weight.shape[0]
    hidden = owned_hidden * fsdp_count
    quarter = width // seq_count
    per_dev = H // seq_count
    head_cols = per_dev * HD
    score_scale = HD ** (-0.5)
    group = line // seq_count
    cut_at = owned_hidden // 2 // 128 * 128
    cuts = [(0, cut_at), (cut_at, owned_hidden)]

    holds_values = place % 2 == 1
    kv_first = (H + KV * (place % 2) + place // 2) * HD
    qkv_own = jnp.concatenate(
        [
            lax.dynamic_slice_in_dim(qkv_weight, place * head_cols, head_cols, 1),
            lax.dynamic_slice_in_dim(qkv_weight, kv_first, HD, 1),
        ],
        axis=1,
    )
    cols = head_cols + HD
    vector = jnp.concatenate([attn_gain, mlp_gain, qkv_bias])
    vector_size = vector.shape[0]
    vector_rows = -(-vector_size // (16 * cols)) * 16
    vector = jnp.pad(vector, (0, vector_rows * cols - vector_size)).reshape(vector_rows, cols)
    proj_cols = lax.dynamic_slice_in_dim(proj_weight, place * quarter, quarter, 1)
    down_cols = lax.dynamic_slice_in_dim(down_weight, place * quarter, quarter, 1)
    fold = quarter // owned

    def folded(value):
        return jnp.concatenate(
            [value[..., j * owned : (j + 1) * owned, :] for j in range(fold)], axis=-1
        )

    def ff_columns(low, high, pair):
        return jnp.concatenate(
            [
                lax.dynamic_slice_in_dim(
                    gate_up_weight,
                    first + ((place * group + member) * 2 + pair) * owned_hidden + low,
                    high - low,
                    1,
                )
                for first in (0, hidden)
                for member in range(group)
            ],
            axis=1,
        )

    ff_sent = []
    for low, high in cuts:
        by_owner = [ff_columns(low, high, pair) for pair in range(2)]
        ff_sent.append((by_owner, folded(jnp.transpose(down_cols[low:high]))))
    segment_row = segment_ids[0]
    inverse = THETA ** (-2.0 * jnp.arange(HD // 2, dtype=F32) / HD)
    inverse = jnp.concatenate([inverse, inverse])[None]

    (
        cosines,
        sines,
        tokens_all,
        qkv_mine,
        vectors,
        proj_mine,
        first_all,
        first_rows,
        second_sent,
        normed_in,
        queries,
        head_keys,
        head_values,
        merged,
        logsum,
        attended,
        cots,
    ) = opening(
        tokens[0],
        cotangent[0],
        jnp.concatenate([qkv_own, vector], axis=0),
        lax.dynamic_slice_in_dim(proj_weight, place * quarter, quarter, 1),
        [part for by_owner, rows in ff_sent for part in (jnp.stack(by_owner), rows)],
        inverse,
        (segment_row[:, None], segment_row[None]),
        (owned, vector_size, per_dev, group, line),
    )
    second_all = line_gather(second_sent)
    hidden_in, mids = middle(attended, tokens[0], vectors)

    spans = [high - low for low, high in cuts]
    first_term, out_first, mid_first = cut_call(
        False, (mids, cots, first_all, first_rows), (group, line, owned, spans[0])
    )
    second_term, block_out, grad_mid, _ = cut_call(
        True, (mids, cots, second_all, out_first, mid_first, hidden_in), (group, line, owned, spans[1])
    )

    sums = [line_reduce(term) for term in (first_term, second_term)]

    tokens_grad, gain_terms, attn_term, *first_blocks = closing(
        (
            grad_mid,
            hidden_in,
            cotangent[0],
            tokens_all,
            normed_in,
            vectors,
            qkv_mine,
            proj_mine,
            queries,
            head_keys,
            head_values,
            merged,
            logsum,
            cosines,
            sines,
            segment_row[:, None],
            segment_row[None],
            sums[0],
        ),
        (owned, vector_rows, qkv_weight.shape[1], per_dev, group, line),
    )
    places_here = jnp.stack([place, lax.axis_index("fsdp") % 2]).astype(jnp.int32)
    corner = attn_term[:1, :16, :HD] + nought(sums[1][0, 0, 0])
    attn_term = lax.dynamic_update_slice(attn_term, corner, (0, 0, 0))
    attn_sum = line_reduce(attn_term)
    second_blocks = spread(sums[1], attn_term)
    hidden_pieces = [first_blocks[0], second_blocks[0]]
    down_pieces = [first_blocks[1], second_blocks[1]]
    down_grad = down_call(places_here, down_pieces, fold)
    gate_up_grad = hidden_call(places_here, hidden_pieces, cuts, group)
    attn_sums = seq_blocks(attn_sum + nought(second_blocks[0][0, 0, 0]))
    proj_grad = columns_call(
        places_here, [jnp.stack([part[:owned, cols:] for part in attn_sums])]
    )
    qkv_sums = in_order([part[:, :cols] for part in attn_sums])
    qkv_grad = jnp.concatenate(
        [part[:owned, :head_cols] for part in qkv_sums]
        + [part[:owned, head_cols:] for part in qkv_sums[0::2]]
        + [part[:owned, head_cols:] for part in qkv_sums[1::2]],
        axis=-1,
    ).astype(F32)
    vector_sum = sum(part[owned:].astype(F32) for part in qkv_sums).reshape(-1)
    return (
        block_out[None],
        tokens_grad[None],
        vector_sum[:owned],
        qkv_grad,
        vector_sum[2 * owned : vector_size],
        proj_grad,
        vector_sum[owned : 2 * owned],
        gate_up_grad,
        down_grad,
    )


def solution(mesh):
    in_specs = (
        P("fsdp", "seq", None),
        P("fsdp", None),
        P("fsdp"),
        P("fsdp", None),
        P("fsdp"),
        P("fsdp", None),
        P("fsdp"),
        P("fsdp", None),
        P("fsdp", None),
        P("fsdp", "seq", None),
    )
    out_specs = (
        P("fsdp", "seq", None),
        P("fsdp", "seq", None),
        P("fsdp"),
        P("fsdp", None),
        P("fsdp"),
        P("fsdp", None),
        P("fsdp"),
        P("fsdp", None),
        P("fsdp", None),
    )
    return jax.shard_map(local, mesh=mesh, in_specs=in_specs, out_specs=out_specs, check_vma=False)
```

```python
import functools

import jax
import jax.numpy as jnp
from jax import lax
from jax.experimental import pallas as pl
from jax.experimental.pallas import tpu as pltpu
from jax.sharding import PartitionSpec as P

H = 12
KV = 2
HD = 128
EPSILON = 1e-06
THETA = 1000000.0
FLOOR = -1e30
LOW = jnp.bfloat16
F32 = jnp.float32


def inverse_rms(value):
    return lax.rsqrt(jnp.mean(value * value, axis=-1, keepdims=True) + EPSILON)


def turned(value):
    halfway = value.shape[-1] // 2
    return jnp.concatenate([-value[..., halfway:], value[..., :halfway]], axis=-1)


def turned_back(value):
    halfway = value.shape[-1] // 2
    return jnp.concatenate([value[..., halfway:], -value[..., :halfway]], axis=-1)


def norm_back(value, factor, gain, upstream):
    weighted = upstream * gain
    gain_term = jnp.sum(upstream * value * factor, axis=0)
    through = factor * weighted - value * factor**3 * jnp.mean(
        weighted * value, axis=-1, keepdims=True
    )
    return (through, gain_term)


def dot(left, right):
    return jnp.dot(left, right, preferred_element_type=F32)


def column_product(left, right):
    return lax.dot_general(left, right, (((0,), (0,)), ((), ())), preferred_element_type=F32)


def times_transpose(left, right):
    return lax.dot_general(left, right, (((1,), (1,)), ((), ())), preferred_element_type=F32)


def swap(value, axis, distance):
    return lax.ppermute(value, axis, [(i, i ^ distance) for i in range(lax.axis_size(axis))])


def lines():
    size = lax.axis_size("fsdp")
    return [list(range(first, size, 2)) for first in range(2)]


def line_gather(value):
    return lax.all_gather(value, "fsdp", axis=0, axis_index_groups=lines(), tiled=False)


def line_reduce(value):
    return lax.psum_scatter(
        value, "fsdp", scatter_dimension=0, axis_index_groups=lines(), tiled=False
    )


def by_pair(own, other):
    second = lax.axis_index("fsdp") % 2 == 1
    return (jnp.where(second, other, own), jnp.where(second, own, other))


def pick(flag, first, second):
    return (jnp.where(flag, second, first), jnp.where(flag, first, second))


def nought(value):
    return jnp.minimum(jnp.abs(value), 0.0).astype(LOW)


def seq_blocks(value):
    across = swap(value, "seq", 2)
    return [value, swap(value, "seq", 1), across, swap(across, "seq", 1)]


def seq_reduce(parts):
    arrived = swap(jnp.stack([parts[1], parts[3]]), "seq", 1)
    across = (parts[2].astype(F32) + arrived[1].astype(F32)).astype(LOW)
    here = parts[0].astype(F32) + arrived[0].astype(F32)
    return here + swap(across, "seq", 2).astype(F32)


def in_order(blocks):
    me = lax.axis_index("seq")
    bits = 1
    while bits < len(blocks):
        flip = (me & bits) != 0
        blocks = [jnp.where(flip, blocks[k ^ bits], blocks[k]) for k in range(len(blocks))]
        bits *= 2
    return blocks


def relative(value):
    size = lax.axis_size("seq")
    me = lax.axis_index("seq")
    cut = value.reshape(size, value.shape[0] // size, *value.shape[1:])
    return [lax.dynamic_index_in_dim(cut, me ^ k, 0, keepdims=False) for k in range(size)]


def seq_exchange(pieces):
    taken = [part[0] for part in relative(pieces)]
    return in_order([taken[0]] + [swap(taken[k], "seq", k) for k in range(1, len(taken))])


MESH = pl.DeviceIdType.MESH


def neighbours():
    me, owner = lax.axis_index("seq"), lax.axis_index("fsdp")
    sibling = me + 1 - 2 * (me % 2)
    across = me + 2 - 4 * (me // 2 % 2)
    partner = owner + 1 - 2 * (owner % 2)
    return (me, sibling, across), ({"seq": sibling}, {"seq": across}, {"fsdp": partner})


def greet(devices):
    barrier = pltpu.get_barrier_semaphore()
    for device in devices:
        pl.semaphore_signal(barrier, inc=1, device_id=device, device_id_type=MESH)
    pl.semaphore_wait(barrier, len(devices))


class Sender:
    def __init__(self, send_sems, recv_sems):
        self.sems = (send_sems, recv_sems)
        self.count, self.open = 0, []

    def send(self, source, target, device):
        number = self.count
        copy = pltpu.make_async_remote_copy(
            src_ref=source,
            dst_ref=target,
            send_sem=self.sems[0].at[number],
            recv_sem=self.sems[1].at[number],
            device_id=device,
            device_id_type=MESH,
        )
        copy.start()
        self.count += 1
        self.open.append(copy)
        return copy

    def release(self, *copies):
        for copy in copies:
            copy.wait_send()
            self.open = [other for other in self.open if other is not copy]

    def finish(self):
        self.release(*self.open)


def plane_gather(link, blocks, ids):
    core, over_x, over_y = ids
    rows = blocks.shape[1]
    halves = (pl.ds(0, rows // 2), pl.ds(rows // 2, rows // 2))
    to_x = [link.send(blocks.at[0, half], blocks.at[2, half], over_x) for half in halves]
    last = [link.send(blocks.at[0], blocks.at[1], core)]
    yield
    to_y = [link.send(blocks.at[0, half], blocks.at[4, half], over_y) for half in halves[::-1]]
    yield
    to_x[0].wait_recv()
    diagonal = [link.send(blocks.at[2, halves[0]], blocks.at[6, halves[0]], over_y)]
    last.append(link.send(blocks.at[2, halves[0]], blocks.at[3, halves[0]], core))
    to_y[0].wait_recv()
    diagonal.append(link.send(blocks.at[4, halves[1]], blocks.at[6, halves[1]], over_x))
    last.append(link.send(blocks.at[4, halves[1]], blocks.at[5, halves[1]], core))
    to_x[1].wait_recv()
    last.append(link.send(blocks.at[2, halves[1]], blocks.at[3, halves[1]], core))
    to_y[1].wait_recv()
    last.append(link.send(blocks.at[4, halves[0]], blocks.at[5, halves[0]], core))
    for copy, half in zip(diagonal, halves):
        copy.wait_recv()
        last.append(link.send(blocks.at[6, half], blocks.at[7, half], core))
    for copy in last:
        copy.wait_recv()
    yield


def opening_kernel(
    shape,
    tokens,
    cotangent,
    qkv,
    proj,
    ff_own,
    ff_down,
    second_own,
    second_down,
    inverse,
    seg_col,
    seg_row,
    cosines,
    sines,
    tokens_out,
    weight,
    vectors,
    proj_mine,
    ff_all,
    ff_rows,
    second_out,
    normed_out,
    queries,
    keys,
    values,
    merged,
    logsum,
    part_out,
    cots_out,
    tokens_all,
    normed,
    part,
    cots,
    qkv_all,
    proj_all,
    ff_line,
    kv,
    send_sems,
    recv_sems,
    hand_send,
    hand_recv,
    local_sem,
):
    owned, vector_size, per_dev, group = shape
    (me, sibling, across), ids = neighbours()
    core, over_x, over_y = ids
    far = across + 1 - 2 * (across % 2)
    line = qkv_all.shape[0]
    size = 2 * line
    owner = lax.axis_index("fsdp")
    at, pair = owner // 2, owner % 2
    below, above = ({"fsdp": (owner + size - 2) % size}, {"fsdp": (owner + 2) % size})
    rows, width = tokens.shape
    seq_count = tokens_all.shape[0]
    seq_len = seq_count * rows
    halves = (pl.ds(0, rows // 2), pl.ds(rows // 2, rows // 2))
    others = (sibling, across, far)
    greet((*ids, {"seq": far}, below, above))
    link = Sender(send_sems, recv_sems)

    own_copy = pltpu.make_async_copy(ff_own.at[pair], ff_all.at[at, pair], local_sem.at[0])
    own_copy.start()
    leaving = [own_copy]

    def leave(source, target):
        copy = pltpu.make_async_copy(source, target, local_sem.at[len(leaving)])
        copy.start()
        leaving.append(copy)

    leave(second_own.at[pair], second_out.at[pair])
    leave(second_down, second_out.at[2])
    ff_line[at] = ff_down[...]
    tokens_all[me] = tokens[...]
    qkv_all[at, pair] = qkv[...]
    proj_all[at, pair] = proj[...]

    turned, handed = [], []

    def hand_on(k):
        z = (at + k) % line
        target, member = z // group, z % group
        copy = pltpu.make_async_remote_copy(
            src_ref=ff_line.at[z],
            dst_ref=ff_rows.at[me, member],
            send_sem=hand_send.at[k],
            recv_sem=hand_recv.at[me * group + member],
            device_id={"seq": target},
            device_id_type=MESH,
        )

        @pl.when(target != me)
        def _():
            copy.start()

        @pl.when(target == me)
        def _():
            ff_rows[me, member] = ff_line[z]

        handed.append((copy, target))

    def ring_steps():
        before = [None] * 3
        for k in range(line):
            z = (at + k) % line
            here = (ff_line.at[z], ff_all.at[z, pair], ff_all.at[z, 1 - pair])
            for place, target in enumerate(here):
                source = ff_own.at[pair] if k == 0 and place == 1 else target
                if k > 0:
                    before[place].wait_recv()
                elif place == 2:
                    turned[0].wait_recv()
                if k < line - 1:
                    before[place] = link.send(source, target, below)
                if place == 0:
                    hand_on(k)
                yield

    ring = ring_steps()

    def pump(count):
        for _ in range(count):
            next(ring, None)

    def along_line(array, k):
        here = array.at[(at + k) % line, pair]
        return link.send(here, here, below)

    def to_partner(array, k):
        here = array.at[(at + k) % line, pair]
        return link.send(here, here, over_y)

    onward = along_line(qkv_all, 0)
    last = [to_partner(qkv_all, 0)]
    to_x = [link.send(tokens_all.at[me, half], tokens_all.at[me, half], over_x) for half in halves]
    last.append(link.send(tokens_all.at[me], tokens_all.at[me], core))
    proj_onward = along_line(proj_all, 0)

    lanes = lax.broadcasted_iota(jnp.int32, (rows, HD), 1)
    for block in range(seq_count):
        here = pl.ds(block * rows, rows)
        before = jnp.sum((seg_row[...] < seg_col[here, :]).astype(F32), axis=1, keepdims=True)
        index = (block * rows + lax.broadcasted_iota(jnp.int32, (rows, 1), 0)).astype(F32)
        angles = (index - before) * inverse[...]
        cosines[here, :] = jnp.cos(angles)
        sines[here, :] = jnp.where(lanes < HD // 2, -jnp.sin(angles), jnp.sin(angles))
    for k in range(1, line):
        onward.wait_recv()
        if k < line - 1:
            onward = along_line(qkv_all, k)
        last.append(to_partner(qkv_all, k))
        proj_onward.wait_recv()
        if k < line - 1:
            proj_onward = along_line(proj_all, k)
        if k == line - 2:
            pump(2)
    turned.append(link.send(ff_own.at[1 - pair], ff_all.at[at, pair], over_y))
    for copy, half in zip(to_x, halves):
        copy.wait_recv()
        last.append(link.send(tokens_all.at[across, half], tokens_all.at[across, half], core))
    for copy in last:
        copy.wait_recv()
    proj_over = [to_partner(proj_all, k) for k in range(line)]
    second_over = link.send(second_own.at[1 - pair], second_out.at[pair], over_y)
    leave(tokens_all, tokens_out)
    cots[0] = cotangent[...]
    gather_cots = plane_gather(link, cots, ids)
    next(gather_cots)

    for z in range(line):
        for y in range(2):
            owner_row = 2 * z + y
            weight[pl.ds(owner_row * owned, owned), :] = qkv_all[z, y, :owned, :]
            done = 0
            cols = qkv_all.shape[3]
            for start, count, target in (
                (0, owned, 0),
                (owned, owned, 1),
                (2 * owned, vector_size - 2 * owned, 2),
            ):
                while count > 0:
                    row, col = start // cols, start % cols
                    span = min(count, cols - col)
                    length = (owned, owned, vector_size - 2 * owned)[target]
                    to = owner_row * length + (length - count)
                    vectors[target : target + 1, to : to + span] = qkv_all[
                        z, y, owned + row : owned + row + 1, col : col + span
                    ].astype(F32)
                    start, count = start + span, count - span

    head_cols = per_dev * HD
    holds_values = me % 2 == 1
    kv_first = (H + KV * (me % 2) + me // 2) * HD
    bias = jnp.concatenate(
        [
            vectors[2:3, pl.ds(pl.multiple_of(me * head_cols, HD), head_cols)],
            vectors[2:3, pl.ds(pl.multiple_of(kv_first, HD), HD)],
        ],
        axis=1,
    )
    for block in range(seq_count):
        here = pl.ds(block * rows, rows)
        value = tokens_all[block].astype(F32)
        normal = (value * inverse_rms(value) * vectors[0:1, :width]).astype(LOW)
        normed[block] = normal
        projected = dot(normal, weight[...]) + bias
        cosine, sine = cosines[here, :], sines[here, :]

        def rotate(head):
            return head * cosine + pltpu.roll(head, HD // 2, 1) * sine

        for head in range(per_dev):
            queries[head, here, :] = rotate(projected[:, head * HD : (head + 1) * HD]).astype(LOW)
        plain = projected[:, head_cols:]
        kv[0, here, :] = jnp.where(holds_values, plain, rotate(plain)).astype(LOW)
    swapped = link.send(kv.at[0], kv.at[1], core)
    leave(normed, normed_out)
    pump(3)
    swapped.wait_recv()
    keys[...] = jnp.where(holds_values, kv[1], kv[0])
    values[...] = jnp.where(holds_values, kv[0], kv[1])

    for copy in proj_over:
        copy.wait_recv()
    exchange = [
        link.send(proj_all.at[pl.ds(target * group, group)], proj_mine.at[me], {"seq": target})
        for target in others
    ]
    next(gather_cots)
    proj_mine[me] = proj_all[pl.ds(me * group, group)]

    for block in range(seq_count):
        here, last_key = pl.ds(block * rows, rows), (block + 1) * rows
        row_index = block * rows + lax.broadcasted_iota(jnp.int32, (rows, last_key), 0)
        key_index = lax.broadcasted_iota(jnp.int32, (rows, last_key), 1)
        allowed = (key_index <= row_index) & (seg_col[here, :] == seg_row[:, :last_key])
        for head in range(per_dev):
            scores = times_transpose(queries[head, here, :], keys[:last_key, :]) * HD ** (-0.5)
            scores = jnp.where(allowed, scores, FLOOR)
            highest = jnp.max(scores, axis=-1, keepdims=True)
            exponent = jnp.exp(scores - highest)
            total = jnp.sum(exponent, axis=-1, keepdims=True)
            mixture = dot((exponent / total).astype(LOW), values[:last_key, :])
            merged[here, head * HD : (head + 1) * HD] = mixture.astype(LOW)
            logsum[head, here, :] = highest + jnp.log(total)
    pump(2)
    for copy in exchange:
        copy.wait_recv()
    quarter = proj.shape[1]
    for block in range(seq_count):
        for k in range(seq_count):
            columns = proj_mine[k].reshape(-1, quarter)
            part[block, :, k * quarter : (k + 1) * quarter] = dot(
                merged[block * rows : (block + 1) * rows, :], columns
            ).astype(LOW)

    leave(part, part_out)
    pump(1)
    next(gather_cots)
    leave(cots, cots_out)
    pump(3 * line)
    for copy in leaving:
        copy.wait()
    second_over.wait_recv()
    for source in others:
        for member in range(group):
            pltpu.make_async_remote_copy(
                src_ref=ff_line.at[0],
                dst_ref=ff_rows.at[source, member],
                send_sem=hand_send.at[0],
                recv_sem=hand_recv.at[source * group + member],
                device_id=core,
                device_id_type=MESH,
            ).wait_recv()
    for copy, target in handed:

        @pl.when(target != me)
        def _():
            copy.wait_send()

    link.finish()


def opening(tokens, cotangent, qkv, proj, ff, inverse, segments, sizes):
    owned, vector_size, per_dev, group, line = sizes
    rows, width = tokens.shape
    block = (rows, width)
    seq_len = 4 * rows
    cols = qkv.shape[1]
    heads = (seq_len, HD)
    vmem, hbm = (pl.BlockSpec(memory_space=pltpu.VMEM), pl.BlockSpec(memory_space=pl.ANY))

    def like(*shape, dtype=LOW):
        return jax.ShapeDtypeStruct(shape, dtype)

    outs = [
        (like(*heads, dtype=F32), vmem),
        (like(*heads, dtype=F32), vmem),
        (like(4, *block), hbm),
        (like(width, cols), vmem),
        (like(3, max(width, 2048), dtype=F32), vmem),
        (like(4, group, 2, *proj.shape), vmem),
        (like(line, *ff[0].shape), hbm),
        (like(4, group, *ff[1].shape), vmem),
        (like(3, *ff[2].shape[1:]), hbm),
        (like(4, *block), hbm),
        (like(per_dev, *heads), vmem),
        (like(*heads), vmem),
        (like(*heads), vmem),
        (like(seq_len, per_dev * HD), vmem),
        (like(per_dev, seq_len, 1, dtype=F32), vmem),
        (like(4, *block), hbm),
        (like(8, *block), hbm),
    ]
    copies = 10 * line + 40
    return pl.pallas_call(
        functools.partial(opening_kernel, (owned, vector_size, per_dev, group)),
        out_shape=[shape for shape, _ in outs],
        in_specs=[vmem] * 6 + [hbm] * 2 + [vmem] * 3,
        out_specs=[place for _, place in outs],
        scratch_shapes=[
            pltpu.VMEM((4, *block), LOW),
            pltpu.VMEM((4, *block), LOW),
            pltpu.VMEM((4, *block), LOW),
            pltpu.VMEM((8, *block), LOW),
            pltpu.VMEM((line, 2, *qkv.shape), LOW),
            pltpu.VMEM((line, 2, *proj.shape), LOW),
            pltpu.VMEM((line, *ff[1].shape), LOW),
            pltpu.VMEM((2, *heads), LOW),
            pltpu.SemaphoreType.DMA((copies,)),
            pltpu.SemaphoreType.DMA((copies,)),
            pltpu.SemaphoreType.DMA((line,)),
            pltpu.SemaphoreType.DMA((4 * group,)),
            pltpu.SemaphoreType.DMA((8,)),
        ],
        cost_estimate=pl.CostEstimate(
            flops=100_000_000_000, bytes_accessed=40_000_000, transcendentals=4_000_000
        ),
        compiler_params=pltpu.CompilerParams(
            collective_id=0, has_side_effects=True, vmem_limit_bytes=58 << 20
        ),
    )(tokens, cotangent, qkv, proj, *ff, inverse, *segments)


def middle_kernel(
    part, tokens, vectors, hidden, mids, arrived, summed, across_in, send_sems, recv_sems
):
    (me, sibling, across), ids = neighbours()
    far = across + 1 - 2 * (across % 2)
    width = tokens.shape[1]
    greet(ids)
    link = Sender(send_sems, recv_sems)
    first = link.send(part.at[far], arrived.at[0], ids[0])
    second = link.send(part.at[sibling], arrived.at[1], ids[0])
    first.wait_recv()
    summed[...] = (part[across].astype(F32) + arrived[0].astype(F32)).astype(LOW)
    third = link.send(summed, across_in, ids[1])
    second.wait_recv()
    hidden[...] = tokens[...].astype(F32) + (part[me].astype(F32) + arrived[1].astype(F32))
    third.wait_recv()
    total = hidden[...] + across_in[...].astype(F32)
    hidden[...] = total
    mids[0] = (total * inverse_rms(total) * vectors[1:2, :width]).astype(LOW)
    for _ in plane_gather(link, mids, ids):
        pass
    link.finish()


def middle(part, tokens, vectors):
    block = tokens.shape
    vmem = pl.BlockSpec(memory_space=pltpu.VMEM)
    return pl.pallas_call(
        middle_kernel,
        out_shape=[jax.ShapeDtypeStruct(block, F32), jax.ShapeDtypeStruct((8, *block), LOW)],
        in_specs=[vmem] * 3,
        out_specs=[vmem] * 2,
        scratch_shapes=[
            pltpu.VMEM((2, *block), LOW),
            pltpu.VMEM(block, LOW),
            pltpu.VMEM(block, LOW),
            pltpu.SemaphoreType.DMA((16,)),
            pltpu.SemaphoreType.DMA((16,)),
        ],
        compiler_params=pltpu.CompilerParams(
            collective_id=1, has_side_effects=True, vmem_limit_bytes=58 << 20
        ),
    )(part, tokens, vectors)


def cut_kernel(shape, *refs):
    follows, group, units = shape
    if follows:
        mids_in, cots_in, whole_in, out_before, mid_before, hidden_in, *refs = refs
    else:
        mids_in, cots_in, weight_in, rows_in, *refs = refs
    term, out, mid, *refs = refs
    if follows:
        ahead, *refs = refs
    mids, cots, weight, rows, down, act, grad, stage, before, *refs = refs
    if follows:
        odd, arrived, held, from_y, corner, total, slots, ahead_sems, *refs = refs
    load_sems, weight_sems, stage_sems, before_sems, send_sems, recv_sems = refs
    (me, sibling, across), ids = neighbours()
    far = across + 1 - 2 * (across % 2)
    others = (sibling, across, far)
    line, _, owned, cols = weight.shape
    count, block, width = mids.shape
    quarter = width // 4
    fold = quarter // owned
    core, over_x, over_y = ids
    greet((core, over_x, {"seq": far}, over_y))
    link = Sender(send_sems, recv_sems)

    def load(source, target, sem):
        copy = pltpu.make_async_copy(source, target, sem)
        copy.start()
        return copy

    if follows:
        sent = [
            link.send(whole_in.at[pl.ds(k * group, group), 2], rows.at[me], {"seq": k})
            for k in others
        ]
        loads = [load(whole_in.at[pl.ds(me * group, group), 2], rows.at[me], weight_sems.at[line])]
        loads += [
            load(whole_in.at[z, pl.ds(0, 2)], weight.at[z], weight_sems.at[z]) for z in range(line)
        ]
    else:
        sent = []
        loads = [load(rows_in, rows, weight_sems.at[line]), load(weight_in, weight, weight_sems.at[0])]
    for t in range(count):
        load(mids_in.at[t], mids.at[t], load_sems.at[0, t])
        load(cots_in.at[t], cots.at[t], load_sems.at[1, t])
    if follows:
        loads.append(load(hidden_in, total, ahead_sems.at[2]))
    for copy in loads:
        copy.wait()

    def put(t):
        return pltpu.make_async_copy(slots.at[t % 2], ahead.at[t], ahead_sems.at[t % 2])

    def take(t):
        return pltpu.make_async_copy(ahead.at[t], slots.at[t % 2], ahead_sems.at[t % 2])

    def forward(t, carry):
        pltpu.make_async_copy(mids_in.at[t], mids.at[t], load_sems.at[0, t]).wait()

        @pl.when(t >= 2)
        def _():
            put(t - 2).wait()

        slots[t % 2] = dot(mids[t], weight[...].reshape(width, cols))
        put(t).start()
        return carry

    if follows:
        lax.fori_loop(0, count, forward, 0)
        for t in (count - 2, count - 1):
            put(t).wait()
        take(0).start()
    for copy in sent:
        copy.wait_recv()
    for k in range(4):
        for member in range(group):
            for j in range(fold):
                first = k * quarter + j * owned
                down[first : first + owned, member * units : (member + 1) * units] = rows[
                    k, member, :, j * units : (j + 1) * units
                ]

    def tokens(t, carry):
        if follows:

            @pl.when(t + 1 < count)
            def _():
                take(t + 1).start()

            take(t).wait()
            gate_up = slots[t % 2]
        else:
            pltpu.make_async_copy(mids_in.at[t], mids.at[t], load_sems.at[0, t]).wait()
            gate_up = dot(mids[t], weight[...].reshape(width, cols))
        pltpu.make_async_copy(cots_in.at[t], cots.at[t], load_sems.at[1, t]).wait()
        grad_act = dot(cots[t], down[...])
        gate, upward = gate_up[:, : cols // 2], gate_up[:, cols // 2 :]
        sigmoid_gate = jax.nn.sigmoid(gate)
        silu = gate * sigmoid_gate
        act[t] = (silu * upward).astype(LOW)
        grad[t, :, : cols // 2] = (
            grad_act * upward * sigmoid_gate * (1.0 + gate * (1.0 - sigmoid_gate))
        ).astype(LOW)
        grad[t, :, cols // 2 :] = (grad_act * silu).astype(LOW)
        return carry

    lax.fori_loop(0, count, tokens, 0)

    def ask(source, t, slot):
        return load(source.at[t], before.at[slot], before_sems.at[slot])

    all_act = act[...].reshape(count * block, cols // 2)
    for k in range(4):
        value = column_product(
            cots[:, :, k * quarter : (k + 1) * quarter].reshape(count * block, quarter), all_act
        ).astype(LOW)
        for member in range(group):
            for j in range(fold):
                rows[k, member, :, j * units : (j + 1) * units] = value[
                    j * owned : (j + 1) * owned, member * units : (member + 1) * units
                ]
    sent = [
        link.send(rows.at[k], term.at[pl.ds(me * group, group), 2], {"seq": k}) for k in others
    ]
    term[pl.ds(me * group, group), 2] = rows[me]
    if follows:
        order = (7, 5, 6, 3, 4, 1, 2, 0)
        asked = ask(out_before, order[0], 0)
        halved = {}
        for number, t in enumerate(order):
            ready = asked
            if number + 1 < count:
                asked = ask(out_before, order[number + 1], (number + 1) % 2)
            value = times_transpose(act[t], down[...])
            ready.wait()
            value = value + before[number % 2].astype(F32)
            if t % 2 == 1:
                slot = t // 2 % 2
                if t < 4:
                    link.release(halved[t + 3])
                odd[slot] = value.astype(LOW)
                halved[t - 1] = link.send(odd.at[slot], arrived.at[t // 2], core)
                continue
            halved[t].wait_recv()
            value = value + arrived[t // 2].astype(F32)
            if t == 0:
                total[...] += value
            else:
                held[t // 2 - 1] = value.astype(LOW)
            if t == 6:
                turn = link.send(held.at[2], corner, over_y)
            if t == 4:
                direct = link.send(held.at[1], from_y, over_y)

    all_grad = grad[...].reshape(count * block, cols)
    for z in range(line):
        value = column_product(
            mids[:, :, 2 * owned * z : 2 * owned * (z + 1)].reshape(count * block, 2 * owned),
            all_grad,
        ).astype(LOW)
        for y in range(2):
            term[z, y] = value[y * owned : (y + 1) * owned, :]
        if follows and z == line - 2:
            turn.wait_recv()
            held[0] = (held[0].astype(F32) + corner[...].astype(F32)).astype(LOW)
            last = link.send(held.at[0], out, over_x)

    targets = {0: mid} if follows else {0: mid, 1: out}
    if follows:
        ask(mid_before, 0, 0)

    def hand_over(t, place):
        return pltpu.make_async_copy(
            stage.at[t % 2, place], targets[place].at[t], stage_sems.at[t % 2, place]
        )

    def back(t, carry):
        @pl.when(t >= 2)
        def _():
            for place in targets:
                hand_over(t - 2, place).wait()

        values = {0: times_transpose(grad[t], weight[...].reshape(width, cols))}
        if follows:

            @pl.when(t + 1 < count)
            def _():
                ask(mid_before, t + 1, (t + 1) % 2)

            pltpu.make_async_copy(
                mid_before.at[t], before.at[t % 2], before_sems.at[t % 2]
            ).wait()
            values[0] = values[0] + before[t % 2].astype(F32)
        else:
            values[1] = times_transpose(act[t], down[...])
        for place in targets:
            stage[t % 2, place] = values[place].astype(LOW)
            hand_over(t, place).start()
        return carry

    lax.fori_loop(0, count, back, 0)
    for t in (count - 2, count - 1):
        for place in targets:
            hand_over(t, place).wait()
    for copy in sent:
        copy.wait_recv()
    if follows:
        direct.wait_recv()
        last.wait_recv()
        out[...] = (total[...] + out[...].astype(F32) + from_y[...].astype(F32)).astype(LOW)
    link.finish()


def cut_call(follows, args, sizes):
    group, line, owned, units = sizes
    mids = args[0]
    count, block, width = mids.shape
    cols = 2 * group * units
    hbm, vmem = (pl.BlockSpec(memory_space=pl.ANY), pl.BlockSpec(memory_space=pltpu.VMEM))
    rows = (4, group, owned, cols)
    like_mids = jax.ShapeDtypeStruct(mids.shape, LOW)
    low_scratch = [
        mids.shape,
        mids.shape,
        (line, 2, owned, cols),
        rows,
        (width, cols // 2),
        (count, block, cols // 2),
        (count, block, cols),
        (2, 1 if follows else 2, block, width),
        (2, block, width),
    ]
    ahead, late_scratch = [], []
    if follows:
        for size in (2, 4, 3):
            low_scratch.append((size, block, width))
        low_scratch += [(block, width)] * 2
        ahead = [jax.ShapeDtypeStruct((count, block, cols), F32)]
        late_scratch = [
            pltpu.VMEM((block, width), F32),
            pltpu.VMEM((2, block, cols), F32),
            pltpu.SemaphoreType.DMA((3,)),
        ]
    return pl.pallas_call(
        functools.partial(cut_kernel, (follows, group, units)),
        out_shape=[
            jax.ShapeDtypeStruct((line, 3, owned, cols), LOW),
            jax.ShapeDtypeStruct((block, width), LOW) if follows else like_mids,
            like_mids,
            *ahead,
        ],
        in_specs=[hbm] * len(args),
        out_specs=[vmem, vmem if follows else hbm, hbm] + [hbm] * len(ahead),
        scratch_shapes=[pltpu.VMEM(shape, LOW) for shape in low_scratch]
        + late_scratch
        + [
            pltpu.SemaphoreType.DMA((2, count)),
            pltpu.SemaphoreType.DMA((line + 1,)),
            pltpu.SemaphoreType.DMA((2, 2)),
            pltpu.SemaphoreType.DMA((2,)),
            pltpu.SemaphoreType.DMA((16,)),
            pltpu.SemaphoreType.DMA((16,)),
        ],
        compiler_params=pltpu.CompilerParams(
            collective_id=4 if follows else 3, has_side_effects=True, vmem_limit_bytes=61 << 20
        ),
        cost_estimate=pl.CostEstimate(
            flops=50_000_000_000, bytes_accessed=40_000_000, transcendentals=2_000_000
        ),
    )(*args)


def spread_blocks(link, ids, pair, ff_sum, hidden_blocks, down_blocks, local_sems):
    core, over_x, over_y = ids
    kept, down = ff_sum.at[pair], ff_sum.at[2]
    local = [
        pltpu.make_async_copy(kept, hidden_blocks.at[0], local_sems.at[0]),
        pltpu.make_async_copy(down, down_blocks.at[0], local_sems.at[1]),
    ]
    for copy in local:
        copy.start()
    to_x = [
        link.send(kept, hidden_blocks.at[2], over_x),
        link.send(down, down_blocks.at[2], over_x),
    ]
    last = [
        link.send(kept, hidden_blocks.at[1], core),
        link.send(down, down_blocks.at[1], core),
    ]
    yield
    over = link.send(ff_sum.at[1 - pair], hidden_blocks.at[4], over_y)
    yield
    over.wait_recv()
    far = link.send(hidden_blocks.at[4], hidden_blocks.at[6], over_x)
    last.append(link.send(hidden_blocks.at[4], hidden_blocks.at[5], core))
    for copy, blocks in zip(to_x, (hidden_blocks, down_blocks)):
        copy.wait_recv()
        last.append(link.send(blocks.at[2], blocks.at[3], core))
    yield
    far.wait_recv()
    last.append(link.send(hidden_blocks.at[6], hidden_blocks.at[7], core))
    yield
    for copy in last:
        copy.wait_recv()
    for copy in local:
        copy.wait()
    yield


def spread_kernel(ff_sum, _, hidden_blocks, down_blocks, send_sems, recv_sems, local_sems):
    _, ids = neighbours()
    greet(ids)
    link = Sender(send_sems, recv_sems)
    pair = lax.axis_index("fsdp") % 2
    for _ in spread_blocks(link, ids, pair, ff_sum, hidden_blocks, down_blocks, local_sems):
        pass
    link.finish()


def spread(ff_sum, earlier):
    hbm, vmem = (pl.BlockSpec(memory_space=pl.ANY), pl.BlockSpec(memory_space=pltpu.VMEM))
    return pl.pallas_call(
        spread_kernel,
        out_shape=[
            jax.ShapeDtypeStruct((count, *ff_sum.shape[1:]), LOW) for count in (8, 4)
        ],
        in_specs=[vmem, hbm],
        out_specs=[hbm] * 2,
        scratch_shapes=[pltpu.SemaphoreType.DMA((12,))] * 2 + [pltpu.SemaphoreType.DMA((2,))],
        compiler_params=pltpu.CompilerParams(
            collective_id=5, has_side_effects=True, vmem_limit_bytes=58 << 20
        ),
        cost_estimate=pl.CostEstimate(
            flops=50_000_000_000, bytes_accessed=20_000_000, transcendentals=0
        ),
    )(ff_sum, earlier)


def closing_kernel(shape, late, *refs):
    count = 18
    given, places, sems = list(refs[:count]), refs[-len(late) - 1 : -1], refs[-1]
    late_loads = []
    for number, place in zip(late, places):
        late_loads.append(
            pltpu.make_async_copy(given[number], place, sems.at[len(late_loads)])
        )
        given[number] = place
    closing_body(shape, late_loads, *given, *refs[count : -len(late) - 1])


def closing_body(
    shape,
    late_loads,
    terms_in,
    hidden,
    upstream,
    tokens_in,
    normed_in,
    vectors,
    weight,
    proj_mine,
    queries,
    keys,
    values,
    merged,
    logsum,
    cosines,
    sines,
    seg_col,
    seg_row,
    ff_sum,
    tokens_grad,
    gain_terms,
    attn_sum,
    hidden_blocks,
    down_blocks,
    mid_terms,
    tokens_all,
    normed,
    arrived,
    held,
    from_x,
    from_y,
    corner,
    upper,
    grad_heads,
    grad_queries,
    grad_keys,
    grad_values,
    kv,
    projected,
    proj_part,
    proj_in,
    proj_half,
    bias_row,
    qkv_part,
    qkv_in,
    late,
    late_x,
    send_sems,
    recv_sems,
    local_sems,
    load_sems,
):
    owned, per_dev, group = shape
    (me, sibling, across), (core, over_x, over_y) = neighbours()
    far = across + 1 - 2 * (across % 2)
    others = (sibling, across, far)
    pair = lax.axis_index("fsdp") % 2
    rows, width = hidden.shape
    seq_count = tokens_all.shape[0]
    quarter = width // seq_count
    low, high = (pl.ds(0, rows // 2), pl.ds(rows // 2, rows // 2))
    gains = (vectors[0:1, :width], vectors[1:2, :width])
    greet((core, over_x, {"seq": far}, over_y))
    link = Sender(send_sems, recv_sems)

    loads = {}
    for k in (7, 3, 5, 1, 6, 2, 4, 0):
        loads[k] = pltpu.make_async_copy(terms_in.at[k], mid_terms.at[k], load_sems.at[k])
        loads[k].start()
    kept_loads = [
        pltpu.make_async_copy(source, target, load_sems.at[8 + number])
        for number, (source, target) in enumerate(((tokens_in, tokens_all), (normed_in, normed)))
    ]
    for copy in (*kept_loads, *late_loads):
        copy.start()
    halved = {}
    for k in (6, 2, 4, 0):
        loads[k + 1].wait()
        halved[k] = link.send(mid_terms.at[k + 1], arrived.at[k // 2], core)

    def chip_sum(k):
        loads[k].wait()
        halved[k].wait_recv()
        return mid_terms[k].astype(F32) + arrived[k // 2].astype(F32)

    held[2] = chip_sum(6).astype(LOW)
    turn_y = link.send(held.at[2, low], corner.at[0], over_x)
    turn_x = link.send(held.at[2, high], corner.at[1], over_y)
    held[0] = chip_sum(2).astype(LOW)
    direct_x = link.send(held.at[0, low], from_x.at[low], over_x)
    held[1] = chip_sum(4).astype(LOW)
    direct_y = link.send(held.at[1, high], from_y.at[high], over_y)
    tokens_grad[...] = chip_sum(0)
    turn_x.wait_recv()
    held[0, high] = (held[0, high].astype(F32) + corner[1].astype(F32)).astype(LOW)
    second_x = link.send(held.at[0, high], from_x.at[high], over_x)
    turn_y.wait_recv()
    held[1, low] = (held[1, low].astype(F32) + corner[0].astype(F32)).astype(LOW)
    second_y = link.send(held.at[1, low], from_y.at[low], over_y)
    for copy in (direct_x, direct_y, second_x, second_y):
        copy.wait_recv()

    grad_mid = tokens_grad[...] + from_x[...].astype(F32) + from_y[...].astype(F32)
    through, term = norm_back(hidden[...], inverse_rms(hidden[...]), gains[1], grad_mid)
    gain_terms[1:2, :] = term[None]
    total = upstream[...].astype(F32) + through
    tokens_grad[...] = total
    upper[me] = total.astype(LOW)
    last = [link.send(upper.at[me], upper.at[me], core)]
    to_x = [link.send(upper.at[me, half], upper.at[me, half], over_x) for half in (low, high)]
    last[0].wait_recv()
    for copy in late_loads:
        copy.wait()
    head_rows, cols = per_dev * HD, weight.shape[1]
    scale = HD ** (-0.5)
    grad_keys[...] = jnp.zeros_like(grad_keys)
    grad_values[...] = jnp.zeros_like(grad_values)

    def attend_back(block):
        grad_heads[block * rows : (block + 1) * rows, :] = sum(
            times_transpose(
                upper[block, :, k * quarter : (k + 1) * quarter],
                proj_mine[k].reshape(head_rows, quarter),
            )
            for k in range(seq_count)
        ).astype(LOW)
        here, last_key = pl.ds(block * rows, rows), (block + 1) * rows
        row_index = block * rows + lax.broadcasted_iota(jnp.int32, (rows, last_key), 0)
        key_index = lax.broadcasted_iota(jnp.int32, (rows, last_key), 1)
        allowed = (key_index <= row_index) & (seg_col[here, :] == seg_row[:, :last_key])
        for head in range(per_dev):
            query = queries[head, here, :]
            upper_head = grad_heads[here, head * HD : (head + 1) * HD]
            scores = times_transpose(query, keys[:last_key, :]) * scale
            probs = jnp.where(allowed, jnp.exp(scores - logsum[head, here, :]), 0.0)
            grad_probs = times_transpose(upper_head, values[:last_key, :])
            inner = jnp.sum(probs * grad_probs, axis=-1, keepdims=True)
            grad_scores = (probs * (grad_probs - inner)).astype(LOW)
            grad_queries[head, here, :] = (dot(grad_scores, keys[:last_key, :]) * scale).astype(LOW)
            grad_keys[:last_key, :] += column_product(grad_scores, query)
            grad_values[:last_key, :] += column_product(probs.astype(LOW), upper_head)

    here_first = [block // 2 == me // 2 for block in range(seq_count)]
    for block in range(seq_count):
        pl.when(here_first[block])(functools.partial(attend_back, block))
    for copy, half in zip(to_x, (low, high)):
        copy.wait_recv()
        last.append(link.send(upper.at[across, half], upper.at[across, half], core))
    for copy in last[1:]:
        copy.wait_recv()
    spread = spread_blocks(
        link, (core, over_x, over_y), pair, ff_sum, hidden_blocks, down_blocks, local_sems
    )
    next(spread)
    next(spread)
    for block in range(seq_count):
        pl.when(jnp.logical_not(here_first[block]))(functools.partial(attend_back, block))

    for k in range(seq_count):
        term = sum(
            column_product(
                merged[block * rows : (block + 1) * rows, :],
                upper[block, :, k * quarter : (k + 1) * quarter],
            )
            for block in range(seq_count)
        ).astype(LOW)
        for member in range(group):
            for y in range(2):
                first = (2 * member + y) * owned
                proj_part[y, k, member] = term[first : first + owned, :]
    proj_over = link.send(proj_part.at[1 - pair], proj_in, over_y)
    next(spread)
    for copy in kept_loads:
        copy.wait()
    holds_values = me % 2 == 1
    key_copy = (grad_keys[...] * scale).astype(LOW)
    value_copy = grad_values[...].astype(LOW)
    kv[0] = jnp.where(holds_values, key_copy, value_copy)
    swapped = link.send(kv.at[0], kv.at[1], core)
    grad_keys[...] = jnp.where(holds_values, value_copy, key_copy).astype(F32)
    swapped.wait_recv()
    grad_kv = grad_keys[...] + kv[1].astype(F32)

    bias_row[...] = jnp.zeros_like(bias_row)
    bias_parts = 0.0
    gain_terms[0:1, :] = jnp.zeros((1, width), F32)
    for block in range(seq_count):
        here = pl.ds(block * rows, rows)
        cosine, sine = cosines[here, :], sines[here, :]

        def rotate_back(head):
            return head * cosine - pltpu.roll(head, HD // 2, 1) * sine

        for head in range(per_dev):
            projected[here, head * HD : (head + 1) * HD] = rotate_back(
                grad_queries[head, here, :].astype(F32)
            ).astype(LOW)
        plain = grad_kv[block * rows : (block + 1) * rows, :]
        projected[here, head_rows:] = jnp.where(holds_values, plain, rotate_back(plain)).astype(LOW)
        grad_block = projected[here, :]
        bias_parts += jnp.sum(grad_block.astype(F32), axis=0, keepdims=True)
        grad_in = times_transpose(grad_block, weight[...])
        value = tokens_all[block].astype(F32)
        gain_terms[0:1, :] += jnp.sum(
            grad_in * value * inverse_rms(value), axis=0, keepdims=True
        )
        arrived[block] = grad_in.astype(LOW)
    first = link.send(arrived.at[far], late.at[0], core)
    second = link.send(arrived.at[sibling], late.at[1], core)
    first.wait_recv()
    link.release(direct_x, second_x)
    held[0] = (arrived[across].astype(F32) + late[0].astype(F32)).astype(LOW)
    third = link.send(held.at[0], late_x, over_x)
    proj_over.wait_recv()
    proj_half[...] = (proj_part[pair].astype(F32) + proj_in[...].astype(F32)).astype(LOW)

    def proj_place(device):
        return (pl.ds(device * group, group), pl.ds(0, owned), pl.ds(cols, quarter))

    last = [
        link.send(proj_half.at[k], attn_sum.at[proj_place(me)], {"seq": k}) for k in others
    ]
    attn_sum[proj_place(me)] = proj_half[me]
    kv_first = (H + KV * (me % 2) + me // 2) * HD
    bias_row[0:1, pl.ds(pl.multiple_of(me * head_rows, HD), head_rows)] = bias_parts[:, :head_rows]
    bias_row[0:1, pl.ds(pl.multiple_of(kv_first, HD), HD)] = bias_parts[:, head_rows:]
    line = qkv_in.shape[0]
    owned_bias = bias_row.shape[1] // (2 * line)
    qkv_part[:, :, owned:, :] = jnp.zeros_like(qkv_part[:, :, owned:, :])
    for z in range(line):
        for y in range(2):
            owner, at = 2 * z + y, 0
            for source, row, length in (
                (gain_terms, 0, owned),
                (gain_terms, 1, owned),
                (bias_row, 0, owned_bias),
            ):
                done = 0
                while done < length:
                    span = min(length - done, cols - at % cols)
                    first_col = owner * length + done
                    qkv_part[
                        y, z, owned + at // cols : owned + at // cols + 1, at % cols : at % cols + span
                    ] = source[row : row + 1, first_col : first_col + span].astype(LOW)
                    done, at = done + span, at + span
    for z in range(line):
        term = sum(
            column_product(
                normed[block, :, 2 * owned * z : 2 * owned * (z + 1)],
                projected[block * rows : (block + 1) * rows, :],
            )
            for block in range(seq_count)
        ).astype(LOW)
        for y in range(2):
            qkv_part[y, z, :owned, :] = term[y * owned : (y + 1) * owned, :]
    qkv_over = link.send(qkv_part.at[1 - pair], qkv_in, over_y)
    next(spread)
    second.wait_recv()
    third.wait_recv()
    grad_in = arrived[me].astype(F32) + late[1].astype(F32) + late_x[...].astype(F32)
    value = tokens_all[me].astype(F32)
    through, _ = norm_back(value, inverse_rms(value), gains[0], grad_in)
    tokens_grad[...] += through
    qkv_over.wait_recv()
    attn_sum[:, :, :cols] = (qkv_part[pair].astype(F32) + qkv_in[...].astype(F32)).astype(LOW)
    attn_sum[:, owned:, cols:] = jnp.zeros_like(attn_sum[:, owned:, cols:])
    for copy in last:
        copy.wait_recv()
    next(spread)
    link.finish()


def closing(args, sizes):
    owned, vector_rows, bias_cols, per_dev, group, line = sizes
    hidden, weight, proj_mine = args[1], args[6], args[7]
    rows, width = hidden.shape
    block = (rows, width)
    cols = weight.shape[1]
    quarter = proj_mine.shape[-1]
    heads = (4 * rows, HD)
    rows_in = (4, group, owned, quarter)
    outs = [
        jax.ShapeDtypeStruct(block, F32),
        jax.ShapeDtypeStruct((2, width), F32),
        jax.ShapeDtypeStruct((line, owned + vector_rows, cols + quarter), LOW),
        jax.ShapeDtypeStruct((8, *args[-1].shape[1:]), LOW),
        jax.ShapeDtypeStruct((4, *args[-1].shape[1:]), LOW),
    ]
    low_scratch = [
        (8, *block),
        (4, *block),
        (4, *block),
        (4, *block),
        (3, *block),
        block,
        block,
        (2, rows // 2, width),
        (4, *block),
        (4 * rows, per_dev * HD),
        (per_dev, *heads),
    ]
    late = (6, 7, 8, 9, 10, 11, 12, 13, 14, 15, 17)
    return pl.pallas_call(
        functools.partial(closing_kernel, (owned, per_dev, group), late),
        out_shape=outs,
        in_specs=[
            pl.BlockSpec(memory_space=pl.ANY if k in (0, 3, 4, *late) else pltpu.VMEM)
            for k in range(len(args))
        ],
        out_specs=[pl.BlockSpec(memory_space=pltpu.VMEM)] * (len(outs) - 2)
        + [pl.BlockSpec(memory_space=pl.ANY)] * 2,
        scratch_shapes=[pltpu.VMEM(shape, LOW) for shape in low_scratch]
        + [pltpu.VMEM(heads, F32)] * 2
        + [
            pltpu.VMEM(shape, LOW)
            for shape in (
                (2, *heads),
                (4 * rows, cols),
                (2, *rows_in),
                rows_in,
                rows_in,
            )
        ]
        + [pltpu.VMEM((1, bias_cols), F32)]
        + [
            pltpu.VMEM(shape, LOW)
            for shape in (
                (2, line, owned + vector_rows, cols),
                (line, owned + vector_rows, cols),
                (2, *block),
                block,
            )
        ]
        + [pltpu.SemaphoreType.DMA((48,))] * 2
        + [pltpu.SemaphoreType.DMA((2,)), pltpu.SemaphoreType.DMA((10,))]
        + [pltpu.VMEM(args[k].shape, args[k].dtype) for k in late]
        + [pltpu.SemaphoreType.DMA((len(late),))],
        compiler_params=pltpu.CompilerParams(
            collective_id=2, has_side_effects=True, vmem_limit_bytes=58 << 20
        ),
        cost_estimate=pl.CostEstimate(
            flops=100_000_000_000, bytes_accessed=40_000_000, transcendentals=4_000_000
        ),
    )(*args)


def columns_kernel(place, *refs):
    *pieces, out = refs
    row = 0
    for piece in pieces:
        count, rows, quarter = piece.shape
        for k in range(count):
            here = place[0] + k - 2 * ((place[0] % 2) * (k % 2)) - 4 * (
                (place[0] // 2 % 2) * (k // 2 % 2)
            )
            out[pl.ds(row, rows), pl.ds(k * quarter, quarter)] = piece[here].astype(F32)
        row += rows


def columns_call(place, pieces):
    rows = sum(piece.shape[1] for piece in pieces)
    width = pieces[0].shape[0] * pieces[0].shape[2]
    return pl.pallas_call(
        columns_kernel,
        out_shape=jax.ShapeDtypeStruct((rows, width), F32),
        in_specs=[pl.BlockSpec(memory_space=pltpu.SMEM)]
        + [pl.BlockSpec(memory_space=pltpu.VMEM)] * len(pieces),
        out_specs=pl.BlockSpec(memory_space=pltpu.VMEM),
        compiler_params=pltpu.CompilerParams(vmem_limit_bytes=40 << 20),
    )(place, *pieces)


def down_kernel(fold, place, _, *refs):
    *pieces, out = refs
    row = 0
    for piece in pieces:
        count, owned, width = piece.shape
        span = width // fold
        for k in range(count):
            here = place[0] + k - 2 * ((place[0] % 2) * (k % 2)) - 4 * (
                (place[0] // 2 % 2) * (k // 2 % 2)
            )
            whole = piece[here].astype(F32)
            for j in range(fold):
                whole_part = whole[:, j * span : (j + 1) * span]
                out[pl.ds(row, span), pl.ds((k * fold + j) * owned, owned)] = whole_part.T
        row += span


def down_call(place, earlier, pieces, fold):
    rows = sum(piece.shape[2] // fold for piece in pieces)
    width = pieces[0].shape[0] * pieces[0].shape[1] * fold
    return pl.pallas_call(
        functools.partial(down_kernel, fold),
        out_shape=jax.ShapeDtypeStruct((rows, width), F32),
        in_specs=[pl.BlockSpec(memory_space=pltpu.SMEM), pl.BlockSpec(memory_space=pl.ANY)]
        + [pl.BlockSpec(memory_space=pltpu.VMEM)] * len(pieces),
        out_specs=pl.BlockSpec(memory_space=pltpu.VMEM),
        compiler_params=pltpu.CompilerParams(vmem_limit_bytes=40 << 20),
    )(place, earlier, *pieces)


def hidden_kernel(cuts, group, place, *refs):
    *pieces, out = refs
    units = cuts[-1][1]
    count = pieces[0].shape[0] // 2
    for k in range(count):
        here = place[0] + k - 2 * ((place[0] % 2) * (k % 2)) - 4 * (
            (place[0] // 2 % 2) * (k // 2 % 2)
        )
        for pair in range(2):
            entry = (pair + place[1] - 2 * pair * place[1]) * count + here
            for part in range(2):
                for member in range(group):
                    first = (((part * count + k) * group + member) * 2 + pair) * units
                    for piece, (low, high) in zip(pieces, cuts):
                        span = high - low
                        at = (part * group + member) * span
                        out[:, first + low : first + high] = piece[entry][
                            :, at : at + span
                        ].astype(F32)


def hidden_call(place, pieces, cuts, group):
    rows = pieces[0].shape[1]
    units = cuts[-1][1]
    width = 2 * 8 * group * units
    step = 16
    return pl.pallas_call(
        functools.partial(hidden_kernel, cuts, group),
        grid=(rows // step,),
        out_shape=jax.ShapeDtypeStruct((rows, width), F32),
        in_specs=[pl.BlockSpec(memory_space=pltpu.SMEM)]
        + [pl.BlockSpec((8, step, piece.shape[2]), lambda i: (0, i, 0)) for piece in pieces],
        out_specs=pl.BlockSpec((step, width), lambda i: (i, 0)),
        compiler_params=pltpu.CompilerParams(vmem_limit_bytes=40 << 20),
    )(place, *pieces)


def local(
    tokens,
    segment_ids,
    attn_gain,
    qkv_weight,
    qkv_bias,
    proj_weight,
    mlp_gain,
    gate_up_weight,
    down_weight,
    cotangent,
):
    seq_count = lax.axis_size("seq")
    fsdp_count = lax.axis_size("fsdp")
    line = fsdp_count // 2
    place = lax.axis_index("seq")
    odd = lax.axis_index("fsdp") % 2 == 1
    tok_rows, width = tokens.shape[1:]
    seq_len = tok_rows * seq_count
    owned = qkv_weight.shape[0]
    owned_hidden = down_weight.shape[0]
    hidden = owned_hidden * fsdp_count
    quarter = width // seq_count
    per_dev = H // seq_count
    head_cols = per_dev * HD
    score_scale = HD ** (-0.5)
    group = line // seq_count
    cut_at = owned_hidden // 2 // 128 * 128
    cuts = [(0, cut_at), (cut_at, owned_hidden)]

    holds_values = place % 2 == 1
    kv_first = (H + KV * (place % 2) + place // 2) * HD
    qkv_own = jnp.concatenate(
        [
            lax.dynamic_slice_in_dim(qkv_weight, place * head_cols, head_cols, 1),
            lax.dynamic_slice_in_dim(qkv_weight, kv_first, HD, 1),
        ],
        axis=1,
    )
    cols = head_cols + HD
    vector = jnp.concatenate([attn_gain, mlp_gain, qkv_bias])
    vector_size = vector.shape[0]
    vector_rows = -(-vector_size // (16 * cols)) * 16
    vector = jnp.pad(vector, (0, vector_rows * cols - vector_size)).reshape(vector_rows, cols)
    proj_cols = lax.dynamic_slice_in_dim(proj_weight, place * quarter, quarter, 1)
    down_cols = lax.dynamic_slice_in_dim(down_weight, place * quarter, quarter, 1)
    fold = quarter // owned

    def folded(value):
        return jnp.concatenate(
            [value[..., j * owned : (j + 1) * owned, :] for j in range(fold)], axis=-1
        )

    def ff_columns(low, high, pair):
        return jnp.concatenate(
            [
                lax.dynamic_slice_in_dim(
                    gate_up_weight,
                    first + ((place * group + member) * 2 + pair) * owned_hidden + low,
                    high - low,
                    1,
                )
                for first in (0, hidden)
                for member in range(group)
            ],
            axis=1,
        )

    ff_sent = []
    for low, high in cuts:
        by_owner = [ff_columns(low, high, pair) for pair in range(2)]
        ff_sent.append((by_owner, folded(jnp.transpose(down_cols[low:high]))))
    segment_row = segment_ids[0]
    inverse = THETA ** (-2.0 * jnp.arange(HD // 2, dtype=F32) / HD)
    inverse = jnp.concatenate([inverse, inverse])[None]

    (
        cosines,
        sines,
        tokens_all,
        qkv_mine,
        vectors,
        proj_mine,
        first_all,
        first_rows,
        second_sent,
        normed_in,
        queries,
        head_keys,
        head_values,
        merged,
        logsum,
        attended,
        cots,
    ) = opening(
        tokens[0],
        cotangent[0],
        jnp.concatenate([qkv_own, vector], axis=0),
        lax.dynamic_slice_in_dim(proj_weight, place * quarter, quarter, 1),
        [part for by_owner, rows in ff_sent for part in (jnp.stack(by_owner), rows)],
        inverse,
        (segment_row[:, None], segment_row[None]),
        (owned, vector_size, per_dev, group, line),
    )
    second_all = line_gather(second_sent)
    hidden_in, mids = middle(attended, tokens[0], vectors)

    spans = [high - low for low, high in cuts]
    first_term, out_first, mid_first = cut_call(
        False, (mids, cots, first_all, first_rows), (group, line, owned, spans[0])
    )
    second_term, block_out, grad_mid, _ = cut_call(
        True, (mids, cots, second_all, out_first, mid_first, hidden_in), (group, line, owned, spans[1])
    )

    sums = [line_reduce(term) for term in (first_term, second_term)]

    tokens_grad, gain_terms, attn_term, *first_blocks = closing(
        (
            grad_mid,
            hidden_in,
            cotangent[0],
            tokens_all,
            normed_in,
            vectors,
            qkv_mine,
            proj_mine,
            queries,
            head_keys,
            head_values,
            merged,
            logsum,
            cosines,
            sines,
            segment_row[:, None],
            segment_row[None],
            sums[0],
        ),
        (owned, vector_rows, qkv_weight.shape[1], per_dev, group, line),
    )
    places_here = jnp.stack([place, lax.axis_index("fsdp") % 2]).astype(jnp.int32)
    corner = attn_term[:1, :16, :HD] + nought(sums[1][0, 0, 0])
    attn_term = lax.dynamic_update_slice(attn_term, corner, (0, 0, 0))
    attn_sum = line_reduce(attn_term)
    second_blocks = spread(sums[1], attn_term)
    hidden_pieces = [first_blocks[0], second_blocks[0]]
    down_pieces = [first_blocks[1], second_blocks[1]]
    gate_up_grad = hidden_call(places_here, hidden_pieces, cuts, group)
    attn_sums = seq_blocks(attn_sum + nought(second_blocks[0][0, 0, 0]))
    down_grad = down_call(places_here, attn_sums[2], down_pieces, fold)
    proj_grad = columns_call(
        places_here, [jnp.stack([part[:owned, cols:] for part in attn_sums])]
    )
    qkv_sums = in_order([part[:, :cols] for part in attn_sums])
    qkv_grad = jnp.concatenate(
        [part[:owned, :head_cols] for part in qkv_sums]
        + [part[:owned, head_cols:] for part in qkv_sums[0::2]]
        + [part[:owned, head_cols:] for part in qkv_sums[1::2]],
        axis=-1,
    ).astype(F32)
    vector_sum = sum(part[owned:].astype(F32) for part in qkv_sums).reshape(-1)
    return (
        block_out[None],
        tokens_grad[None],
        vector_sum[:owned],
        qkv_grad,
        vector_sum[2 * owned : vector_size],
        proj_grad,
        vector_sum[owned : 2 * owned],
        gate_up_grad,
        down_grad,
    )


def solution(mesh):
    in_specs = (
        P("fsdp", "seq", None),
        P("fsdp", None),
        P("fsdp"),
        P("fsdp", None),
        P("fsdp"),
        P("fsdp", None),
        P("fsdp"),
        P("fsdp", None),
        P("fsdp", None),
        P("fsdp", "seq", None),
    )
    out_specs = (
        P("fsdp", "seq", None),
        P("fsdp", "seq", None),
        P("fsdp"),
        P("fsdp", None),
        P("fsdp"),
        P("fsdp", None),
        P("fsdp"),
        P("fsdp", None),
        P("fsdp", None),
    )
    return jax.shard_map(local, mesh=mesh, in_specs=in_specs, out_specs=out_specs, check_vma=False)
```
